32 devices in a mesh: rows: 8 (over y, x, core), seq: 4 (over z).
Axes of the slice: x: 2, y: 2, z: 4, core: 2. Of those that a mesh axis runs over, the one named last changes fastest.
Arguments:
- tokens: bfloat16 [16, 2048, 768], P('rows', 'seq'), may hold values from -6 to 6
- segment_ids: int32 [16, 2048], P('rows'), may hold values from 0 to 3, as said below
- cotangent: bfloat16 [16, 2048, 768], P('rows', 'seq'), may hold values from -6 to 6
- query_key_value: bfloat16 [768, 2304], replicated, may hold values from -0.21875 to 0.21875
- out_weight: bfloat16 [768, 768], replicated, may hold values from -0.21875 to 0.21875
- up_weight: bfloat16 [768, 3072], replicated, may hold values from -0.21875 to 0.21875
- down_weight: bfloat16 [3072, 768], replicated, may hold values from -0.109375 to 0.109375
- attend_gain: float32 [768], replicated, may hold values from 0.25 to 1.75
- inner_gain: float32 [768], replicated, may hold values from 0.25 to 1.75
- feed_gain: float32 [768], replicated, may hold values from 0.25 to 1.75
- hidden_gain: float32 [3072], replicated, may hold values from 0.25 to 1.75
Outputs:
- output: bfloat16 [16, 2048, 768], P('rows', 'seq')
- tokens_grad: bfloat16 [16, 2048, 768], P('rows', 'seq')
- query_key_value_grad: float32 [768, 2304], replicated
- out_weight_grad: float32 [768, 768], replicated
- up_weight_grad: float32 [768, 3072], replicated
- down_weight_grad: float32 [3072, 768], replicated
- attend_gain_grad: float32 [768], replicated
- inner_gain_grad: float32 [768], replicated
- feed_gain_grad: float32 [768], replicated
- hidden_gain_grad: float32 [3072], replicated
The draws below stay inside these ranges and needn't reach their ends.
Inputs may be any that keep to these rules, and one draw needn't show every extreme that they name: `segment_ids`: within each row the ids are 0 everywhere (one document of 2048 tokens) or 0, 1, 2, 3 on four equal runs of 512 tokens; of the 2 rows at one index of rows at least one is of each kind.
All inputs are finite; a program needn't handle non-finite values.
Results may differ from the reference program's by a relative error of at most 0.02.
Values may be sent and summed in bfloat16 or wider, within the bound.
A program may use at most 256 MiB of HBM per device.

```python
import math
import jax
import jax.numpy as jnp
from jax import lax

D = 768
HEADS = 12
HEAD_DIM = 64
FF = 3072
ROW_LEN = 2048
ROWS_DEV = 2
ROWS = 16


def draw_segment_ids(key, part):
    key = jax.random.fold_in(key, 7)
    long_key, pack_key, coin_key = jax.random.split(key, 3)
    blocks = ROWS // ROWS_DEV
    long_place = jax.random.randint(long_key, (blocks, 1), 0, ROWS_DEV)
    pack_place = (long_place + jax.random.randint(pack_key, (blocks, 1), 1, ROWS_DEV)) % ROWS_DEV
    coin_flip = (jax.random.randint(coin_key, (blocks, ROWS_DEV), 0, 5) < 2).astype(jnp.int32)
    row_place = jnp.arange(ROWS_DEV, dtype=jnp.int32)[None, :]
    packed = jnp.where(row_place == pack_place, 1, jnp.where(row_place == long_place, 0, coin_flip)).reshape(ROWS)
    run_index = jnp.arange(ROW_LEN, dtype=jnp.int32) // (ROW_LEN // 4)
    return (packed[:, None] * run_index[None, :]).astype(jnp.int32)


def with_spikes(array, own_key, source, target, parts, factor):
    def block_of(position):
        return (jnp.arange(array.shape[position]) // (array.shape[position] // parts)).reshape((-1,) + (1,) * (array.ndim - 1 - position))

    near = jax.random.permutation(own_key, parts)[block_of(target)]
    far = (block_of(target) + parts // 2) % parts
    return jnp.where((block_of(source) == near) | (block_of(source) == far), factor * array, array)


def shard_levels(rng, shape, cuts, least, top_value):
    def one(position, blocks):
        steps = jax.random.uniform(jax.random.fold_in(jax.random.fold_in(rng, 6), position), (blocks,), jnp.float32, least / len(cuts), top_value / len(cuts))
        return jnp.repeat(jnp.exp(steps), shape[position] // blocks).reshape((-1,) + (1,) * (len(shape) - position - 1))

    level = one(*cuts[0])
    for cut in cuts[1:]:
        level = level * one(*cut)
    return level


def noise(rng, shape, deviation, most, pieces=(), kind=jnp.bfloat16):
    entries = jax.random.normal(rng, shape, jnp.float32) * deviation
    if len(pieces) > 0:
        entries = shard_levels(rng, shape, pieces, -0.22, 0.18) * entries
    return jnp.clip(entries, min=-most, max=most).astype(kind)


def gaussian_with(own_key, extent, deviation, bound, cuts, heavy, kind=jnp.bfloat16):
    values = deviation * jax.random.normal(own_key, extent, jnp.float32)
    if cuts:
        values = values * shard_levels(own_key, extent, cuts, -0.22, 0.18)
    return jnp.clip(with_spikes(values, jax.random.fold_in(own_key, 3), *heavy), -bound, bound).astype(kind)


def setup_inputs(seed: int = 0) -> dict:
    seeds = jax.random.split(jax.random.key(seed), 12)
    tokens = noise(seeds[0], (ROWS, ROW_LEN, D), 1.0, 6.0, ((0, 8), (1, 4)))
    segment_ids = draw_segment_ids(jax.random.fold_in(seeds[11], 71), 0)
    cotangent = gaussian_with(seeds[2], (ROWS, ROW_LEN, D), 1.0, 6.0, ((0, 8), (1, 4)), (1, 2, 4, 2.0))
    query_key_value = noise(seeds[3], (D, 3 * D), D ** -0.5, 0.21875)
    out_weight = noise(seeds[4], (D, D), D ** -0.5, 0.21875)
    up_weight = noise(seeds[5], (D, FF), D ** -0.5, 0.21875)
    down_weight = noise(seeds[6], (FF, D), FF ** -0.5, 0.109375)
    attend_gain = jnp.clip(1.0 + 0.15 * jax.random.normal(seeds[7], (D,), jnp.float32), 0.25, 1.75)
    inner_gain = jnp.clip(1.0 + 0.15 * jax.random.normal(seeds[8], (D,), jnp.float32), 0.25, 1.75)
    feed_gain = jnp.clip(1.0 + 0.15 * jax.random.normal(seeds[9], (D,), jnp.float32), 0.25, 1.75)
    hidden_gain = jnp.clip(1.0 + 0.15 * jax.random.normal(seeds[10], (FF,), jnp.float32), 0.25, 1.75)
    return dict(tokens=tokens, segment_ids=segment_ids, cotangent=cotangent, query_key_value=query_key_value, out_weight=out_weight, up_weight=up_weight, down_weight=down_weight, attend_gain=attend_gain, inner_gain=inner_gain, feed_gain=feed_gain, hidden_gain=hidden_gain)


EPSILON = 1e-05
MASKED = -1e+30
HIGHEST = lax.Precision.HIGHEST

@jax.custom_vjp
def low(v):
    return lax.optimization_barrier(v.astype(jnp.bfloat16)).astype(jnp.float32)

@jax.custom_vjp
def low_back(v):
    return v

def low_keep(v):
    return (low(v), None)

def low_pass(kept, grad):
    return (grad,)

def back_keep(v):
    return (v, None)

def back_low(kept, grad):
    return (low(grad),)
low.defvjp(low_keep, low_pass)
low_back.defvjp(back_keep, back_low)

def layer_norm(values, gain):
    average = lax.optimization_barrier(jnp.mean(values, axis=-1, keepdims=True))
    centred = values - average
    return centred * lax.rsqrt(lax.optimization_barrier(jnp.mean(centred * centred, axis=-1, keepdims=True)) + EPSILON) * gain

def matmul(left, right):
    return jnp.dot(left, right, precision=HIGHEST, preferred_element_type=jnp.float32)

def attend(queries, key_rows, value_rows, segments):
    length = queries.shape[0]
    block_width = math.gcd(512, length)
    block_count = length // block_width
    positions = jnp.arange(length, dtype=jnp.int32)

    def one_block(block_item):
        query_block, query_pos, query_seg = block_item
        logits = jnp.einsum('qhd,khd->hqk', query_block, key_rows, precision=HIGHEST) * HEAD_DIM ** (-0.5)
        logits = low_back(logits)
        allowed = (positions[None, :] <= query_pos[:, None]) & (segments[None, :] == query_seg[:, None])
        masked_logits = jnp.where(allowed[None], logits, MASKED)
        row_peak = lax.optimization_barrier(jnp.max(masked_logits, axis=-1, keepdims=True))
        softmax_total = lax.optimization_barrier(jnp.sum(jnp.where(allowed[None], jnp.exp(masked_logits - row_peak), 0.0), axis=-1, keepdims=True))
        log_total = row_peak + jnp.log(softmax_total)
        softmax_weights = jnp.where(allowed[None], jnp.exp(masked_logits - log_total), 0.0)
        return jnp.einsum('hqk,khd->qhd', low(softmax_weights), value_rows, precision=HIGHEST)
    blocks_out = lax.map(jax.checkpoint(one_block), (queries.reshape(block_count, block_width, HEADS, HEAD_DIM), positions.reshape(block_count, block_width), segments.reshape(block_count, block_width)))
    return blocks_out.reshape(length, HEADS * HEAD_DIM)

def forward(row_input, segments, parameters):
    qkv_weight, proj_weight, first_weight, second_weight, gain_one, gain_two, gain_three, gain_four = parameters
    normed_in = low(layer_norm(row_input, gain_one))
    mixed = matmul(normed_in, qkv_weight)
    queries = low(low_back(mixed[:, :D])).reshape(-1, HEADS, HEAD_DIM)
    key_rows = low(low_back(mixed[:, D:2 * D])).reshape(-1, HEADS, HEAD_DIM)
    value_rows = low(low_back(mixed[:, 2 * D:])).reshape(-1, HEADS, HEAD_DIM)
    attended = low_back(attend(queries, key_rows, value_rows, segments))
    inner = low(layer_norm(attended, gain_two))
    state = row_input + low_back(matmul(inner, proj_weight))
    feed = low(layer_norm(state, gain_three))
    hidden = jax.nn.gelu(low_back(matmul(feed, first_weight)), approximate=False)
    hidden_in = low(layer_norm(hidden, gain_four))
    return state + low_back(matmul(hidden_in, second_weight))

def reference(tokens, segment_ids, cotangent, query_key_value, out_weight, up_weight, down_weight, attend_gain, inner_gain, feed_gain, hidden_gain):
    weights = (query_key_value.astype(jnp.float32), out_weight.astype(jnp.float32), up_weight.astype(jnp.float32), down_weight.astype(jnp.float32), attend_gain.astype(jnp.float32), inner_gain.astype(jnp.float32), feed_gain.astype(jnp.float32), hidden_gain.astype(jnp.float32))

    def per_row(grad_sums, row_item):
        row_values, row_segments, upstream = row_item
        result, backward = jax.vjp(lambda row_input, parameters: forward(row_input, row_segments, parameters), row_values.astype(jnp.float32), weights)
        row_grad, param_grads = backward(upstream.astype(jnp.float32))
        grad_sums = jax.tree.map(lambda running, extra: running + extra, grad_sums, param_grads)
        return (grad_sums, (result.astype(jnp.bfloat16), row_grad.astype(jnp.bfloat16)))
    start_sums = jax.tree.map(jnp.zeros_like, weights)
    grad_sums, outputs = lax.scan(per_row, start_sums, (tokens, segment_ids, cotangent))
    return (outputs[0], outputs[1], grad_sums[0], grad_sums[1], grad_sums[2], grad_sums[3], grad_sums[4], grad_sums[5], grad_sums[6], grad_sums[7])
```

```python
import functools
import math

import jax
import jax.numpy as jnp
from jax import lax
from jax.experimental import pallas as pl
from jax.experimental.pallas import tpu as pltpu
from jax.sharding import PartitionSpec as P

D = 768
HEADS = 12
HEAD_DIM = 64


EPSILON = 1e-05
MASKED = -1e30


def passed_along(value, axis, steps):
    count = lax.axis_size(axis)
    initial, last = (max(0, -steps), min(count, count - steps))
    return lax.ppermute(value, axis, [(source, source + steps) for source in range(initial, last)])


def from_behind(value, axis, steps):
    count = lax.axis_size(axis)
    pairs = [(source, (source + steps) % count) for source in range(count)]
    return lax.ppermute(value, axis, pairs)


def layer_norm(values, gain):
    average = jnp.mean(values, axis=-1, keepdims=True)
    centred = values - average
    inverse = lax.rsqrt(jnp.mean(centred * centred, axis=-1, keepdims=True) + EPSILON)
    normed = centred * inverse
    return (normed * gain, normed, inverse)


def norm_back(upstream, normed, inverse, gain):
    scaled = upstream * gain
    spread = (
        scaled
        - jnp.mean(scaled, axis=-1, keepdims=True)
        - normed * jnp.mean(scaled * normed, axis=-1, keepdims=True)
    )
    return (spread * inverse, jnp.sum(upstream * normed, axis=0))


def gelu_exact(values):
    return jax.nn.gelu(values, approximate=False)


def matmul(left, right):
    return jnp.dot(left, right, preferred_element_type=jnp.float32)


def left_t(left, right):
    return lax.dot_general(
        left, right, (((0,), (0,)), ((), ())), preferred_element_type=jnp.float32
    )


def right_t(left, right):
    return lax.dot_general(
        left, right, (((1,), (1,)), ((), ())), preferred_element_type=jnp.float32
    )


def split_heads(values):
    return values.reshape(values.shape[0], values.shape[1], HEADS, HEAD_DIM)


def allowed_pairs(query_pos, query_seg, key_pos, key_seg):
    causal = key_pos[None, None, None, :] <= query_pos[None, None, :, None]
    same_doc = key_seg[:, None, None, :] == query_seg[:, None, :, None]
    return causal & same_doc


def scores(queries, key_rows):
    return jnp.einsum(
        "rqhd,rkhd->rhqk",
        split_heads(queries),
        split_heads(key_rows),
        preferred_element_type=jnp.float32,
    ) * HEAD_DIM ** (-0.5)


def fold_keys(carry, piece, queries, query_pos, query_seg, segment_ids):
    key_rows, value_rows = piece
    row_count = key_rows.shape[0]
    key_count = key_rows.shape[1]
    block_width = math.gcd(key_count, queries.shape[1])
    block_count = key_count // block_width
    key_blocks = key_rows.reshape(row_count, block_count, block_width, D).transpose(1, 0, 2, 3)
    value_blocks = value_rows.reshape(row_count, block_count, block_width, D).transpose(1, 0, 2, 3)

    def one_block(state, block_item):
        accum, running, softmax_total = state
        key_block, value_block, offset = block_item
        key_start = offset * block_width
        key_pos = key_start + jnp.arange(block_width, dtype=jnp.int32)
        key_seg = lax.dynamic_slice_in_dim(segment_ids, key_start, block_width, 1)
        allowed = allowed_pairs(query_pos, query_seg, key_pos, key_seg)
        logits = jnp.where(allowed, scores(queries, key_block), MASKED)
        new_peak = jnp.maximum(running, jnp.max(logits, axis=-1))
        weights = jnp.where(allowed, jnp.exp(logits - new_peak[..., None]), 0.0)
        factor = jnp.exp(running - new_peak)
        softmax_total = softmax_total * factor + jnp.sum(weights, axis=-1)
        accum = accum * factor[..., None] + jnp.einsum(
            "rhqk,rkhd->rhqd",
            weights.astype(jnp.bfloat16),
            split_heads(value_block),
            preferred_element_type=jnp.float32,
        )
        return ((accum, new_peak, softmax_total), None)

    carry, unused = lax.scan(
        one_block, carry, (key_blocks, value_blocks, jnp.arange(block_count, dtype=jnp.int32))
    )
    return carry


def back_block(queries, grad_rows, log_total, delta, key_rows, value_rows, allowed):
    logits = jnp.where(allowed, scores(queries, key_rows), MASKED)
    probs = jnp.where(allowed, jnp.exp(logits - log_total[..., None]), 0.0)
    dprobs = jnp.einsum(
        "rqhd,rkhd->rhqk",
        split_heads(grad_rows),
        split_heads(value_rows),
        preferred_element_type=jnp.float32,
    )
    dlogits = (probs * (dprobs - delta[..., None])).astype(jnp.bfloat16)
    factor = HEAD_DIM ** (-0.5)
    query_part = (
        jnp.einsum(
            "rhqk,rkhd->rqhd", dlogits, split_heads(key_rows), preferred_element_type=jnp.float32
        )
        * factor
    )
    key_part = (
        jnp.einsum(
            "rhqk,rqhd->rkhd", dlogits, split_heads(queries), preferred_element_type=jnp.float32
        )
        * factor
    )
    value_part = jnp.einsum(
        "rhqk,rqhd->rkhd",
        probs.astype(jnp.bfloat16),
        split_heads(grad_rows),
        preferred_element_type=jnp.float32,
    )
    return (
        query_part.reshape(queries.shape),
        key_part.reshape(key_rows.shape),
        value_part.reshape(value_rows.shape),
    )


def ring_layer(
    tokens,
    segment_ids,
    cotangent,
    query_key_value,
    out_weight,
    up_weight,
    down_weight,
    attend_gain,
    inner_gain,
    feed_gain,
    hidden_gain,
):
    row_count = tokens.shape[0]
    width_q = tokens.shape[1]
    model_width = tokens.shape[2]
    token_count = row_count * width_q
    seq_index = lax.axis_index("seq")
    seq_size = lax.axis_size("seq")
    local_pos = seq_index * width_q + jnp.arange(width_q, dtype=jnp.int32)
    local_seg = lax.dynamic_slice_in_dim(segment_ids, seq_index * width_q, width_q, 1)
    residual = tokens.reshape(token_count, model_width).astype(jnp.float32)
    attend_out, attend_normed, attend_inverse = layer_norm(residual, attend_gain)
    attend_low = attend_out.astype(jnp.bfloat16)
    projected = matmul(attend_low, query_key_value).astype(jnp.bfloat16)
    queries = projected[:, :model_width].reshape(row_count, width_q, model_width)
    key_rows = projected[:, model_width : 2 * model_width].reshape(row_count, width_q, model_width)
    value_rows = projected[:, 2 * model_width :].reshape(row_count, width_q, model_width)
    start_state = (
        jnp.zeros((row_count, HEADS, width_q, HEAD_DIM), jnp.float32),
        jnp.full((row_count, HEADS, width_q), MASKED, jnp.float32),
        jnp.zeros((row_count, HEADS, width_q), jnp.float32),
    )
    accum, running, softmax_total = fold_keys(
        start_state,
        (
            lax.all_gather(key_rows, "seq", axis=1, tiled=True),
            lax.all_gather(value_rows, "seq", axis=1, tiled=True),
        ),
        queries,
        local_pos,
        local_seg,
        segment_ids,
    )
    log_total = running + jnp.log(softmax_total)
    attended = (accum / softmax_total[..., None]).transpose(0, 2, 1, 3)
    attended_flat = attended.reshape(token_count, model_width)
    inner_out, inner_normed, inner_inverse = layer_norm(attended_flat, inner_gain)
    inner_low = inner_out.astype(jnp.bfloat16)
    state = residual + matmul(inner_low, out_weight)
    feed_out, feed_normed, feed_inverse = layer_norm(state, feed_gain)
    feed_low = feed_out.astype(jnp.bfloat16)
    pre_act = matmul(feed_low, up_weight)
    hidden, gelu_back = jax.vjp(gelu_exact, pre_act)
    hidden_out, hidden_normed, hidden_inverse = layer_norm(hidden, hidden_gain)
    hidden_low = hidden_out.astype(jnp.bfloat16)
    result = state + matmul(hidden_low, down_weight)
    output = result.astype(jnp.bfloat16).reshape(tokens.shape)
    upstream_low = cotangent.reshape(token_count, model_width)
    upstream = upstream_low.astype(jnp.float32)
    down_term = left_t(hidden_low, upstream_low)
    hidden_grad, hidden_gain_term = norm_back(
        right_t(upstream_low, down_weight), hidden_normed, hidden_inverse, hidden_gain
    )
    pre_grad = gelu_back(hidden_grad)[0]
    pre_low = pre_grad.astype(jnp.bfloat16)
    up_term = left_t(feed_low, pre_low)
    feed_grad, feed_gain_term = norm_back(
        right_t(pre_low, up_weight), feed_normed, feed_inverse, feed_gain
    )
    state_grad = upstream + feed_grad
    state_low = state_grad.astype(jnp.bfloat16)
    out_term = left_t(inner_low, state_low)
    inner_grad, inner_gain_term = norm_back(
        right_t(state_low, out_weight), inner_normed, inner_inverse, inner_gain
    )
    attend_grad_low = inner_grad.astype(jnp.bfloat16).reshape(row_count, width_q, model_width)
    delta = jnp.sum(split_heads(attend_grad_low).astype(jnp.float32) * attended, axis=-1).transpose(
        0, 2, 1
    )
    zero_rows = jnp.zeros((row_count, width_q, model_width), jnp.float32)

    def key_step(step_count, cycle_state):
        moving_keys, moving_values, moving_dkeys, moving_dvalues, query_acc = cycle_state
        source = jnp.remainder(seq_index - step_count, seq_size)
        key_start = source * width_q
        key_pos = key_start + jnp.arange(width_q, dtype=jnp.int32)
        key_seg = lax.dynamic_slice_in_dim(segment_ids, key_start, width_q, 1)
        allowed = allowed_pairs(local_pos, local_seg, key_pos, key_seg)
        query_part, key_part, value_part = back_block(
            queries, attend_grad_low, log_total, delta, moving_keys, moving_values, allowed
        )
        moving_keys, moving_values = passed_along((moving_keys, moving_values), "seq", 1)
        moving_dkeys, moving_dvalues = (
            from_behind((moving_dkeys + key_part).astype(jnp.bfloat16), "seq", 1).astype(
                jnp.float32
            ),
            from_behind((moving_dvalues + value_part).astype(jnp.bfloat16), "seq", 1).astype(
                jnp.float32
            ),
        )
        return (moving_keys, moving_values, moving_dkeys, moving_dvalues, query_acc + query_part)

    cycle_out = lax.fori_loop(
        0, seq_size, key_step, (key_rows, value_rows, zero_rows, zero_rows, zero_rows)
    )
    key_grad, value_grad, query_grad = (cycle_out[2], cycle_out[3], cycle_out[4])
    joined_grad = jnp.concatenate(
        [
            query_grad.astype(jnp.bfloat16),
            key_grad.astype(jnp.bfloat16),
            value_grad.astype(jnp.bfloat16),
        ],
        axis=-1,
    ).reshape(token_count, 3 * model_width)
    qkv_term = left_t(attend_low, joined_grad)
    attend_back, attend_gain_term = norm_back(
        right_t(joined_grad, query_key_value), attend_normed, attend_inverse, attend_gain
    )
    tokens_grad = (state_grad + attend_back).astype(jnp.bfloat16).reshape(tokens.shape)
    all_sectioned = (
        lax.psum_scatter(
            qkv_term.astype(jnp.bfloat16), "rows", scatter_dimension=0, tiled=True
        ).astype(jnp.float32),
        lax.psum_scatter(
            out_term.astype(jnp.bfloat16), "rows", scatter_dimension=0, tiled=True
        ).astype(jnp.float32),
        lax.psum_scatter(
            up_term.astype(jnp.bfloat16), "rows", scatter_dimension=0, tiled=True
        ).astype(jnp.float32),
        lax.psum_scatter(
            down_term.astype(jnp.bfloat16), "rows", scatter_dimension=0, tiled=True
        ).astype(jnp.float32),
    )
    seq_sectioned = (
        lax.psum_scatter(
            all_sectioned[0].astype(jnp.bfloat16), "seq", scatter_dimension=1, tiled=True
        ).astype(jnp.float32),
        lax.psum_scatter(
            all_sectioned[1].astype(jnp.bfloat16), "seq", scatter_dimension=1, tiled=True
        ).astype(jnp.float32),
        lax.psum_scatter(
            all_sectioned[2].astype(jnp.bfloat16), "seq", scatter_dimension=1, tiled=True
        ).astype(jnp.float32),
        lax.psum_scatter(
            all_sectioned[3].astype(jnp.bfloat16), "seq", scatter_dimension=1, tiled=True
        ).astype(jnp.float32),
    )
    seq_whole = (
        lax.all_gather(seq_sectioned[0].astype(jnp.bfloat16), "seq", axis=1, tiled=True).astype(
            jnp.float32
        ),
        lax.all_gather(seq_sectioned[1].astype(jnp.bfloat16), "seq", axis=1, tiled=True).astype(
            jnp.float32
        ),
        lax.all_gather(seq_sectioned[2].astype(jnp.bfloat16), "seq", axis=1, tiled=True).astype(
            jnp.float32
        ),
        lax.all_gather(seq_sectioned[3].astype(jnp.bfloat16), "seq", axis=1, tiled=True).astype(
            jnp.float32
        ),
    )
    qkv_grad, out_grad, up_grad, down_grad = (
        lax.all_gather(seq_whole[0].astype(jnp.bfloat16), "rows", axis=0, tiled=True).astype(
            jnp.float32
        ),
        lax.all_gather(seq_whole[1].astype(jnp.bfloat16), "rows", axis=0, tiled=True).astype(
            jnp.float32
        ),
        lax.all_gather(seq_whole[2].astype(jnp.bfloat16), "rows", axis=0, tiled=True).astype(
            jnp.float32
        ),
        lax.all_gather(seq_whole[3].astype(jnp.bfloat16), "rows", axis=0, tiled=True).astype(
            jnp.float32
        ),
    )
    attend_total, inner_total, feed_total, hidden_total = lax.psum(
        (attend_gain_term, inner_gain_term, feed_gain_term, hidden_gain_term), ("rows", "seq")
    )
    return (
        output,
        tokens_grad,
        qkv_grad,
        out_grad,
        up_grad,
        down_grad,
        attend_total,
        inner_total,
        feed_total,
        hidden_total,
    )


FF = 3072
SEQ = 4
BLOCK = 512
HEADS_OWN = HEADS // SEQ
GROUP = HEADS_OWN * 3 * HEAD_DIM
MESH = pl.DeviceIdType.MESH
F32 = jnp.float32
BF16 = jnp.bfloat16
VMEM_LIMIT = 56 * 2**20


def causal_mask(key_start, key_count, query_count):
    key_pos = lax.broadcasted_iota(jnp.int32, (key_count, query_count), 0) + key_start
    query_pos = lax.broadcasted_iota(jnp.int32, (key_count, query_count), 1)
    return key_pos <= query_pos


def attend_kernel(block_count, qkv_ref, o_ref, lse_ref):
    for query_block in range(block_count):
        here = slice(query_block * BLOCK, (query_block + 1) * BLOCK)
        queries = (qkv_ref[0:64, here].astype(F32) * 0.125).astype(BF16)
        peak = jnp.full((1, BLOCK), MASKED, F32)
        total = jnp.zeros((1, BLOCK), F32)
        accum = jnp.zeros((64, BLOCK), F32)
        for key_block in range(query_block + 1):
            there = slice(key_block * BLOCK, (key_block + 1) * BLOCK)
            logits = matmul(qkv_ref[64:128, there].T, queries)
            if key_block == query_block:
                logits = jnp.where(causal_mask(0, BLOCK, BLOCK), logits, MASKED)
            new_peak = jnp.maximum(peak, jnp.max(logits, axis=0, keepdims=True))
            weights = jnp.exp(logits - new_peak)
            factor = jnp.exp(peak - new_peak)
            total = total * factor + jnp.sum(weights, axis=0, keepdims=True)
            accum = accum * factor + matmul(qkv_ref[128:192, there], weights.astype(BF16))
            peak = new_peak
        o_ref[:, here] = accum / total
        lse_ref[0:1, here] = peak + jnp.log(total)


def attend_forward(qkv, heads):
    length = qkv.shape[1]
    pairs = heads * length * (length + BLOCK) // 2
    return pl.pallas_call(
        functools.partial(attend_kernel, length // BLOCK),
        grid=(heads,),
        in_specs=[pl.BlockSpec((192, length), lambda h: (h, 0))],
        out_specs=[
            pl.BlockSpec((64, length), lambda h: (h, 0)),
            pl.BlockSpec((8, length), lambda h: (h, 0)),
        ],
        out_shape=[
            jax.ShapeDtypeStruct((heads * 64, length), F32),
            jax.ShapeDtypeStruct((heads * 8, length), F32),
        ],
        compiler_params=pltpu.CompilerParams(vmem_limit_bytes=VMEM_LIMIT),
        cost_estimate=pl.CostEstimate(
            flops=pairs * 1024, bytes_accessed=heads * length * 700, transcendentals=pairs
        ),
    )(qkv)


def attend_back_kernel(block_count, qkv_ref, o_ref, lse_ref, do_ref, d_ref, dk_acc, dv_acc):
    dk_acc[...] = jnp.zeros_like(dk_acc)
    dv_acc[...] = jnp.zeros_like(dv_acc)
    for query_block in range(block_count):
        here = slice(query_block * BLOCK, (query_block + 1) * BLOCK)
        queries_t = (qkv_ref[0:64, here].astype(F32) * 0.125).astype(BF16)
        queries = queries_t.T
        do_t = do_ref[:, here]
        do_rows = do_t.T
        lse = lse_ref[0:1, here]
        delta = jnp.sum(do_t.astype(F32) * o_ref[:, here], axis=0, keepdims=True)
        dq = jnp.zeros((64, BLOCK), F32)
        for key_block in range(query_block + 1):
            there = slice(key_block * BLOCK, (key_block + 1) * BLOCK)
            keys_t = qkv_ref[64:128, there]
            probs = jnp.exp(matmul(keys_t.T, queries_t) - lse)
            if key_block == query_block:
                probs = jnp.where(causal_mask(0, BLOCK, BLOCK), probs, 0.0)
            dprobs = matmul(qkv_ref[128:192, there].T, do_t)
            dlogits = (probs * (dprobs - delta)).astype(BF16)
            dq = dq + matmul(keys_t, dlogits)
            dv_acc[there, :] += matmul(probs.astype(BF16), do_rows)
            dk_acc[there, :] += matmul(dlogits, queries)
        d_ref[0:64, here] = (dq * 0.125).astype(BF16)
    d_ref[64:128, :] = dk_acc[...].T.astype(BF16)
    d_ref[128:192, :] = dv_acc[...].T.astype(BF16)


def attend_backward(qkv, o_t, lse, do_t, heads):
    length = qkv.shape[1]
    pairs = heads * length * (length + BLOCK) // 2
    spec = lambda rows: pl.BlockSpec((rows, length), lambda h: (h, 0))
    return pl.pallas_call(
        functools.partial(attend_back_kernel, length // BLOCK),
        grid=(heads,),
        in_specs=[spec(192), spec(64), spec(8), spec(64)],
        out_specs=spec(192),
        out_shape=jax.ShapeDtypeStruct((heads * 192, length), BF16),
        scratch_shapes=[pltpu.VMEM((length, 64), F32), pltpu.VMEM((length, 64), F32)],
        compiler_params=pltpu.CompilerParams(vmem_limit_bytes=VMEM_LIMIT),
        cost_estimate=pl.CostEstimate(
            flops=pairs * 2048, bytes_accessed=heads * length * 1300, transcendentals=pairs
        ),
    )(qkv, o_t, lse, do_t)


def widened(gain, width):
    return jnp.concatenate([gain] * (width // 128), axis=1)


def column_stats(values):
    size = values.shape[0]
    average = jnp.sum(values, axis=0, keepdims=True) * (1.0 / size)
    centred = values - average
    spread = jnp.sum(centred * centred, axis=0, keepdims=True) * (1.0 / size)
    return average, lax.rsqrt(spread + EPSILON)


def gelu_both(values):
    t = 1.0 / (1.0 + (0.3275911 * 0.7071067811865476) * jnp.abs(values))
    density = jnp.exp(-0.5 * (values * values))
    tail = 0.5 * -1.453152027 + t * (0.5 * 1.061405429)
    tail = 0.5 * 1.421413741 + t * tail
    tail = 0.5 * -0.284496736 + t * tail
    tail = 0.5 * 0.254829592 + t * tail
    tail = tail * t * density
    below = jnp.where(values >= 0, 1.0 - tail, tail)
    return values * below, below + values * (density * 0.3989422804014327)


def feed_kernel(steps, chunk, sub, has_partial, *refs):
    names = iter(refs)
    o_ref, x_ref, dy_ref, ig_ref, fg_ref, hg_ref, wo_t, wo, wu_t, wd, wd_t, wu = [
        next(names) for _ in range(12)
    ]
    if has_partial:
        part_d, part_u, part_o = [next(names) for _ in range(3)]
    out_ref, dh_ref, do_ref, gd_ref, gu_ref, go_ref = [next(names) for _ in range(6)]
    b_s, h_s, c_s, cn_s, dyt_s, n_s, slope_s, t_s, out_s, dc_s, st = [next(names) for _ in range(11)]
    width = x_ref.shape[0]
    step = pl.program_id(0)

    @pl.when(step == 0)
    def _():
        o = o_ref[...].astype(F32)
        average, inverse = column_stats(o)
        b = ((o - average) * inverse * widened(ig_ref[...], width)).astype(BF16)
        b_s[...] = b
        st[0:1] = average
        st[1:2] = inverse
        dyt_s[...] = dy_ref[...].T
        h = x_ref[...].T.astype(F32) + matmul(wo_t[...], b)
        h_s[...] = h
        average, inverse = column_stats(h)
        st[2:3] = average
        st[3:4] = inverse
        c = ((h - average) * inverse * widened(fg_ref[...], width)).astype(BF16)
        c_s[...] = c
        cn_s[...] = c.T

    @pl.when(step < steps)
    def _():
        base = pl.multiple_of(step * chunk, chunk)
        for k in range(chunk // sub):
            z, slope = gelu_both(matmul(wu_t[k * sub : (k + 1) * sub, :], c_s[...]))
            n_s[pl.ds(base + k * sub, sub), :] = z
            slope_s[pl.ds(base + k * sub, sub), :] = slope.astype(BF16)

    @pl.when(step == steps - 1)
    def _():
        total = jnp.zeros((1, width), F32)
        for k in range(FF // sub):
            total = total + jnp.sum(n_s[k * sub : (k + 1) * sub, :], axis=0, keepdims=True)
        average = total * (1.0 / FF)
        total = jnp.zeros((1, width), F32)
        for k in range(FF // sub):
            centred = n_s[k * sub : (k + 1) * sub, :] - average
            total = total + jnp.sum(centred * centred, axis=0, keepdims=True)
        st[4:5] = average
        st[5:6] = lax.rsqrt(total * (1.0 / FF) + EPSILON)
        st[6:8] = jnp.zeros((2, width), F32)
        out_s[...] = h_s[...]

    @pl.when((step >= steps) & (step < 2 * steps))
    def _():
        base = pl.multiple_of((step - steps) * chunk, chunk)
        average = st[4:5]
        inverse = st[5:6]
        first = jnp.zeros((1, width), F32)
        second = jnp.zeros((1, width), F32)
        pieces = []
        for k in range(chunk // sub):
            rows = slice(k * sub, (k + 1) * sub)
            n = (n_s[pl.ds(base + k * sub, sub), :] - average) * inverse
            n_s[pl.ds(base + k * sub, sub), :] = n
            gain = widened(hg_ref[rows, :], width)
            e = (n * gain).astype(BF16)
            pieces.append(e)
            t = matmul(wd[rows, :], dyt_s[...]) * gain
            t_s[pl.ds(base + k * sub, sub), :] = t
            first = first + jnp.sum(t, axis=0, keepdims=True)
            second = second + jnp.sum(t * n, axis=0, keepdims=True)
            grad = matmul(e, dy_ref[...])
            if has_partial:
                grad = grad + part_d[rows, :]
            gd_ref[rows, :] = grad.astype(gd_ref.dtype)
        out_s[...] += matmul(wd_t[...], jnp.concatenate(pieces, axis=0))
        st[6:7] += first
        st[7:8] += second

    @pl.when(step == 2 * steps - 1)
    def _():
        out_ref[...] = out_s[...].astype(BF16).T
        st[6:8] = st[6:8] * (1.0 / FF)
        dc_s[...] = jnp.zeros_like(dc_s)

    @pl.when(step >= 2 * steps)
    def _():
        base = pl.multiple_of((step - 2 * steps) * chunk, chunk)
        inverse = st[5:6]
        first = st[6:7]
        second = st[7:8]
        pieces = []
        for k in range(chunk // sub):
            rows = pl.ds(base + k * sub, sub)
            n = n_s[rows, :]
            du = ((t_s[rows, :] - first - n * second) * inverse * slope_s[rows, :].astype(F32)).astype(BF16)
            pieces.append(du)
            grad = matmul(du, cn_s[...])
            if has_partial:
                grad = grad + part_u[k * sub : (k + 1) * sub, :]
            gu_ref[k * sub : (k + 1) * sub, :] = grad.astype(gu_ref.dtype)
        dc_s[...] += matmul(wu[...], jnp.concatenate(pieces, axis=0))

    @pl.when(step == 3 * steps - 1)
    def _():
        n = (h_s[...] - st[2:3]) * st[3:4]
        t = dc_s[...] * widened(fg_ref[...], width)
        first = jnp.sum(t, axis=0, keepdims=True) * (1.0 / D)
        second = jnp.sum(t * n, axis=0, keepdims=True) * (1.0 / D)
        dh = dyt_s[...].astype(F32) + (t - first - n * second) * st[3:4]
        dh_rows = dh.T
        dh_ref[...] = dh_rows
        grad = matmul(b_s[...], dh_rows.astype(BF16))
        if has_partial:
            grad = grad + part_o[...]
        go_ref[...] = grad.astype(go_ref.dtype)
        n = (o_ref[...].astype(F32) - st[0:1]) * st[1:2]
        t = matmul(wo[...], dh.astype(BF16)) * widened(ig_ref[...], width)
        first = jnp.sum(t, axis=0, keepdims=True) * (1.0 / D)
        second = jnp.sum(t * n, axis=0, keepdims=True) * (1.0 / D)
        do_ref[...] = ((t - first - n * second) * st[1:2]).astype(BF16)


def feed_both(o_t, x, dy, gains, weights, partial=None, chunk=768, sub=256):
    width = x.shape[0]
    steps = FF // chunk
    has_partial = partial is not None
    once = lambda *shape: pl.BlockSpec(shape, lambda i: (0, 0), pipeline_mode=pl.Buffered(1))
    first = lambda i: jnp.clip(i, 0, steps - 1)
    second = lambda i: jnp.clip(i - steps, 0, steps - 1)
    third = lambda i: jnp.clip(i - 2 * steps, 0, steps - 1)
    by_rows = lambda phase: pl.BlockSpec((chunk, D), lambda i: (phase(i), 0))
    by_columns = lambda phase: pl.BlockSpec((D, chunk), lambda i: (0, phase(i)))
    in_specs = [once(D, width), once(width, D), once(width, D), once(D, 128), once(D, 128)]
    in_specs += [pl.BlockSpec((chunk, 128), lambda i: (second(i), 0)), once(D, D), once(D, D)]
    in_specs += [by_rows(first), by_rows(second), by_columns(second), by_columns(third)]
    args = [o_t, x, dy, *gains, *weights]
    kind = F32
    if has_partial:
        in_specs += [by_rows(second), by_rows(third), once(D, D)]
        args += list(partial)
        kind = BF16
    whole = lambda *shape: pl.BlockSpec(shape, lambda i: (0, 0))
    return pl.pallas_call(
        functools.partial(feed_kernel, steps, chunk, sub, has_partial),
        grid=(3 * steps,),
        in_specs=in_specs,
        out_specs=[
            whole(width, D),
            whole(width, D),
            whole(D, width),
            by_rows(second),
            by_rows(third),
            whole(D, D),
        ],
        out_shape=[
            jax.ShapeDtypeStruct((width, D), BF16),
            jax.ShapeDtypeStruct((width, D), F32),
            jax.ShapeDtypeStruct((D, width), BF16),
            jax.ShapeDtypeStruct((FF, D), kind),
            jax.ShapeDtypeStruct((FF, D), kind),
            jax.ShapeDtypeStruct((D, D), kind),
        ],
        scratch_shapes=[
            pltpu.VMEM((D, width), BF16),
            pltpu.VMEM((D, width), F32),
            pltpu.VMEM((D, width), BF16),
            pltpu.VMEM((width, D), BF16),
            pltpu.VMEM((D, width), BF16),
            pltpu.VMEM((FF, width), F32),
            pltpu.VMEM((FF, width), BF16),
            pltpu.VMEM((FF, width), F32),
            pltpu.VMEM((D, width), F32),
            pltpu.VMEM((D, width), F32),
            pltpu.VMEM((8, width), F32),
        ],
        compiler_params=pltpu.CompilerParams(vmem_limit_bytes=62 * 2**20),
        cost_estimate=pl.CostEstimate(
            flops=6 * width * D * (D + 2 * FF), bytes_accessed=80 * 2**20, transcendentals=width * FF
        ),
    )(*args)


PIECE = 768
HALF = PIECE // 2
COLS = D // 2


def sum_kernel(counts, *refs):
    piece_count = sum(counts)
    grads = refs[: len(counts)]
    out_ref, own, r0, r1, r2, r3, r4, fin, own_sem, send_sem, recv_sem, fin_sem = refs[len(counts) :]
    r = lax.axis_index("rows")
    s = lax.axis_index("seq")
    core, xb, yb, z_low, z_high = r % 2, (r // 2) % 2, r // 4, s % 2, s // 2
    to_core = (r + 1 - 2 * core, s)
    to_x = (r + 2 - 4 * xb, s)
    to_y = (r + 4 - 8 * yb, s)
    to_z_low = (r, s + 1 - 2 * z_low)
    to_z_high = (r, s + 2 - 4 * z_high)
    barrier = pltpu.get_barrier_semaphore()
    for device in (to_core, to_x, to_y, to_z_low, to_z_high):
        pl.semaphore_signal(barrier, inc=1, device_id=device, device_id_type=MESH)
    pl.semaphore_wait(barrier, 5)
    bits = [(xb, yb), (yb, xb)]
    partners = [(to_x, to_y), (to_y, to_x)]

    def rows_at(start, count):
        return pl.ds(pl.multiple_of(start, 16), count)

    def remote(source, target, kind, p, device):
        return pltpu.make_async_remote_copy(
            src_ref=source,
            dst_ref=target,
            send_sem=send_sem.at[kind, p],
            recv_sem=recv_sem.at[kind, p],
            device_id=device,
            device_id_type=MESH,
        )

    def columns(o):
        return slice(o * COLS, (o + 1) * COLS)

    def base(o):
        return bits[o][0] * 192 + bits[o][1] * 96

    def core_copy(ref, q, p):
        return remote(ref.at[rows_at(q * PIECE + (1 - core) * HALF, HALF), :], r0.at[p], 0, p, to_core)

    def own_copy(ref, q, p):
        return pltpu.make_async_copy(
            ref.at[rows_at(q * PIECE + core * HALF, HALF), :], own.at[p], own_sem.at[p]
        )

    def first_copy(p, o):
        part = own.at[p, rows_at((1 - bits[o][0]) * 192, 192), columns(o)]
        return remote(part, r1.at[p, o], 1 + o, p, partners[o][0])

    def second_copy(p, o):
        part = own.at[p, rows_at(bits[o][0] * 192 + (1 - bits[o][1]) * 96, 96), columns(o)]
        return remote(part, r2.at[p, o], 3 + o, p, partners[o][1])

    def low_copy(p, o):
        part = own.at[p, rows_at(base(o) + (1 - z_low) * 48, 48), columns(o)]
        return remote(part, r3.at[p, o], 5 + o, p, to_z_low)

    def high_copy(p, o):
        part = own.at[p, rows_at(base(o) + z_low * 48, 48), columns(o)]
        return remote(part, r4.at[p, o], 7 + o, p, to_z_high)

    def region(p, start, count, o):
        return out_ref.at[rows_at(p * PIECE + core * HALF + start, count), columns(o)]

    def fin_copy(p, o):
        return pltpu.make_async_copy(
            fin.at[p, o], region(p, base(o) + z_low * 48, 48, o), fin_sem.at[o, p]
        )

    def low_back(p, o):
        return remote(fin.at[p, o], region(p, base(o) + z_low * 48, 48, o), 9 + o, p, to_z_low)

    def second_back(p, o):
        part = region(p, base(o), 96, o)
        return remote(part, part, 11 + o, p, partners[o][1])

    def first_back(p, o):
        part = region(p, bits[o][0] * 192, 192, o)
        return remote(part, part, 13 + o, p, partners[o][0])

    def core_back(p):
        part = out_ref.at[rows_at(p * PIECE + core * HALF, HALF), :]
        return remote(part, part, 15, p, to_core)

    offset = 0
    for ref, count in zip(grads, counts):

        def begin(q, carry, ref=ref, offset=offset):
            core_copy(ref, q, q + offset).start()
            own_copy(ref, q, q + offset).start()
            return carry

        lax.fori_loop(0, count, begin, 0)
        offset += count

    def added(index, other):
        own[index] = (own[index].astype(F32) + other.astype(F32)).astype(BF16)

    def after_core(p):
        own_copy(grads[0], 0, p).wait()
        core_copy(grads[0], 0, p).wait()
        own[p] = (own[p].astype(F32) + r0[p].astype(F32)).astype(BF16)
        for o in range(2):
            first_copy(p, o).start()

    def after_first(p):
        for o in range(2):
            first_copy(p, o).wait()
            added((p, rows_at(bits[o][0] * 192, 192), columns(o)), r1[p, o])
            second_copy(p, o).start()

    def after_second(p):
        for o in range(2):
            second_copy(p, o).wait()
            added((p, rows_at(base(o), 96), columns(o)), r2[p, o])
            low_copy(p, o).start()

    def after_low(p):
        for o in range(2):
            low_copy(p, o).wait()
            added((p, rows_at(base(o) + z_low * 48, 48), columns(o)), r3[p, o])
            high_copy(p, o).start()

    def after_high(p):
        for o in range(2):
            high_copy(p, o).wait()
            mine = own[p, rows_at(base(o) + z_low * 48, 48), columns(o)].astype(F32)
            fin[p, o] = (mine + r4[p, o].astype(F32)).astype(BF16)
            low_back(p, o).start()
            fin_copy(p, o).start()

    def after_low_back(p):
        for o in range(2):
            fin_copy(p, o).wait()
            low_back(p, o).wait()
            second_back(p, o).start()

    def after_second_back(p):
        for o in range(2):
            second_back(p, o).wait()
            first_back(p, o).start()

    def after_first_back(p):
        for o in range(2):
            first_back(p, o).wait()
        core_back(p).start()

    def after_core_back(p):
        core_back(p).wait()

    stages = [
        after_core,
        after_first,
        after_second,
        after_low,
        after_high,
        after_low_back,
        after_second_back,
        after_first_back,
        after_core_back,
    ]

    def tick(t, carry):
        for lag, stage in enumerate(stages):
            p = t - lag

            @pl.when((p >= 0) & (p < piece_count))
            def _():
                stage(p)

        return carry

    lax.fori_loop(0, piece_count + len(stages) - 1, tick, 0)


def summed_everywhere(grads, collective_id):
    counts = [grad.shape[0] // PIECE for grad in grads]
    n = sum(counts)
    dma = pltpu.SemaphoreType.DMA
    return pl.pallas_call(
        functools.partial(sum_kernel, counts),
        out_shape=jax.ShapeDtypeStruct((n * PIECE, D), BF16),
        in_specs=[pl.BlockSpec(memory_space=pl.ANY)] * len(grads),
        out_specs=pl.BlockSpec(memory_space=pl.ANY),
        scratch_shapes=[
            pltpu.VMEM((n, HALF, D), BF16),
            pltpu.VMEM((n, HALF, D), BF16),
            pltpu.VMEM((n, 2, 192, COLS), BF16),
            pltpu.VMEM((n, 2, 96, COLS), BF16),
            pltpu.VMEM((n, 2, 48, COLS), BF16),
            pltpu.VMEM((n, 2, 48, COLS), BF16),
            pltpu.VMEM((n, 2, 48, COLS), BF16),
            dma((n,)),
            dma((16, n)),
            dma((16, n)),
            dma((2, n)),
        ],
        compiler_params=pltpu.CompilerParams(
            collective_id=collective_id, has_side_effects=True, vmem_limit_bytes=VMEM_LIMIT
        ),
        cost_estimate=pl.CostEstimate(flops=0, bytes_accessed=n * PIECE * D * 64, transcendentals=0),
    )(*grads)


def exchanged(pieces, own_index):
    out = jnp.zeros_like(pieces)
    own = lax.dynamic_index_in_dim(pieces, own_index, 0, keepdims=True)
    out = lax.dynamic_update_slice_in_dim(out, own, own_index, 0)
    for shift in range(1, SEQ):
        leaving = lax.dynamic_index_in_dim(pieces, (own_index + shift) % SEQ, 0, keepdims=True)
        arrived = lax.ppermute(leaving, "seq", [(i, (i + shift) % SEQ) for i in range(SEQ)])
        out = lax.dynamic_update_slice_in_dim(out, arrived, (own_index - shift) % SEQ, 0)
    return out


def normed_rows(x, gain):
    out, normed, inverse = layer_norm(x.astype(F32), gain)
    return out.astype(BF16), normed, inverse


def layer_back(upstream, normed, inverse, gain):
    scaled = upstream * gain
    return inverse * (
        scaled
        - jnp.mean(scaled, axis=-1, keepdims=True)
        - normed * jnp.mean(scaled * normed, axis=-1, keepdims=True)
    )


def split_layer(
    tokens,
    segment_ids,
    cotangent,
    query_key_value,
    out_weight,
    up_weight,
    down_weight,
    attend_gain,
    inner_gain,
    feed_gain,
    hidden_gain,
):
    place = lax.axis_index("seq")
    long_first = segment_ids[0, -1] == 0
    x_long = jnp.where(long_first, tokens[0], tokens[1])
    x_pack = jnp.where(long_first, tokens[1], tokens[0])
    dy_long = jnp.where(long_first, cotangent[0], cotangent[1])
    dy_pack = jnp.where(long_first, cotangent[1], cotangent[0])
    ring = [(i, (i + 1) % SEQ) for i in range(SEQ)]
    x_blocks = [x_long]
    for _ in range(1, SEQ):
        x_blocks.append(lax.ppermute(x_blocks[-1], "seq", ring))
    qkv_t = query_key_value.reshape(D, 3, HEADS, HEAD_DIM).transpose(2, 1, 3, 0).reshape(3 * D, D)
    wide = lambda gain: jnp.broadcast_to(gain[:, None], (gain.shape[0], 128))
    gains = (wide(inner_gain), wide(feed_gain), wide(hidden_gain))
    weights = (out_weight.T, out_weight, up_weight.T, down_weight, down_weight.T, up_weight)
    a_pack, pack_normed, pack_inverse = normed_rows(x_pack, attend_gain)
    qkv_pack = right_t(qkv_t, a_pack).astype(BF16)
    o_pack, lse_pack = attend_forward(qkv_pack, HEADS)
    out_pack, dh_pack, do_pack, gd_pack, gu_pack, go_pack = feed_both(
        o_pack, x_pack, dy_pack, gains, weights
    )
    dqkv_pack = attend_backward(qkv_pack, o_pack, lse_pack, do_pack, HEADS)
    gq_pack = matmul(dqkv_pack, a_pack)
    dxa_pack = layer_back(left_t(dqkv_pack, qkv_t), pack_normed, pack_inverse, attend_gain)
    dx_pack = (dh_pack + dxa_pack).astype(BF16)
    own_t = lax.dynamic_slice_in_dim(qkv_t, place * GROUP, GROUP, 0)
    a_all = jnp.zeros((SEQ, BLOCK, D), BF16)
    for shift, block in enumerate(x_blocks):
        a_block, normed, inverse = normed_rows(block, attend_gain)
        if shift == 0:
            long_normed, long_inverse = normed, inverse
        a_all = lax.dynamic_update_slice_in_dim(a_all, a_block[None], (place - shift) % SEQ, 0)
    a_all = a_all.reshape(SEQ * BLOCK, D)
    qkv_long = right_t(own_t, a_all).astype(BF16)
    o_long, lse_long = attend_forward(qkv_long, HEADS_OWN)
    o_pieces = o_long.astype(BF16).reshape(HEADS_OWN * HEAD_DIM, SEQ, BLOCK).transpose(1, 0, 2)
    o_mine = exchanged(o_pieces, place).reshape(D, BLOCK)
    out_long, dh_long, do_long, gd, gu, go = feed_both(
        o_mine, x_long, dy_long, gains, weights, (gd_pack, gu_pack, go_pack)
    )
    do_own = exchanged(do_long.reshape(SEQ, HEADS_OWN * HEAD_DIM, BLOCK), place)
    do_own = do_own.transpose(1, 0, 2).reshape(HEADS_OWN * HEAD_DIM, SEQ * BLOCK)
    dqkv_own = attend_backward(qkv_long, o_long, lse_long, do_own, HEADS_OWN)
    gq_long = matmul(dqkv_own, a_all)
    gq_own = lax.dynamic_slice_in_dim(gq_pack, place * GROUP, GROUP, 0) + gq_long
    gq = lax.dynamic_update_slice_in_dim(gq_pack, gq_own, place * GROUP, 0).astype(BF16)
    dqkv_long = exchanged(dqkv_own.reshape(GROUP, SEQ, BLOCK).transpose(1, 0, 2), place)
    dqkv_long = dqkv_long.reshape(3 * D, BLOCK)
    dxa_long = layer_back(left_t(dqkv_long, qkv_t), long_normed, long_inverse, attend_gain)
    dx_long = (dh_long + dxa_long).astype(BF16)
    total = summed_everywhere((gd, gu, go, gq), 0)
    down_grad = total[:FF].astype(F32)
    up_grad_t = total[FF : 2 * FF].astype(F32)
    out_grad = total[2 * FF : 2 * FF + D].astype(F32)
    qkv_grad_t = total[2 * FF + D :].astype(F32)
    qkv_grad = qkv_grad_t.reshape(HEADS, 3, HEAD_DIM, D).transpose(3, 1, 0, 2).reshape(D, 3 * D)
    attend_total = jnp.sum(qkv_grad_t * qkv_t.astype(F32), axis=0) / attend_gain
    inner_total = jnp.sum(out_grad * out_weight.astype(F32), axis=1) / inner_gain
    feed_total = jnp.sum(up_grad_t * weights[2].astype(F32), axis=0) / feed_gain
    hidden_total = jnp.sum(down_grad * down_weight.astype(F32), axis=1) / hidden_gain
    output = jnp.where(long_first, jnp.stack([out_long, out_pack]), jnp.stack([out_pack, out_long]))
    tokens_grad = jnp.where(long_first, jnp.stack([dx_long, dx_pack]), jnp.stack([dx_pack, dx_long]))
    return (
        output,
        tokens_grad,
        qkv_grad,
        out_grad,
        up_grad_t.T,
        down_grad,
        attend_total,
        inner_total,
        feed_total,
        hidden_total,
    )


def per_device(tokens, *others):
    split = lax.axis_size("seq") == SEQ and lax.axis_size("rows") == 8
    if split and tokens.shape == (2, BLOCK, D):
        return split_layer(tokens, *others)
    return ring_layer(tokens, *others)


def solution(mesh):
    return jax.shard_map(
        per_device,
        mesh=mesh,
        in_specs=(
            P("rows", "seq", None),
            P("rows", None),
            P("rows", "seq", None),
            P(),
            P(),
            P(),
            P(),
            P(),
            P(),
            P(),
            P(),
        ),
        out_specs=(
            P("rows", "seq", None),
            P("rows", "seq", None),
            P(),
            P(),
            P(),
            P(),
            P(),
            P(),
            P(),
            P(),
        ),
        check_vma=False,
    )
```

```python
import functools
import math

import jax
import jax.numpy as jnp
from jax import lax
from jax.experimental import pallas as pl
from jax.experimental.pallas import tpu as pltpu
from jax.sharding import PartitionSpec as P

D = 768
HEADS = 12
HEAD_DIM = 64


EPSILON = 1e-05
MASKED = -1e30


def passed_along(value, axis, steps):
    count = lax.axis_size(axis)
    initial, last = (max(0, -steps), min(count, count - steps))
    return lax.ppermute(value, axis, [(source, source + steps) for source in range(initial, last)])


def from_behind(value, axis, steps):
    count = lax.axis_size(axis)
    pairs = [(source, (source + steps) % count) for source in range(count)]
    return lax.ppermute(value, axis, pairs)


def layer_norm(values, gain):
    average = jnp.mean(values, axis=-1, keepdims=True)
    centred = values - average
    inverse = lax.rsqrt(jnp.mean(centred * centred, axis=-1, keepdims=True) + EPSILON)
    normed = centred * inverse
    return (normed * gain, normed, inverse)


def norm_back(upstream, normed, inverse, gain):
    scaled = upstream * gain
    spread = (
        scaled
        - jnp.mean(scaled, axis=-1, keepdims=True)
        - normed * jnp.mean(scaled * normed, axis=-1, keepdims=True)
    )
    return (spread * inverse, jnp.sum(upstream * normed, axis=0))


def gelu_exact(values):
    return jax.nn.gelu(values, approximate=False)


def matmul(left, right):
    return jnp.dot(left, right, preferred_element_type=jnp.float32)


def left_t(left, right):
    return lax.dot_general(
        left, right, (((0,), (0,)), ((), ())), preferred_element_type=jnp.float32
    )


def right_t(left, right):
    return lax.dot_general(
        left, right, (((1,), (1,)), ((), ())), preferred_element_type=jnp.float32
    )


def split_heads(values):
    return values.reshape(values.shape[0], values.shape[1], HEADS, HEAD_DIM)


def allowed_pairs(query_pos, query_seg, key_pos, key_seg):
    causal = key_pos[None, None, None, :] <= query_pos[None, None, :, None]
    same_doc = key_seg[:, None, None, :] == query_seg[:, None, :, None]
    return causal & same_doc


def scores(queries, key_rows):
    return jnp.einsum(
        "rqhd,rkhd->rhqk",
        split_heads(queries),
        split_heads(key_rows),
        preferred_element_type=jnp.float32,
    ) * HEAD_DIM ** (-0.5)


def fold_keys(carry, piece, queries, query_pos, query_seg, segment_ids):
    key_rows, value_rows = piece
    row_count = key_rows.shape[0]
    key_count = key_rows.shape[1]
    block_width = math.gcd(key_count, queries.shape[1])
    block_count = key_count // block_width
    key_blocks = key_rows.reshape(row_count, block_count, block_width, D).transpose(1, 0, 2, 3)
    value_blocks = value_rows.reshape(row_count, block_count, block_width, D).transpose(1, 0, 2, 3)

    def one_block(state, block_item):
        accum, running, softmax_total = state
        key_block, value_block, offset = block_item
        key_start = offset * block_width
        key_pos = key_start + jnp.arange(block_width, dtype=jnp.int32)
        key_seg = lax.dynamic_slice_in_dim(segment_ids, key_start, block_width, 1)
        allowed = allowed_pairs(query_pos, query_seg, key_pos, key_seg)
        logits = jnp.where(allowed, scores(queries, key_block), MASKED)
        new_peak = jnp.maximum(running, jnp.max(logits, axis=-1))
        weights = jnp.where(allowed, jnp.exp(logits - new_peak[..., None]), 0.0)
        factor = jnp.exp(running - new_peak)
        softmax_total = softmax_total * factor + jnp.sum(weights, axis=-1)
        accum = accum * factor[..., None] + jnp.einsum(
            "rhqk,rkhd->rhqd",
            weights.astype(jnp.bfloat16),
            split_heads(value_block),
            preferred_element_type=jnp.float32,
        )
        return ((accum, new_peak, softmax_total), None)

    carry, unused = lax.scan(
        one_block, carry, (key_blocks, value_blocks, jnp.arange(block_count, dtype=jnp.int32))
    )
    return carry


def back_block(queries, grad_rows, log_total, delta, key_rows, value_rows, allowed):
    logits = jnp.where(allowed, scores(queries, key_rows), MASKED)
    probs = jnp.where(allowed, jnp.exp(logits - log_total[..., None]), 0.0)
    dprobs = jnp.einsum(
        "rqhd,rkhd->rhqk",
        split_heads(grad_rows),
        split_heads(value_rows),
        preferred_element_type=jnp.float32,
    )
    dlogits = (probs * (dprobs - delta[..., None])).astype(jnp.bfloat16)
    factor = HEAD_DIM ** (-0.5)
    query_part = (
        jnp.einsum(
            "rhqk,rkhd->rqhd", dlogits, split_heads(key_rows), preferred_element_type=jnp.float32
        )
        * factor
    )
    key_part = (
        jnp.einsum(
            "rhqk,rqhd->rkhd", dlogits, split_heads(queries), preferred_element_type=jnp.float32
        )
        * factor
    )
    value_part = jnp.einsum(
        "rhqk,rqhd->rkhd",
        probs.astype(jnp.bfloat16),
        split_heads(grad_rows),
        preferred_element_type=jnp.float32,
    )
    return (
        query_part.reshape(queries.shape),
        key_part.reshape(key_rows.shape),
        value_part.reshape(value_rows.shape),
    )


def ring_layer(
    tokens,
    segment_ids,
    cotangent,
    query_key_value,
    out_weight,
    up_weight,
    down_weight,
    attend_gain,
    inner_gain,
    feed_gain,
    hidden_gain,
):
    row_count = tokens.shape[0]
    width_q = tokens.shape[1]
    model_width = tokens.shape[2]
    token_count = row_count * width_q
    seq_index = lax.axis_index("seq")
    seq_size = lax.axis_size("seq")
    local_pos = seq_index * width_q + jnp.arange(width_q, dtype=jnp.int32)
    local_seg = lax.dynamic_slice_in_dim(segment_ids, seq_index * width_q, width_q, 1)
    residual = tokens.reshape(token_count, model_width).astype(jnp.float32)
    attend_out, attend_normed, attend_inverse = layer_norm(residual, attend_gain)
    attend_low = attend_out.astype(jnp.bfloat16)
    projected = matmul(attend_low, query_key_value).astype(jnp.bfloat16)
    queries = projected[:, :model_width].reshape(row_count, width_q, model_width)
    key_rows = projected[:, model_width : 2 * model_width].reshape(row_count, width_q, model_width)
    value_rows = projected[:, 2 * model_width :].reshape(row_count, width_q, model_width)
    start_state = (
        jnp.zeros((row_count, HEADS, width_q, HEAD_DIM), jnp.float32),
        jnp.full((row_count, HEADS, width_q), MASKED, jnp.float32),
        jnp.zeros((row_count, HEADS, width_q), jnp.float32),
    )
    accum, running, softmax_total = fold_keys(
        start_state,
        (
            lax.all_gather(key_rows, "seq", axis=1, tiled=True),
            lax.all_gather(value_rows, "seq", axis=1, tiled=True),
        ),
        queries,
        local_pos,
        local_seg,
        segment_ids,
    )
    log_total = running + jnp.log(softmax_total)
    attended = (accum / softmax_total[..., None]).transpose(0, 2, 1, 3)
    attended_flat = attended.reshape(token_count, model_width)
    inner_out, inner_normed, inner_inverse = layer_norm(attended_flat, inner_gain)
    inner_low = inner_out.astype(jnp.bfloat16)
    state = residual + matmul(inner_low, out_weight)
    feed_out, feed_normed, feed_inverse = layer_norm(state, feed_gain)
    feed_low = feed_out.astype(jnp.bfloat16)
    pre_act = matmul(feed_low, up_weight)
    hidden, gelu_back = jax.vjp(gelu_exact, pre_act)
    hidden_out, hidden_normed, hidden_inverse = layer_norm(hidden, hidden_gain)
    hidden_low = hidden_out.astype(jnp.bfloat16)
    result = state + matmul(hidden_low, down_weight)
    output = result.astype(jnp.bfloat16).reshape(tokens.shape)
    upstream_low = cotangent.reshape(token_count, model_width)
    upstream = upstream_low.astype(jnp.float32)
    down_term = left_t(hidden_low, upstream_low)
    hidden_grad, hidden_gain_term = norm_back(
        right_t(upstream_low, down_weight), hidden_normed, hidden_inverse, hidden_gain
    )
    pre_grad = gelu_back(hidden_grad)[0]
    pre_low = pre_grad.astype(jnp.bfloat16)
    up_term = left_t(feed_low, pre_low)
    feed_grad, feed_gain_term = norm_back(
        right_t(pre_low, up_weight), feed_normed, feed_inverse, feed_gain
    )
    state_grad = upstream + feed_grad
    state_low = state_grad.astype(jnp.bfloat16)
    out_term = left_t(inner_low, state_low)
    inner_grad, inner_gain_term = norm_back(
        right_t(state_low, out_weight), inner_normed, inner_inverse, inner_gain
    )
    attend_grad_low = inner_grad.astype(jnp.bfloat16).reshape(row_count, width_q, model_width)
    delta = jnp.sum(split_heads(attend_grad_low).astype(jnp.float32) * attended, axis=-1).transpose(
        0, 2, 1
    )
    zero_rows = jnp.zeros((row_count, width_q, model_width), jnp.float32)

    def key_step(step_count, cycle_state):
        moving_keys, moving_values, moving_dkeys, moving_dvalues, query_acc = cycle_state
        source = jnp.remainder(seq_index - step_count, seq_size)
        key_start = source * width_q
        key_pos = key_start + jnp.arange(width_q, dtype=jnp.int32)
        key_seg = lax.dynamic_slice_in_dim(segment_ids, key_start, width_q, 1)
        allowed = allowed_pairs(local_pos, local_seg, key_pos, key_seg)
        query_part, key_part, value_part = back_block(
            queries, attend_grad_low, log_total, delta, moving_keys, moving_values, allowed
        )
        moving_keys, moving_values = passed_along((moving_keys, moving_values), "seq", 1)
        moving_dkeys, moving_dvalues = (
            from_behind((moving_dkeys + key_part).astype(jnp.bfloat16), "seq", 1).astype(
                jnp.float32
            ),
            from_behind((moving_dvalues + value_part).astype(jnp.bfloat16), "seq", 1).astype(
                jnp.float32
            ),
        )
        return (moving_keys, moving_values, moving_dkeys, moving_dvalues, query_acc + query_part)

    cycle_out = lax.fori_loop(
        0, seq_size, key_step, (key_rows, value_rows, zero_rows, zero_rows, zero_rows)
    )
    key_grad, value_grad, query_grad = (cycle_out[2], cycle_out[3], cycle_out[4])
    joined_grad = jnp.concatenate(
        [
            query_grad.astype(jnp.bfloat16),
            key_grad.astype(jnp.bfloat16),
            value_grad.astype(jnp.bfloat16),
        ],
        axis=-1,
    ).reshape(token_count, 3 * model_width)
    qkv_term = left_t(attend_low, joined_grad)
    attend_back, attend_gain_term = norm_back(
        right_t(joined_grad, query_key_value), attend_normed, attend_inverse, attend_gain
    )
    tokens_grad = (state_grad + attend_back).astype(jnp.bfloat16).reshape(tokens.shape)
    all_sectioned = (
        lax.psum_scatter(
            qkv_term.astype(jnp.bfloat16), "rows", scatter_dimension=0, tiled=True
        ).astype(jnp.float32),
        lax.psum_scatter(
            out_term.astype(jnp.bfloat16), "rows", scatter_dimension=0, tiled=True
        ).astype(jnp.float32),
        lax.psum_scatter(
            up_term.astype(jnp.bfloat16), "rows", scatter_dimension=0, tiled=True
        ).astype(jnp.float32),
        lax.psum_scatter(
            down_term.astype(jnp.bfloat16), "rows", scatter_dimension=0, tiled=True
        ).astype(jnp.float32),
    )
    seq_sectioned = (
        lax.psum_scatter(
            all_sectioned[0].astype(jnp.bfloat16), "seq", scatter_dimension=1, tiled=True
        ).astype(jnp.float32),
        lax.psum_scatter(
            all_sectioned[1].astype(jnp.bfloat16), "seq", scatter_dimension=1, tiled=True
        ).astype(jnp.float32),
        lax.psum_scatter(
            all_sectioned[2].astype(jnp.bfloat16), "seq", scatter_dimension=1, tiled=True
        ).astype(jnp.float32),
        lax.psum_scatter(
            all_sectioned[3].astype(jnp.bfloat16), "seq", scatter_dimension=1, tiled=True
        ).astype(jnp.float32),
    )
    seq_whole = (
        lax.all_gather(seq_sectioned[0].astype(jnp.bfloat16), "seq", axis=1, tiled=True).astype(
            jnp.float32
        ),
        lax.all_gather(seq_sectioned[1].astype(jnp.bfloat16), "seq", axis=1, tiled=True).astype(
            jnp.float32
        ),
        lax.all_gather(seq_sectioned[2].astype(jnp.bfloat16), "seq", axis=1, tiled=True).astype(
            jnp.float32
        ),
        lax.all_gather(seq_sectioned[3].astype(jnp.bfloat16), "seq", axis=1, tiled=True).astype(
            jnp.float32
        ),
    )
    qkv_grad, out_grad, up_grad, down_grad = (
        lax.all_gather(seq_whole[0].astype(jnp.bfloat16), "rows", axis=0, tiled=True).astype(
            jnp.float32
        ),
        lax.all_gather(seq_whole[1].astype(jnp.bfloat16), "rows", axis=0, tiled=True).astype(
            jnp.float32
        ),
        lax.all_gather(seq_whole[2].astype(jnp.bfloat16), "rows", axis=0, tiled=True).astype(
            jnp.float32
        ),
        lax.all_gather(seq_whole[3].astype(jnp.bfloat16), "rows", axis=0, tiled=True).astype(
            jnp.float32
        ),
    )
    attend_total, inner_total, feed_total, hidden_total = lax.psum(
        (attend_gain_term, inner_gain_term, feed_gain_term, hidden_gain_term), ("rows", "seq")
    )
    return (
        output,
        tokens_grad,
        qkv_grad,
        out_grad,
        up_grad,
        down_grad,
        attend_total,
        inner_total,
        feed_total,
        hidden_total,
    )


FF = 3072
SEQ = 4
BLOCK = 512
HEADS_OWN = HEADS // SEQ
GROUP = HEADS_OWN * 3 * HEAD_DIM
MESH = pl.DeviceIdType.MESH
F32 = jnp.float32
BF16 = jnp.bfloat16
VMEM_LIMIT = 56 * 2**20


def causal_mask(key_start, key_count, query_count):
    key_pos = lax.broadcasted_iota(jnp.int32, (key_count, query_count), 0) + key_start
    query_pos = lax.broadcasted_iota(jnp.int32, (key_count, query_count), 1)
    return key_pos <= query_pos


def attend_kernel(block_count, qkv_ref, o_ref, lse_ref):
    for query_block in range(block_count):
        here = slice(query_block * BLOCK, (query_block + 1) * BLOCK)
        queries = (qkv_ref[0, :, here].astype(F32) * 0.125).astype(BF16)
        peak = jnp.full((1, BLOCK), MASKED, F32)
        total = jnp.zeros((1, BLOCK), F32)
        accum = jnp.zeros((64, BLOCK), F32)
        for key_block in range(query_block + 1):
            there = slice(key_block * BLOCK, (key_block + 1) * BLOCK)
            logits = matmul(qkv_ref[1, :, there].T, queries)
            if key_block == query_block:
                logits = jnp.where(causal_mask(0, BLOCK, BLOCK), logits, MASKED)
            new_peak = jnp.maximum(peak, jnp.max(logits, axis=0, keepdims=True))
            weights = jnp.exp(logits - new_peak)
            factor = jnp.exp(peak - new_peak)
            total = total * factor + jnp.sum(weights, axis=0, keepdims=True)
            accum = accum * factor + matmul(qkv_ref[2, :, there], weights.astype(BF16))
            peak = new_peak
        o_ref[:, here] = accum / total
        lse_ref[0:1, here] = peak + jnp.log(total)


def attend_forward(qkv, heads):
    length = qkv.shape[2]
    pairs = heads * length * (length + BLOCK) // 2
    return pl.pallas_call(
        functools.partial(attend_kernel, length // BLOCK),
        grid=(heads,),
        in_specs=[pl.BlockSpec((3, 64, length), lambda h: (0, h, 0))],
        out_specs=[
            pl.BlockSpec((64, length), lambda h: (h, 0)),
            pl.BlockSpec((8, length), lambda h: (h, 0)),
        ],
        out_shape=[
            jax.ShapeDtypeStruct((heads * 64, length), F32),
            jax.ShapeDtypeStruct((heads * 8, length), F32),
        ],
        compiler_params=pltpu.CompilerParams(vmem_limit_bytes=VMEM_LIMIT),
        cost_estimate=pl.CostEstimate(
            flops=pairs * 1024, bytes_accessed=heads * length * 700, transcendentals=pairs
        ),
    )(qkv)


def attend_back_kernel(block_count, qkv_ref, o_ref, lse_ref, do_ref, d_ref, dk_acc, dv_acc):
    dk_acc[...] = jnp.zeros_like(dk_acc)
    dv_acc[...] = jnp.zeros_like(dv_acc)
    for query_block in range(block_count):
        here = slice(query_block * BLOCK, (query_block + 1) * BLOCK)
        queries_t = (qkv_ref[0, :, here].astype(F32) * 0.125).astype(BF16)
        queries = queries_t.T
        do_t = do_ref[:, here]
        do_rows = do_t.T
        lse = lse_ref[0:1, here]
        delta = jnp.sum(do_t.astype(F32) * o_ref[:, here], axis=0, keepdims=True)
        dq = jnp.zeros((64, BLOCK), F32)
        for key_block in range(query_block + 1):
            there = slice(key_block * BLOCK, (key_block + 1) * BLOCK)
            keys_t = qkv_ref[1, :, there]
            probs = jnp.exp(matmul(keys_t.T, queries_t) - lse)
            if key_block == query_block:
                probs = jnp.where(causal_mask(0, BLOCK, BLOCK), probs, 0.0)
            dprobs = matmul(qkv_ref[2, :, there].T, do_t)
            dlogits = (probs * (dprobs - delta)).astype(BF16)
            dq = dq + matmul(keys_t, dlogits)
            dv_acc[there, :] += matmul(probs.astype(BF16), do_rows)
            dk_acc[there, :] += matmul(dlogits, queries)
        d_ref[0, :, here] = (dq * 0.125).astype(BF16)
    d_ref[1] = dk_acc[...].T.astype(BF16)
    d_ref[2] = dv_acc[...].T.astype(BF16)


def attend_backward(qkv, o_t, lse, do_t, heads):
    length = qkv.shape[2]
    pairs = heads * length * (length + BLOCK) // 2
    spec = lambda rows: pl.BlockSpec((rows, length), lambda h: (h, 0))
    triple = pl.BlockSpec((3, 64, length), lambda h: (0, h, 0))
    return pl.pallas_call(
        functools.partial(attend_back_kernel, length // BLOCK),
        grid=(heads,),
        in_specs=[triple, spec(64), spec(8), spec(64)],
        out_specs=triple,
        out_shape=jax.ShapeDtypeStruct((3, heads * 64, length), BF16),
        scratch_shapes=[pltpu.VMEM((length, 64), F32), pltpu.VMEM((length, 64), F32)],
        compiler_params=pltpu.CompilerParams(vmem_limit_bytes=VMEM_LIMIT),
        cost_estimate=pl.CostEstimate(
            flops=pairs * 2048, bytes_accessed=heads * length * 1300, transcendentals=pairs
        ),
    )(qkv, o_t, lse, do_t)


def widened(gain, width):
    return jnp.concatenate([gain] * (width // 128), axis=1)


def column_stats(values):
    size = values.shape[0]
    average = jnp.sum(values, axis=0, keepdims=True) * (1.0 / size)
    centred = values - average
    spread = jnp.sum(centred * centred, axis=0, keepdims=True) * (1.0 / size)
    return average, lax.rsqrt(spread + EPSILON)


def gelu_both(values):
    t = 1.0 / (1.0 + (0.3275911 * 0.7071067811865476) * jnp.abs(values))
    density = jnp.exp(-0.5 * (values * values))
    tail = 0.5 * -1.453152027 + t * (0.5 * 1.061405429)
    tail = 0.5 * 1.421413741 + t * tail
    tail = 0.5 * -0.284496736 + t * tail
    tail = 0.5 * 0.254829592 + t * tail
    tail = tail * t * density
    below = jnp.where(values >= 0, 1.0 - tail, tail)
    return values * below, below + values * (density * 0.3989422804014327)


def feed_kernel(steps, chunk, sub, has_partial, *refs):
    names = iter(refs)
    o_ref, x_ref, dy_ref, ig_ref, fg_ref, hg_ref, wo, wu_first, wd, wu_last = [
        next(names) for _ in range(10)
    ]
    if has_partial:
        part_d, part_u, part_o = [next(names) for _ in range(3)]
    out_ref, dh_ref, do_ref, gd_ref, gu_ref, go_ref = [next(names) for _ in range(6)]
    b_s, h_s, c_s, cn_s, dyt_s, n_s, slope_s, t_s, out_s, dc_s, st = [next(names) for _ in range(11)]
    width = x_ref.shape[0]
    step = pl.program_id(0)

    @pl.when(step == 0)
    def _():
        o = o_ref[...].astype(F32)
        average, inverse = column_stats(o)
        b = ((o - average) * inverse * widened(ig_ref[...], width)).astype(BF16)
        b_s[...] = b
        st[0:1] = average
        st[1:2] = inverse
        dyt_s[...] = dy_ref[...].T
        h = x_ref[...].T.astype(F32) + left_t(wo[...], b)
        h_s[...] = h
        average, inverse = column_stats(h)
        st[2:3] = average
        st[3:4] = inverse
        c = ((h - average) * inverse * widened(fg_ref[...], width)).astype(BF16)
        c_s[...] = c
        cn_s[...] = c.T

    @pl.when(step < steps)
    def _():
        base = pl.multiple_of(step * chunk, chunk)
        for k in range(chunk // sub):
            z, slope = gelu_both(left_t(wu_first[:, k * sub : (k + 1) * sub], c_s[...]))
            n_s[pl.ds(base + k * sub, sub), :] = z
            slope_s[pl.ds(base + k * sub, sub), :] = slope.astype(BF16)

    @pl.when(step == steps - 1)
    def _():
        total = jnp.zeros((1, width), F32)
        for k in range(FF // sub):
            total = total + jnp.sum(n_s[k * sub : (k + 1) * sub, :], axis=0, keepdims=True)
        average = total * (1.0 / FF)
        total = jnp.zeros((1, width), F32)
        for k in range(FF // sub):
            centred = n_s[k * sub : (k + 1) * sub, :] - average
            total = total + jnp.sum(centred * centred, axis=0, keepdims=True)
        st[4:5] = average
        st[5:6] = lax.rsqrt(total * (1.0 / FF) + EPSILON)
        st[6:8] = jnp.zeros((2, width), F32)
        out_s[...] = h_s[...]

    @pl.when((step >= steps) & (step < 2 * steps))
    def _():
        base = pl.multiple_of((step - steps) * chunk, chunk)
        average = st[4:5]
        inverse = st[5:6]
        first = jnp.zeros((1, width), F32)
        second = jnp.zeros((1, width), F32)
        pieces = []
        for k in range(chunk // sub):
            rows = slice(k * sub, (k + 1) * sub)
            n = (n_s[pl.ds(base + k * sub, sub), :] - average) * inverse
            n_s[pl.ds(base + k * sub, sub), :] = n
            gain = widened(hg_ref[rows, :], width)
            e = (n * gain).astype(BF16)
            pieces.append(e)
            t = matmul(wd[rows, :], dyt_s[...]) * gain
            t_s[pl.ds(base + k * sub, sub), :] = t
            first = first + jnp.sum(t, axis=0, keepdims=True)
            second = second + jnp.sum(t * n, axis=0, keepdims=True)
            grad = matmul(e, dy_ref[...])
            if has_partial:
                grad = grad + part_d[rows, :].astype(F32)
            gd_ref[rows, :] = grad.astype(BF16)
        out_s[...] += left_t(wd[...], jnp.concatenate(pieces, axis=0))
        st[6:7] += first
        st[7:8] += second

    @pl.when(step == 2 * steps - 1)
    def _():
        out_ref[...] = out_s[...].astype(BF16).T
        st[6:8] = st[6:8] * (1.0 / FF)
        dc_s[...] = jnp.zeros_like(dc_s)

    @pl.when(step >= 2 * steps)
    def _():
        base = pl.multiple_of((step - 2 * steps) * chunk, chunk)
        inverse = st[5:6]
        first = st[6:7]
        second = st[7:8]
        pieces = []
        for k in range(chunk // sub):
            rows = pl.ds(base + k * sub, sub)
            n = n_s[rows, :]
            du = ((t_s[rows, :] - first - n * second) * inverse * slope_s[rows, :].astype(F32)).astype(BF16)
            pieces.append(du)
            grad = matmul(du, cn_s[...])
            if has_partial:
                grad = grad + part_u[k * sub : (k + 1) * sub, :].astype(F32)
            gu_ref[k * sub : (k + 1) * sub, :] = grad.astype(BF16)
        dc_s[...] += matmul(wu_last[...], jnp.concatenate(pieces, axis=0))

    @pl.when(step == 3 * steps - 1)
    def _():
        n = (h_s[...] - st[2:3]) * st[3:4]
        t = dc_s[...] * widened(fg_ref[...], width)
        first = jnp.sum(t, axis=0, keepdims=True) * (1.0 / D)
        second = jnp.sum(t * n, axis=0, keepdims=True) * (1.0 / D)
        dh = dyt_s[...].astype(F32) + (t - first - n * second) * st[3:4]
        dh_rows = dh.T
        dh_ref[...] = dh_rows
        grad = matmul(b_s[...], dh_rows.astype(BF16))
        if has_partial:
            grad = grad + part_o[...].astype(F32)
        go_ref[...] = grad.astype(BF16)
        n = (o_ref[...].astype(F32) - st[0:1]) * st[1:2]
        t = matmul(wo[...], dh.astype(BF16)) * widened(ig_ref[...], width)
        first = jnp.sum(t, axis=0, keepdims=True) * (1.0 / D)
        second = jnp.sum(t * n, axis=0, keepdims=True) * (1.0 / D)
        do_ref[...] = ((t - first - n * second) * st[1:2]).astype(BF16)


def feed_both(o_t, x, dy, gains, weights, partial=None, chunk=768, sub=256):
    width = x.shape[0]
    steps = FF // chunk
    has_partial = partial is not None
    once = lambda *shape: pl.BlockSpec(shape, lambda i: (0, 0), pipeline_mode=pl.Buffered(1))
    first = lambda i: jnp.clip(i, 0, steps - 1)
    second = lambda i: jnp.clip(i - steps, 0, steps - 1)
    third = lambda i: jnp.clip(i - 2 * steps, 0, steps - 1)
    by_rows = lambda phase: pl.BlockSpec((chunk, D), lambda i: (phase(i), 0))
    by_columns = lambda phase: pl.BlockSpec((D, chunk), lambda i: (0, phase(i)))
    in_specs = [once(D, width), once(width, D), once(width, D), once(D, 128), once(D, 128)]
    in_specs += [pl.BlockSpec((chunk, 128), lambda i: (second(i), 0)), once(D, D)]
    in_specs += [by_columns(first), by_rows(second), by_columns(third)]
    args = [o_t, x, dy, *gains, *weights]
    if has_partial:
        in_specs += [by_rows(second), by_rows(third), once(D, D)]
        args += list(partial)
    whole = lambda *shape: pl.BlockSpec(shape, lambda i: (0, 0))
    return pl.pallas_call(
        functools.partial(feed_kernel, steps, chunk, sub, has_partial),
        grid=(3 * steps,),
        in_specs=in_specs,
        out_specs=[
            whole(width, D),
            whole(width, D),
            whole(D, width),
            by_rows(second),
            by_rows(third),
            whole(D, D),
        ],
        out_shape=[
            jax.ShapeDtypeStruct((width, D), BF16),
            jax.ShapeDtypeStruct((width, D), F32),
            jax.ShapeDtypeStruct((D, width), BF16),
            jax.ShapeDtypeStruct((FF, D), BF16),
            jax.ShapeDtypeStruct((FF, D), BF16),
            jax.ShapeDtypeStruct((D, D), BF16),
        ],
        scratch_shapes=[
            pltpu.VMEM((D, width), BF16),
            pltpu.VMEM((D, width), F32),
            pltpu.VMEM((D, width), BF16),
            pltpu.VMEM((width, D), BF16),
            pltpu.VMEM((D, width), BF16),
            pltpu.VMEM((FF, width), F32),
            pltpu.VMEM((FF, width), BF16),
            pltpu.VMEM((FF, width), F32),
            pltpu.VMEM((D, width), F32),
            pltpu.VMEM((D, width), F32),
            pltpu.VMEM((8, width), F32),
        ],
        compiler_params=pltpu.CompilerParams(vmem_limit_bytes=62 * 2**20),
        cost_estimate=pl.CostEstimate(
            flops=6 * width * D * (D + 2 * FF), bytes_accessed=80 * 2**20, transcendentals=width * FF
        ),
    )(*args)


PIECE = 768
HALF = PIECE // 2
COLS = D // 2
FEED_PIECES = (2 * FF + D) // PIECE
QKV_PIECES = 3 * D // PIECE
PIECES = FEED_PIECES + QKV_PIECES
ATTEND_TICK = 2
GAP = 0


def sum_kernel(*refs):
    gd, gu, go, gq, do_ref, qkv_ref, o_ref, lse_ref, a_ref, total_ref, back_ref = refs[:11]
    own, r0, r1, r2, r3, r4, fin, qkv, o_own, lse_own, a_all, gq_own, do_own, d_own = refs[11:25]
    dk_acc, dv_acc, own_sem, send_sem, recv_sem, fin_sem, in_sem, swap_send, swap_recv = refs[25:]
    r = lax.axis_index("rows")
    s = lax.axis_index("seq")
    core, xb, yb = r % 2, (r // 2) % 2, r // 4
    inside = (s == 1) | (s == 2)
    outside = (s == 0) | (s == 3)
    to_core = (r + 1 - 2 * core, s)
    to_x = (r + 2 - 4 * xb, s)
    to_y = (r + 4 - 8 * yb, s)
    to_pair = (r, s + 1 - 2 * (s % 2))
    to_middle = (r, 3 - s)
    shifted = [(r, (s + shift) % SEQ) for shift in range(SEQ)]
    barrier = pltpu.get_barrier_semaphore()
    for device in (to_core, to_x, to_y, *shifted[1:]):
        pl.semaphore_signal(barrier, inc=1, device_id=device, device_id_type=MESH)
    pl.semaphore_wait(barrier, 6)
    bits = [(xb, yb), (yb, xb)]
    partners = [(to_x, to_y), (to_y, to_x)]

    def rows_at(start, count):
        return pl.ds(pl.multiple_of(start, 16), count)

    def remote(source, target, send, recv, device):
        return pltpu.make_async_remote_copy(
            src_ref=source,
            dst_ref=target,
            send_sem=send,
            recv_sem=recv,
            device_id=device,
            device_id_type=MESH,
        )

    def numbered(source, target, kind, p, device):
        return remote(source, target, send_sem.at[kind, p], recv_sem.at[kind, p], device)

    def columns(o):
        return slice(o * COLS, (o + 1) * COLS)

    def base(o):
        return bits[o][0] * 192 + bits[o][1] * 96

    def core_copy(ref, q, p):
        part = ref.at[rows_at(q * PIECE + (1 - core) * HALF, HALF), :]
        return numbered(part, r0.at[p], 0, p, to_core)

    def own_copy(ref, q, p):
        part = ref.at[rows_at(q * PIECE + core * HALF, HALF), :]
        return pltpu.make_async_copy(part, own.at[p], own_sem.at[p])

    def first_copy(p, o):
        part = own.at[p, rows_at((1 - bits[o][0]) * 192, 192), columns(o)]
        return numbered(part, r1.at[p, o], 1 + o, p, partners[o][0])

    def second_copy(p, o):
        part = own.at[p, rows_at(bits[o][0] * 192 + (1 - bits[o][1]) * 96, 96), columns(o)]
        return numbered(part, r2.at[p, o], 3 + o, p, partners[o][1])

    def pair_copy(p, o):
        part = own.at[p, rows_at(base(o), 96), columns(o)]
        return numbered(part, r3.at[p, o], 5 + o, p, to_pair)

    def middle_copy(p, o):
        part = own.at[p, rows_at(base(o), 96), columns(o)]
        return numbered(part, r4.at[p, o], 7 + o, p, to_middle)

    def region(p, start, count, o):
        return total_ref.at[rows_at(p * PIECE + core * HALF + start, count), columns(o)]

    def fin_copy(p, o):
        return pltpu.make_async_copy(fin.at[p, o], region(p, base(o), 96, o), fin_sem.at[o, p])

    def pair_back(p, o):
        return numbered(fin.at[p, o], region(p, base(o), 96, o), 9 + o, p, to_pair)

    def second_back(p, o):
        part = region(p, base(o), 96, o)
        return numbered(part, part, 11 + o, p, partners[o][1])

    def first_back(p, o):
        part = region(p, bits[o][0] * 192, 192, o)
        return numbered(part, part, 13 + o, p, partners[o][0])

    def core_back(p):
        part = total_ref.at[rows_at(p * PIECE + core * HALF, HALF), :]
        return numbered(part, part, 15, p, to_core)

    def do_copy(shift):
        part = do_ref.at[(s + shift) % SEQ]
        if shift == 0:
            return pltpu.make_async_copy(part, do_own.at[s], in_sem.at[5])
        return remote(
            part, do_own.at[s], swap_send.at[0, shift], swap_recv.at[0, shift], shifted[shift]
        )

    def back_copy(h, shift):
        part = d_own.at[(s + shift) % SEQ, :, rows_at(h * HEAD_DIM, HEAD_DIM), :]
        target = back_ref.at[
            :, rows_at(s * (HEADS_OWN * HEAD_DIM) + h * HEAD_DIM, HEAD_DIM), :
        ]
        if shift == 0:
            return pltpu.make_async_copy(part, target, in_sem.at[6 + h])
        return remote(
            part, target, swap_send.at[1 + h, shift], swap_recv.at[1 + h, shift], shifted[shift]
        )

    loads = [
        pltpu.make_async_copy(qkv_ref, qkv, in_sem.at[0]),
        pltpu.make_async_copy(o_ref, o_own, in_sem.at[1]),
        pltpu.make_async_copy(lse_ref, lse_own, in_sem.at[2]),
        pltpu.make_async_copy(a_ref, a_all, in_sem.at[3]),
        pltpu.make_async_copy(gq, gq_own, in_sem.at[4]),
    ]
    for shift in range(1, SEQ):
        do_copy(shift).start()
    offset = 0
    for ref in (gd, gu, go):

        def begin(q, carry, ref=ref, offset=offset):
            core_copy(ref, q, q + offset).start()
            own_copy(ref, q, q + offset).start()
            return carry

        lax.fori_loop(0, ref.shape[0] // PIECE, begin, 0)
        offset += ref.shape[0] // PIECE
    do_copy(0).start()
    for load in loads:
        load.start()

    def added(index, other):
        own[index] = (own[index].astype(F32) + other.astype(F32)).astype(BF16)

    def after_core(p):
        own_copy(gd, 0, p).wait()
        core_copy(gd, 0, p).wait()
        own[p] = (own[p].astype(F32) + r0[p].astype(F32)).astype(BF16)
        for o in range(2):
            first_copy(p, o).start()

    def after_first(p):
        for o in range(2):
            first_copy(p, o).wait()
            added((p, rows_at(bits[o][0] * 192, 192), columns(o)), r1[p, o])
            second_copy(p, o).start()

    def after_second(p):
        for o in range(2):
            second_copy(p, o).wait()
            added((p, rows_at(base(o), 96), columns(o)), r2[p, o])

            @pl.when(outside)
            def _():
                pair_copy(p, o).start()

    def after_pair(p):
        for o in range(2):

            @pl.when(outside)
            def _():
                pair_copy(p, o).wait_send()

            @pl.when(inside)
            def _():
                pair_copy(p, o).wait_recv()
                added((p, rows_at(base(o), 96), columns(o)), r3[p, o])
                middle_copy(p, o).start()

    def after_middle(p):
        for o in range(2):

            @pl.when(inside)
            def _():
                middle_copy(p, o).wait()
                mine = own[p, rows_at(base(o), 96), columns(o)].astype(F32)
                fin[p, o] = (mine + r4[p, o].astype(F32)).astype(BF16)
                pair_back(p, o).start()
                fin_copy(p, o).start()

    def after_pair_back(p):
        for o in range(2):

            @pl.when(inside)
            def _():
                fin_copy(p, o).wait()
                pair_back(p, o).wait_send()

            @pl.when(outside)
            def _():
                pair_back(p, o).wait_recv()

            second_back(p, o).start()

    def after_second_back(p):
        for o in range(2):
            second_back(p, o).wait()
            first_back(p, o).start()

    def after_first_back(p):
        for o in range(2):
            first_back(p, o).wait()
        core_back(p).start()

    def after_core_back(p):
        core_back(p).wait()

    stages = [
        after_core,
        after_first,
        after_second,
        after_pair,
        after_middle,
        after_pair_back,
        after_second_back,
        after_first_back,
        after_core_back,
    ]

    def head_rows(h):
        return rows_at(h * HEAD_DIM, HEAD_DIM)

    def attend(h, query_block):
        rows = head_rows(h)
        here = slice(query_block * BLOCK, (query_block + 1) * BLOCK)
        queries_t = (qkv[0, rows, here].astype(F32) * 0.125).astype(BF16)
        queries = queries_t.T
        do_t = do_own[query_block, rows, :]
        do_rows = do_t.T
        lse = lse_own[h, 0:1, here]
        delta = jnp.sum(do_t.astype(F32) * o_own[rows, here], axis=0, keepdims=True)
        dq = jnp.zeros((HEAD_DIM, BLOCK), F32)
        for key_block in range(query_block + 1):
            there = slice(key_block * BLOCK, (key_block + 1) * BLOCK)
            keys_t = qkv[1, rows, there]
            probs = jnp.exp(matmul(keys_t.T, queries_t) - lse)
            if key_block == query_block:
                probs = jnp.where(causal_mask(0, BLOCK, BLOCK), probs, 0.0)
            dprobs = matmul(qkv[2, rows, there].T, do_t)
            dlogits = (probs * (dprobs - delta)).astype(BF16)
            dq = dq + matmul(keys_t, dlogits)
            dv_acc[there, :] += matmul(probs.astype(BF16), do_rows)
            dk_acc[there, :] += matmul(dlogits, queries)
        d_own[query_block, 0, rows, :] = (dq * 0.125).astype(BF16)

    def finish_head(h):
        rows = head_rows(h)
        total = jnp.zeros((3 * HEAD_DIM, D), F32)
        for block in range(SEQ):
            here = slice(block * BLOCK, (block + 1) * BLOCK)
            d_own[block, 1, rows, :] = dk_acc[here, :].T.astype(BF16)
            d_own[block, 2, rows, :] = dv_acc[here, :].T.astype(BF16)
            joined = d_own[block, :, rows, :].reshape(3 * HEAD_DIM, BLOCK)
            total = total + matmul(joined, a_all[here, :])
        for part in range(3):
            place = rows_at(part * D + s * (HEADS_OWN * HEAD_DIM) + h * HEAD_DIM, HEAD_DIM)
            term = total[part * HEAD_DIM : (part + 1) * HEAD_DIM, :]
            gq_own[place, :] = (gq_own[place, :].astype(F32) + term).astype(BF16)
        for shift in range(SEQ):
            back_copy(h, shift).start()

    def tick(t, carry):
        for lag, stage in enumerate(stages):
            v = t - lag

            @pl.when((v >= 0) & ((v < FEED_PIECES) | (v >= FEED_PIECES + GAP)) & (v < PIECES + GAP))
            def _():
                stage(jnp.where(v < FEED_PIECES, v, v - GAP))

        @pl.when(t == ATTEND_TICK)
        def _():
            for load in loads:
                load.wait()
            for shift in range(SEQ):
                do_copy(shift).wait()

        turn = t - ATTEND_TICK
        h = turn // 2

        @pl.when((turn >= 0) & (turn < 2 * HEADS_OWN) & (turn % 2 == 0))
        def _():
            dk_acc[...] = jnp.zeros_like(dk_acc)
            dv_acc[...] = jnp.zeros_like(dv_acc)
            attend(h, 0)
            attend(h, 3)

        @pl.when((turn >= 0) & (turn < 2 * HEADS_OWN) & (turn % 2 == 1))
        def _():
            attend(h, 1)
            attend(h, 2)
            finish_head(h)

        @pl.when(turn == 2 * HEADS_OWN - 1)
        def _():
            for q in range(QKV_PIECES):
                core_copy(gq_own, q, FEED_PIECES + q).start()
                own_copy(gq_own, q, FEED_PIECES + q).start()

        return carry

    lax.fori_loop(0, PIECES + GAP + len(stages) - 1, tick, 0)
    for h in range(HEADS_OWN):
        for shift in range(SEQ):
            back_copy(h, shift).wait()


def summed_everywhere(gd, gu, go, gq, do_pieces, qkv_own, o_own, lse, a_all, collective_id):
    n = PIECES
    length = SEQ * BLOCK
    own_rows = HEADS_OWN * HEAD_DIM
    dma = pltpu.SemaphoreType.DMA
    anywhere = pl.BlockSpec(memory_space=pl.ANY)
    return pl.pallas_call(
        sum_kernel,
        out_shape=[
            jax.ShapeDtypeStruct((n * PIECE, D), BF16),
            jax.ShapeDtypeStruct((3, D, BLOCK), BF16),
        ],
        in_specs=[anywhere] * 9,
        out_specs=[anywhere] * 2,
        scratch_shapes=[
            pltpu.VMEM((n, HALF, D), BF16),
            pltpu.VMEM((n, HALF, D), BF16),
            pltpu.VMEM((n, 2, 192, COLS), BF16),
            pltpu.VMEM((n, 2, 96, COLS), BF16),
            pltpu.VMEM((n, 2, 96, COLS), BF16),
            pltpu.VMEM((n, 2, 96, COLS), BF16),
            pltpu.VMEM((n, 2, 96, COLS), BF16),
            pltpu.VMEM((3, own_rows, length), BF16),
            pltpu.VMEM((own_rows, length), F32),
            pltpu.VMEM((HEADS_OWN, 8, length), F32),
            pltpu.VMEM((length, D), BF16),
            pltpu.VMEM((3 * D, D), BF16),
            pltpu.VMEM((SEQ, own_rows, BLOCK), BF16),
            pltpu.VMEM((SEQ, 3, own_rows, BLOCK), BF16),
            pltpu.VMEM((length, HEAD_DIM), F32),
            pltpu.VMEM((length, HEAD_DIM), F32),
            dma((n,)),
            dma((16, n)),
            dma((16, n)),
            dma((2, n)),
            dma((6 + HEADS_OWN,)),
            dma((1 + HEADS_OWN, SEQ)),
            dma((1 + HEADS_OWN, SEQ)),
        ],
        compiler_params=pltpu.CompilerParams(
            collective_id=collective_id, has_side_effects=True, vmem_limit_bytes=VMEM_LIMIT
        ),
        cost_estimate=pl.CostEstimate(flops=0, bytes_accessed=n * PIECE * D * 64, transcendentals=0),
    )(gd, gu, go, gq, do_pieces, qkv_own, o_own, lse, a_all)


def by_block(relative, place):
    blocks = [lax.dynamic_index_in_dim(relative, (place - j) % SEQ, 0) for j in range(SEQ)]
    return jnp.concatenate(blocks, axis=0)


def shifted_by(value, shift):
    return lax.ppermute(value, "seq", [(i, (i + shift) % SEQ) for i in range(SEQ)])


FINISH = PIECES


def finish_kernel(total, wd, wu, wo, wq, ig, fg, hg, ag, gd, gu, go, gq, si, sf, sh, sa, acc):
    step = pl.program_id(0)

    def lanes(values):
        folded = values[:, 0:128]
        for k in range(1, D // 128):
            folded = folded + values[:, k * 128 : (k + 1) * 128]
        return folded

    def as_row(folded):
        return jnp.sum(folded.T, axis=0, keepdims=True)

    @pl.when(step < 4)
    def _():
        grad = total[...].astype(F32)
        gd[...] = grad
        sh[...] = as_row(lanes(grad * wd[...].astype(F32))) / hg[...]

    @pl.when((step >= 4) & (step < 8))
    def _():
        grad = total[...].T.astype(F32)
        gu[...] = grad
        acc[0] = lanes(grad * wu[...].astype(F32)) + jnp.where(step == 4, 0.0, acc[0])

    @pl.when(step == 8)
    def _():
        sf[...] = as_row(acc[0]) / fg[...]
        grad = total[...].astype(F32)
        go[...] = grad
        si[...] = as_row(lanes(grad * wo[...].astype(F32))) / ig[...]

    @pl.when(step >= 9)
    def _():
        grad = total[...].T.astype(F32)
        gq[...] = grad
        acc[1] = lanes(grad * wq[...].astype(F32)) + jnp.where(step == 9, 0.0, acc[1])

    @pl.when(step == 11)
    def _():
        sa[...] = as_row(acc[1]) / ag[...]


def finished(total, down_weight, up_weight, out_weight, query_key_value, gains):
    square = lambda index: pl.BlockSpec((D, D), index)
    row = lambda index: pl.BlockSpec((1, D), index)
    at_down = lambda i: (jnp.clip(i, 0, 3), 0)
    at_up = lambda i: (0, jnp.clip(i - 4, 0, 3))
    at_qkv = lambda i: (0, jnp.clip(i - 9, 0, 2))
    still = lambda i: (0, 0)
    hidden = lambda i: (0, jnp.clip(i, 0, 3))
    shapes = [(FF, D), (D, FF), (D, D), (D, 3 * D), (1, D), (1, D), (1, FF), (1, D)]
    return pl.pallas_call(
        finish_kernel,
        grid=(FINISH,),
        in_specs=[
            square(lambda i: (i, 0)),
            square(at_down),
            square(at_up),
            square(still),
            square(at_qkv),
            row(still),
            row(still),
            row(hidden),
            row(still),
        ],
        out_specs=[
            square(at_down),
            square(at_up),
            square(still),
            square(at_qkv),
            row(still),
            row(still),
            row(hidden),
            row(still),
        ],
        out_shape=[jax.ShapeDtypeStruct(shape, F32) for shape in shapes],
        scratch_shapes=[pltpu.VMEM((2, D, 128), F32)],
        compiler_params=pltpu.CompilerParams(vmem_limit_bytes=VMEM_LIMIT),
        cost_estimate=pl.CostEstimate(flops=10**8, bytes_accessed=56 * 2**20, transcendentals=0),
    )(total, down_weight, up_weight, out_weight, query_key_value, *[g[None] for g in gains])


def normed_rows(x, gain):
    out, normed, inverse = layer_norm(x.astype(F32), gain)
    return out.astype(BF16), normed, inverse


def layer_back(upstream, normed, inverse, gain):
    scaled = upstream * gain
    return inverse * (
        scaled
        - jnp.mean(scaled, axis=-1, keepdims=True)
        - normed * jnp.mean(scaled * normed, axis=-1, keepdims=True)
    )


def split_layer(
    tokens,
    segment_ids,
    cotangent,
    query_key_value,
    out_weight,
    up_weight,
    down_weight,
    attend_gain,
    inner_gain,
    feed_gain,
    hidden_gain,
):
    place = lax.axis_index("seq")
    long_first = segment_ids[0, -1] == 0
    x_long = jnp.where(long_first, tokens[0], tokens[1])
    x_pack = jnp.where(long_first, tokens[1], tokens[0])
    dy_long = jnp.where(long_first, cotangent[0], cotangent[1])
    dy_pack = jnp.where(long_first, cotangent[1], cotangent[0])
    x_blocks = [x_long] + [shifted_by(x_long, shift) for shift in range(1, SEQ)]
    wide = lambda gain: jnp.broadcast_to(gain[:, None], (gain.shape[0], 128))
    gains = (wide(inner_gain), wide(feed_gain), wide(hidden_gain))
    weights = (out_weight, up_weight, down_weight, up_weight)
    a_pack, pack_normed, pack_inverse = normed_rows(x_pack, attend_gain)
    qkv_pack = lax.dot_general(
        query_key_value, a_pack, (((0,), (1,)), ((), ())), preferred_element_type=F32
    )
    qkv_pack = qkv_pack.astype(BF16).reshape(3, D, BLOCK)
    o_pack, lse_pack = attend_forward(qkv_pack, HEADS)
    out_pack, dh_pack, do_pack, gd_pack, gu_pack, go_pack = feed_both(
        o_pack, x_pack, dy_pack, gains, weights
    )
    *x_blocks, do_pack = lax.optimization_barrier((*x_blocks, do_pack))
    own_rows = HEADS_OWN * HEAD_DIM
    w_own = lax.dynamic_slice_in_dim(
        query_key_value.reshape(D, 3, D), place * own_rows, own_rows, 2
    ).reshape(D, 3 * own_rows)
    x_all = by_block(jnp.stack(x_blocks), place).reshape(SEQ * BLOCK, D)
    a_all, _, _ = normed_rows(x_all, attend_gain)
    qkv_long = lax.dot_general(w_own, a_all, (((0,), (1,)), ((), ())), preferred_element_type=F32)
    qkv_long = qkv_long.astype(BF16).reshape(3, own_rows, SEQ * BLOCK)
    o_long, lse_long = attend_forward(qkv_long, HEADS_OWN)
    o_low = o_long.astype(BF16)
    o_parts = []
    for shift in range(SEQ):
        leaving = lax.dynamic_slice_in_dim(o_low, ((place + shift) % SEQ) * BLOCK, BLOCK, 1)
        o_parts.append(shifted_by(leaving, shift) if shift else leaving)
    do_pack, _ = lax.optimization_barrier((do_pack, o_low))
    dqkv_pack = attend_backward(qkv_pack, o_pack, lse_pack, do_pack, HEADS).reshape(3 * D, BLOCK)
    gq_pack = matmul(dqkv_pack, a_pack).astype(BF16)
    dxa_pack = layer_back(
        left_t(dqkv_pack, query_key_value.T), pack_normed, pack_inverse, attend_gain
    )
    dx_pack = (dh_pack + dxa_pack).astype(BF16)
    *o_parts, gq_pack, dx_pack = lax.optimization_barrier((*o_parts, gq_pack, dx_pack))
    o_mine = by_block(jnp.stack(o_parts), place).reshape(D, BLOCK)
    out_long, dh_long, do_long, gd, gu, go = feed_both(
        o_mine, x_long, dy_long, gains, weights, (gd_pack, gu_pack, go_pack)
    )
    total, dqkv_long = summed_everywhere(
        gd,
        gu,
        go,
        gq_pack,
        do_long.reshape(SEQ, own_rows, BLOCK),
        qkv_long,
        o_long,
        lse_long.reshape(HEADS_OWN, 8, SEQ * BLOCK),
        a_all,
        0,
    )
    _, long_normed, long_inverse = normed_rows(x_long, attend_gain)
    dxa_long = layer_back(
        left_t(dqkv_long.reshape(3 * D, BLOCK), query_key_value.T),
        long_normed,
        long_inverse,
        attend_gain,
    )
    dx_long = (dh_long + dxa_long).astype(BF16)
    down_grad, up_grad, out_grad, qkv_grad, inner_total, feed_total, hidden_total, attend_total = (
        finished(
            total,
            down_weight,
            up_weight,
            out_weight,
            query_key_value,
            (inner_gain, feed_gain, hidden_gain, attend_gain),
        )
    )
    output = jnp.where(long_first, jnp.stack([out_long, out_pack]), jnp.stack([out_pack, out_long]))
    tokens_grad = jnp.where(long_first, jnp.stack([dx_long, dx_pack]), jnp.stack([dx_pack, dx_long]))
    return (
        output,
        tokens_grad,
        qkv_grad,
        out_grad,
        up_grad,
        down_grad,
        attend_total[0],
        inner_total[0],
        feed_total[0],
        hidden_total[0],
    )


def per_device(tokens, *others):
    split = lax.axis_size("seq") == SEQ and lax.axis_size("rows") == 8
    if split and tokens.shape == (2, BLOCK, D):
        return split_layer(tokens, *others)
    return ring_layer(tokens, *others)


def solution(mesh):
    return jax.shard_map(
        per_device,
        mesh=mesh,
        in_specs=(
            P("rows", "seq", None),
            P("rows", None),
            P("rows", "seq", None),
            P(),
            P(),
            P(),
            P(),
            P(),
            P(),
            P(),
            P(),
        ),
        out_specs=(
            P("rows", "seq", None),
            P("rows", "seq", None),
            P(),
            P(),
            P(),
            P(),
            P(),
            P(),
            P(),
            P(),
        ),
        check_vma=False,
    )
```

```python
import functools
import math

import jax
import jax.numpy as jnp
from jax import lax
from jax.experimental import pallas as pl
from jax.experimental.pallas import tpu as pltpu
from jax.sharding import PartitionSpec as P

D = 768
HEADS = 12
HEAD_DIM = 64


EPSILON = 1e-05
MASKED = -1e30


def passed_along(value, axis, steps):
    count = lax.axis_size(axis)
    initial, last = (max(0, -steps), min(count, count - steps))
    return lax.ppermute(value, axis, [(source, source + steps) for source in range(initial, last)])


def from_behind(value, axis, steps):
    count = lax.axis_size(axis)
    pairs = [(source, (source + steps) % count) for source in range(count)]
    return lax.ppermute(value, axis, pairs)


def layer_norm(values, gain):
    average = jnp.mean(values, axis=-1, keepdims=True)
    centred = values - average
    inverse = lax.rsqrt(jnp.mean(centred * centred, axis=-1, keepdims=True) + EPSILON)
    normed = centred * inverse
    return (normed * gain, normed, inverse)


def norm_back(upstream, normed, inverse, gain):
    scaled = upstream * gain
    spread = (
        scaled
        - jnp.mean(scaled, axis=-1, keepdims=True)
        - normed * jnp.mean(scaled * normed, axis=-1, keepdims=True)
    )
    return (spread * inverse, jnp.sum(upstream * normed, axis=0))


def gelu_exact(values):
    return jax.nn.gelu(values, approximate=False)


def matmul(left, right):
    return jnp.dot(left, right, preferred_element_type=jnp.float32)


def left_t(left, right):
    return lax.dot_general(
        left, right, (((0,), (0,)), ((), ())), preferred_element_type=jnp.float32
    )


def right_t(left, right):
    return lax.dot_general(
        left, right, (((1,), (1,)), ((), ())), preferred_element_type=jnp.float32
    )


def split_heads(values):
    return values.reshape(values.shape[0], values.shape[1], HEADS, HEAD_DIM)


def allowed_pairs(query_pos, query_seg, key_pos, key_seg):
    causal = key_pos[None, None, None, :] <= query_pos[None, None, :, None]
    same_doc = key_seg[:, None, None, :] == query_seg[:, None, :, None]
    return causal & same_doc


def scores(queries, key_rows):
    return jnp.einsum(
        "rqhd,rkhd->rhqk",
        split_heads(queries),
        split_heads(key_rows),
        preferred_element_type=jnp.float32,
    ) * HEAD_DIM ** (-0.5)


def fold_keys(carry, piece, queries, query_pos, query_seg, segment_ids):
    key_rows, value_rows = piece
    row_count = key_rows.shape[0]
    key_count = key_rows.shape[1]
    block_width = math.gcd(key_count, queries.shape[1])
    block_count = key_count // block_width
    key_blocks = key_rows.reshape(row_count, block_count, block_width, D).transpose(1, 0, 2, 3)
    value_blocks = value_rows.reshape(row_count, block_count, block_width, D).transpose(1, 0, 2, 3)

    def one_block(state, block_item):
        accum, running, softmax_total = state
        key_block, value_block, offset = block_item
        key_start = offset * block_width
        key_pos = key_start + jnp.arange(block_width, dtype=jnp.int32)
        key_seg = lax.dynamic_slice_in_dim(segment_ids, key_start, block_width, 1)
        allowed = allowed_pairs(query_pos, query_seg, key_pos, key_seg)
        logits = jnp.where(allowed, scores(queries, key_block), MASKED)
        new_peak = jnp.maximum(running, jnp.max(logits, axis=-1))
        weights = jnp.where(allowed, jnp.exp(logits - new_peak[..., None]), 0.0)
        factor = jnp.exp(running - new_peak)
        softmax_total = softmax_total * factor + jnp.sum(weights, axis=-1)
        accum = accum * factor[..., None] + jnp.einsum(
            "rhqk,rkhd->rhqd",
            weights.astype(jnp.bfloat16),
            split_heads(value_block),
            preferred_element_type=jnp.float32,
        )
        return ((accum, new_peak, softmax_total), None)

    carry, unused = lax.scan(
        one_block, carry, (key_blocks, value_blocks, jnp.arange(block_count, dtype=jnp.int32))
    )
    return carry


def back_block(queries, grad_rows, log_total, delta, key_rows, value_rows, allowed):
    logits = jnp.where(allowed, scores(queries, key_rows), MASKED)
    probs = jnp.where(allowed, jnp.exp(logits - log_total[..., None]), 0.0)
    dprobs = jnp.einsum(
        "rqhd,rkhd->rhqk",
        split_heads(grad_rows),
        split_heads(value_rows),
        preferred_element_type=jnp.float32,
    )
    dlogits = (probs * (dprobs - delta[..., None])).astype(jnp.bfloat16)
    factor = HEAD_DIM ** (-0.5)
    query_part = (
        jnp.einsum(
            "rhqk,rkhd->rqhd", dlogits, split_heads(key_rows), preferred_element_type=jnp.float32
        )
        * factor
    )
    key_part = (
        jnp.einsum(
            "rhqk,rqhd->rkhd", dlogits, split_heads(queries), preferred_element_type=jnp.float32
        )
        * factor
    )
    value_part = jnp.einsum(
        "rhqk,rqhd->rkhd",
        probs.astype(jnp.bfloat16),
        split_heads(grad_rows),
        preferred_element_type=jnp.float32,
    )
    return (
        query_part.reshape(queries.shape),
        key_part.reshape(key_rows.shape),
        value_part.reshape(value_rows.shape),
    )


def ring_layer(
    tokens,
    segment_ids,
    cotangent,
    query_key_value,
    out_weight,
    up_weight,
    down_weight,
    attend_gain,
    inner_gain,
    feed_gain,
    hidden_gain,
):
    row_count = tokens.shape[0]
    width_q = tokens.shape[1]
    model_width = tokens.shape[2]
    token_count = row_count * width_q
    seq_index = lax.axis_index("seq")
    seq_size = lax.axis_size("seq")
    local_pos = seq_index * width_q + jnp.arange(width_q, dtype=jnp.int32)
    local_seg = lax.dynamic_slice_in_dim(segment_ids, seq_index * width_q, width_q, 1)
    residual = tokens.reshape(token_count, model_width).astype(jnp.float32)
    attend_out, attend_normed, attend_inverse = layer_norm(residual, attend_gain)
    attend_low = attend_out.astype(jnp.bfloat16)
    projected = matmul(attend_low, query_key_value).astype(jnp.bfloat16)
    queries = projected[:, :model_width].reshape(row_count, width_q, model_width)
    key_rows = projected[:, model_width : 2 * model_width].reshape(row_count, width_q, model_width)
    value_rows = projected[:, 2 * model_width :].reshape(row_count, width_q, model_width)
    start_state = (
        jnp.zeros((row_count, HEADS, width_q, HEAD_DIM), jnp.float32),
        jnp.full((row_count, HEADS, width_q), MASKED, jnp.float32),
        jnp.zeros((row_count, HEADS, width_q), jnp.float32),
    )
    accum, running, softmax_total = fold_keys(
        start_state,
        (
            lax.all_gather(key_rows, "seq", axis=1, tiled=True),
            lax.all_gather(value_rows, "seq", axis=1, tiled=True),
        ),
        queries,
        local_pos,
        local_seg,
        segment_ids,
    )
    log_total = running + jnp.log(softmax_total)
    attended = (accum / softmax_total[..., None]).transpose(0, 2, 1, 3)
    attended_flat = attended.reshape(token_count, model_width)
    inner_out, inner_normed, inner_inverse = layer_norm(attended_flat, inner_gain)
    inner_low = inner_out.astype(jnp.bfloat16)
    state = residual + matmul(inner_low, out_weight)
    feed_out, feed_normed, feed_inverse = layer_norm(state, feed_gain)
    feed_low = feed_out.astype(jnp.bfloat16)
    pre_act = matmul(feed_low, up_weight)
    hidden, gelu_back = jax.vjp(gelu_exact, pre_act)
    hidden_out, hidden_normed, hidden_inverse = layer_norm(hidden, hidden_gain)
    hidden_low = hidden_out.astype(jnp.bfloat16)
    result = state + matmul(hidden_low, down_weight)
    output = result.astype(jnp.bfloat16).reshape(tokens.shape)
    upstream_low = cotangent.reshape(token_count, model_width)
    upstream = upstream_low.astype(jnp.float32)
    down_term = left_t(hidden_low, upstream_low)
    hidden_grad, hidden_gain_term = norm_back(
        right_t(upstream_low, down_weight), hidden_normed, hidden_inverse, hidden_gain
    )
    pre_grad = gelu_back(hidden_grad)[0]
    pre_low = pre_grad.astype(jnp.bfloat16)
    up_term = left_t(feed_low, pre_low)
    feed_grad, feed_gain_term = norm_back(
        right_t(pre_low, up_weight), feed_normed, feed_inverse, feed_gain
    )
    state_grad = upstream + feed_grad
    state_low = state_grad.astype(jnp.bfloat16)
    out_term = left_t(inner_low, state_low)
    inner_grad, inner_gain_term = norm_back(
        right_t(state_low, out_weight), inner_normed, inner_inverse, inner_gain
    )
    attend_grad_low = inner_grad.astype(jnp.bfloat16).reshape(row_count, width_q, model_width)
    delta = jnp.sum(split_heads(attend_grad_low).astype(jnp.float32) * attended, axis=-1).transpose(
        0, 2, 1
    )
    zero_rows = jnp.zeros((row_count, width_q, model_width), jnp.float32)

    def key_step(step_count, cycle_state):
        moving_keys, moving_values, moving_dkeys, moving_dvalues, query_acc = cycle_state
        source = jnp.remainder(seq_index - step_count, seq_size)
        key_start = source * width_q
        key_pos = key_start + jnp.arange(width_q, dtype=jnp.int32)
        key_seg = lax.dynamic_slice_in_dim(segment_ids, key_start, width_q, 1)
        allowed = allowed_pairs(local_pos, local_seg, key_pos, key_seg)
        query_part, key_part, value_part = back_block(
            queries, attend_grad_low, log_total, delta, moving_keys, moving_values, allowed
        )
        moving_keys, moving_values = passed_along((moving_keys, moving_values), "seq", 1)
        moving_dkeys, moving_dvalues = (
            from_behind((moving_dkeys + key_part).astype(jnp.bfloat16), "seq", 1).astype(
                jnp.float32
            ),
            from_behind((moving_dvalues + value_part).astype(jnp.bfloat16), "seq", 1).astype(
                jnp.float32
            ),
        )
        return (moving_keys, moving_values, moving_dkeys, moving_dvalues, query_acc + query_part)

    cycle_out = lax.fori_loop(
        0, seq_size, key_step, (key_rows, value_rows, zero_rows, zero_rows, zero_rows)
    )
    key_grad, value_grad, query_grad = (cycle_out[2], cycle_out[3], cycle_out[4])
    joined_grad = jnp.concatenate(
        [
            query_grad.astype(jnp.bfloat16),
            key_grad.astype(jnp.bfloat16),
            value_grad.astype(jnp.bfloat16),
        ],
        axis=-1,
    ).reshape(token_count, 3 * model_width)
    qkv_term = left_t(attend_low, joined_grad)
    attend_back, attend_gain_term = norm_back(
        right_t(joined_grad, query_key_value), attend_normed, attend_inverse, attend_gain
    )
    tokens_grad = (state_grad + attend_back).astype(jnp.bfloat16).reshape(tokens.shape)
    all_sectioned = (
        lax.psum_scatter(
            qkv_term.astype(jnp.bfloat16), "rows", scatter_dimension=0, tiled=True
        ).astype(jnp.float32),
        lax.psum_scatter(
            out_term.astype(jnp.bfloat16), "rows", scatter_dimension=0, tiled=True
        ).astype(jnp.float32),
        lax.psum_scatter(
            up_term.astype(jnp.bfloat16), "rows", scatter_dimension=0, tiled=True
        ).astype(jnp.float32),
        lax.psum_scatter(
            down_term.astype(jnp.bfloat16), "rows", scatter_dimension=0, tiled=True
        ).astype(jnp.float32),
    )
    seq_sectioned = (
        lax.psum_scatter(
            all_sectioned[0].astype(jnp.bfloat16), "seq", scatter_dimension=1, tiled=True
        ).astype(jnp.float32),
        lax.psum_scatter(
            all_sectioned[1].astype(jnp.bfloat16), "seq", scatter_dimension=1, tiled=True
        ).astype(jnp.float32),
        lax.psum_scatter(
            all_sectioned[2].astype(jnp.bfloat16), "seq", scatter_dimension=1, tiled=True
        ).astype(jnp.float32),
        lax.psum_scatter(
            all_sectioned[3].astype(jnp.bfloat16), "seq", scatter_dimension=1, tiled=True
        ).astype(jnp.float32),
    )
    seq_whole = (
        lax.all_gather(seq_sectioned[0].astype(jnp.bfloat16), "seq", axis=1, tiled=True).astype(
            jnp.float32
        ),
        lax.all_gather(seq_sectioned[1].astype(jnp.bfloat16), "seq", axis=1, tiled=True).astype(
            jnp.float32
        ),
        lax.all_gather(seq_sectioned[2].astype(jnp.bfloat16), "seq", axis=1, tiled=True).astype(
            jnp.float32
        ),
        lax.all_gather(seq_sectioned[3].astype(jnp.bfloat16), "seq", axis=1, tiled=True).astype(
            jnp.float32
        ),
    )
    qkv_grad, out_grad, up_grad, down_grad = (
        lax.all_gather(seq_whole[0].astype(jnp.bfloat16), "rows", axis=0, tiled=True).astype(
            jnp.float32
        ),
        lax.all_gather(seq_whole[1].astype(jnp.bfloat16), "rows", axis=0, tiled=True).astype(
            jnp.float32
        ),
        lax.all_gather(seq_whole[2].astype(jnp.bfloat16), "rows", axis=0, tiled=True).astype(
            jnp.float32
        ),
        lax.all_gather(seq_whole[3].astype(jnp.bfloat16), "rows", axis=0, tiled=True).astype(
            jnp.float32
        ),
    )
    attend_total, inner_total, feed_total, hidden_total = lax.psum(
        (attend_gain_term, inner_gain_term, feed_gain_term, hidden_gain_term), ("rows", "seq")
    )
    return (
        output,
        tokens_grad,
        qkv_grad,
        out_grad,
        up_grad,
        down_grad,
        attend_total,
        inner_total,
        feed_total,
        hidden_total,
    )


FF = 3072
SEQ = 4
BLOCK = 512
HEADS_OWN = HEADS // SEQ
GROUP = HEADS_OWN * 3 * HEAD_DIM
MESH = pl.DeviceIdType.MESH
F32 = jnp.float32
BF16 = jnp.bfloat16
VMEM_LIMIT = 56 * 2**20


def causal_mask(key_start, key_count, query_count):
    key_pos = lax.broadcasted_iota(jnp.int32, (key_count, query_count), 0) + key_start
    query_pos = lax.broadcasted_iota(jnp.int32, (key_count, query_count), 1)
    return key_pos <= query_pos


def attend_head(read, write, block_count):
    for query_block in range(block_count):
        here = slice(query_block * BLOCK, (query_block + 1) * BLOCK)
        queries = (read(0, here).astype(F32) * 0.125).astype(BF16)
        peak = jnp.full((1, BLOCK), MASKED, F32)
        total = jnp.zeros((1, BLOCK), F32)
        accum = jnp.zeros((HEAD_DIM, BLOCK), F32)
        for key_block in range(query_block + 1):
            there = slice(key_block * BLOCK, (key_block + 1) * BLOCK)
            logits = matmul(read(1, there).T, queries)
            if key_block == query_block:
                logits = jnp.where(causal_mask(0, BLOCK, BLOCK), logits, MASKED)
            new_peak = jnp.maximum(peak, jnp.max(logits, axis=0, keepdims=True))
            weights = jnp.exp(logits - new_peak)
            factor = jnp.exp(peak - new_peak)
            total = total * factor + jnp.sum(weights, axis=0, keepdims=True)
            accum = accum * factor + matmul(read(2, there), weights.astype(BF16))
            peak = new_peak
        write(query_block, here, accum / total, peak + jnp.log(total))


def norm_in(x, gain):
    average = jnp.mean(x, axis=-1, keepdims=True)
    centred = x - average
    inverse = lax.rsqrt(jnp.mean(centred * centred, axis=-1, keepdims=True) + EPSILON)
    return (centred * inverse * gain).astype(BF16)


def pack_kernel(slot_ref, x_ref, w_ref, gain_ref, a_ref, qkv_ref, o_ref, lse_ref, x_out, at):
    h = pl.program_id(0)

    @pl.when(h == 0)
    def _():
        x_out[...] = x_ref[0]
        a = norm_in(x_ref[0].astype(F32), gain_ref[:, 0:D])
        a_ref[...] = a
        at[...] = a.T
        for part in range(3):
            for k in range(0, D, 256):
                columns = slice(part * D + k, part * D + k + 256)
                qkv_ref[part, k : k + 256, :] = left_t(w_ref[:, columns], at[...]).astype(BF16)

    rows = pl.ds(pl.multiple_of(h * HEAD_DIM, HEAD_DIM), HEAD_DIM)

    def write(query_block, here, o, lse):
        o_ref[...] = o
        lse_ref[0:1, :] = lse

    attend_head(lambda part, columns: qkv_ref[part, rows, :], write, 1)


def pack_forward(slot, tokens, weight, gain):
    still = lambda *shape: pl.BlockSpec(shape, lambda h, slot: (0,) * len(shape))
    once = lambda *shape: pl.BlockSpec(
        shape, lambda h, slot: (0,) * len(shape), pipeline_mode=pl.Buffered(1)
    )
    by_head = lambda rows: pl.BlockSpec((rows, BLOCK), lambda h, slot: (h, 0))
    return pl.pallas_call(
        pack_kernel,
        grid_spec=pltpu.PrefetchScalarGridSpec(
            num_scalar_prefetch=1,
            grid=(HEADS,),
            in_specs=[
                pl.BlockSpec((1, BLOCK, D), lambda h, slot: (slot[0], 0, 0)),
                once(D, 3 * D),
                once(1, 3 * D + FF),
            ],
            out_specs=[still(BLOCK, D), still(3, D, BLOCK), by_head(HEAD_DIM), by_head(8)]
            + [still(BLOCK, D)],
            scratch_shapes=[pltpu.VMEM((D, BLOCK), BF16)],
        ),
        out_shape=[
            jax.ShapeDtypeStruct((BLOCK, D), BF16),
            jax.ShapeDtypeStruct((3, D, BLOCK), BF16),
            jax.ShapeDtypeStruct((D, BLOCK), F32),
            jax.ShapeDtypeStruct((HEADS * 8, BLOCK), F32),
            jax.ShapeDtypeStruct((BLOCK, D), BF16),
        ],
        compiler_params=pltpu.CompilerParams(vmem_limit_bytes=VMEM_LIMIT),
        cost_estimate=pl.CostEstimate(
            flops=8 * 10**9, bytes_accessed=10 * 2**20, transcendentals=HEADS * BLOCK * BLOCK
        ),
    )(slot, tokens, weight, gain)


def widened(gain, width):
    return jnp.concatenate([gain] * (width // 128), axis=1)


def column_stats(values):
    size = values.shape[0]
    average = jnp.sum(values, axis=0, keepdims=True) * (1.0 / size)
    centred = values - average
    spread = jnp.sum(centred * centred, axis=0, keepdims=True) * (1.0 / size)
    return average, lax.rsqrt(spread + EPSILON)


def gelu_both(values):
    t = 1.0 / (1.0 + (0.3275911 * 0.7071067811865476) * jnp.abs(values))
    density = jnp.exp(-0.5 * (values * values))
    tail = 0.5 * -1.453152027 + t * (0.5 * 1.061405429)
    tail = 0.5 * 1.421413741 + t * tail
    tail = 0.5 * -0.284496736 + t * tail
    tail = 0.5 * 0.254829592 + t * tail
    tail = tail * t * density
    below = jnp.where(values >= 0, 1.0 - tail, tail)
    return values * below, below + values * (density * 0.3989422804014327)


def feed_kernel(steps, chunk, sub, has_partial, slot, *refs):
    names = iter(refs)
    take = lambda count: [next(names) for _ in range(count)]
    o_in, x_in, dy_in, gain_ref, wo_in, wu_in, wd_in = take(7)
    part_in = take(3) if has_partial else []
    out_to, dh_to, do_to, go_to, gd_ref, gu_ref = take(6)
    o_ref, x_ref, dy_ref, wo, wu, wd, out_s, dh_s, do_s, go_s = take(10)
    ig, fg, hg, b_s, h_s, c_s, cn_s, dyt_s, n_s, slope_s, t_s, sum_s, dc_s, st = take(14)
    parts, part_o = take(2) if has_partial else (None, None)
    load_sem, wu_sem, wd_sem, part_sem, save_sem = take(5)
    width = BLOCK
    step = pl.program_id(0)
    o_load = pltpu.make_async_copy(o_in, o_ref, load_sem.at[0])
    wo_load = pltpu.make_async_copy(wo_in, wo, load_sem.at[1])
    x_load = pltpu.make_async_copy(x_in.at[slot[0]], x_ref, load_sem.at[2])
    dy_load = pltpu.make_async_copy(dy_in.at[slot[0]], dy_ref, load_sem.at[3])

    def span(k):
        return pl.ds(pl.multiple_of(k * chunk, chunk), chunk)

    def wu_load(k):
        return pltpu.make_async_copy(wu_in.at[:, span(k)], wu.at[:, span(k)], wu_sem.at[k])

    def wd_load(k):
        return pltpu.make_async_copy(wd_in.at[span(k), :], wd.at[span(k), :], wd_sem.at[k])

    def part_load(which, k):
        return pltpu.make_async_copy(
            part_in[which].at[span(k), :], parts.at[k], part_sem.at[which, k]
        )

    def save(k):
        source, target = [(out_s, out_to), (dh_s, dh_to), (do_s, do_to), (go_s, go_to)][k]
        return pltpu.make_async_copy(source, target, save_sem.at[k])

    @pl.when(step == 0)
    def _():
        for load in (o_load, wo_load, x_load):
            load.start()
        ig[...] = jnp.broadcast_to(gain_ref[:, D : 2 * D], (128, D)).T
        fg[...] = jnp.broadcast_to(gain_ref[:, 2 * D : 3 * D], (128, D)).T
        hg[...] = jnp.broadcast_to(gain_ref[:, 3 * D :], (128, FF)).T
        o_load.wait()
        o = o_ref[...].astype(F32)
        average, inverse = column_stats(o)
        b = ((o - average) * inverse * widened(ig[...], width)).astype(BF16)
        b_s[...] = b
        st[0:1] = average
        st[1:2] = inverse
        wo_load.wait()
        x_load.wait()
        wu_load(0).start()
        dy_load.start()
        h = x_ref[...].T.astype(F32) + left_t(wo[...], b)
        h_s[...] = h
        average, inverse = column_stats(h)
        st[2:3] = average
        st[3:4] = inverse
        c = ((h - average) * inverse * widened(fg[...], width)).astype(BF16)
        c_s[...] = c
        cn_s[...] = c.T
        dy_load.wait()
        dyt_s[...] = dy_ref[...].T
        for k in range(1, steps):
            wu_load(k).start()
        for k in range(steps):
            wd_load(k).start()
        if has_partial:
            for k in range(steps):
                part_load(0, k).start()
            pltpu.make_async_copy(part_in[2], part_o, load_sem.at[4]).start()

    @pl.when(step < steps)
    def _():
        wu_load(step).wait()
        base = pl.multiple_of(step * chunk, chunk)
        for k in range(chunk // sub):
            u = left_t(wu[:, pl.ds(base + k * sub, sub)], c_s[...])
            z, slope = gelu_both(u)
            n_s[pl.ds(base + k * sub, sub), :] = z
            slope_s[pl.ds(base + k * sub, sub), :] = slope.astype(BF16)

    @pl.when(step == steps - 1)
    def _():
        total = jnp.zeros((1, width), F32)
        for k in range(FF // sub):
            total = total + jnp.sum(n_s[k * sub : (k + 1) * sub, :], axis=0, keepdims=True)
        average = total * (1.0 / FF)
        total = jnp.zeros((1, width), F32)
        for k in range(FF // sub):
            centred = n_s[k * sub : (k + 1) * sub, :] - average
            total = total + jnp.sum(centred * centred, axis=0, keepdims=True)
        st[4:5] = average
        st[5:6] = lax.rsqrt(total * (1.0 / FF) + EPSILON)
        st[6:8] = jnp.zeros((2, width), F32)
        sum_s[...] = h_s[...]

    @pl.when((step >= steps) & (step < 2 * steps))
    def _():
        turn = step - steps
        wd_load(turn).wait()
        if has_partial:
            part_load(0, turn).wait()
        base = pl.multiple_of(turn * chunk, chunk)
        average = st[4:5]
        inverse = st[5:6]
        first = jnp.zeros((1, width), F32)
        second = jnp.zeros((1, width), F32)
        pieces = []
        for k in range(chunk // sub):
            rows = slice(k * sub, (k + 1) * sub)
            here = pl.ds(base + k * sub, sub)
            n = (n_s[here, :] - average) * inverse
            n_s[here, :] = n
            gain = widened(hg[here, :], width)
            e = (n * gain).astype(BF16)
            pieces.append(e)
            t = matmul(wd[here, :], dyt_s[...]) * gain
            t_s[here, :] = t
            first = first + jnp.sum(t, axis=0, keepdims=True)
            second = second + jnp.sum(t * n, axis=0, keepdims=True)
            grad = matmul(e, dy_ref[...])
            if has_partial:
                grad = grad + parts[turn, rows, :].astype(F32)
            gd_ref[rows, :] = grad.astype(BF16)
        sum_s[...] += left_t(wd[pl.ds(base, chunk), :], jnp.concatenate(pieces, axis=0))
        st[6:7] += first
        st[7:8] += second
        if has_partial:
            part_load(1, turn).start()

    @pl.when(step == 2 * steps - 1)
    def _():
        out_s[...] = sum_s[...].astype(BF16).T
        save(0).start()
        st[6:8] = st[6:8] * (1.0 / FF)
        dc_s[...] = jnp.zeros_like(dc_s)

    @pl.when(step >= 2 * steps)
    def _():
        turn = step - 2 * steps
        if has_partial:
            part_load(1, turn).wait()
        base = pl.multiple_of(turn * chunk, chunk)
        inverse = st[5:6]
        first = st[6:7]
        second = st[7:8]
        pieces = []
        for k in range(chunk // sub):
            rows = slice(k * sub, (k + 1) * sub)
            here = pl.ds(base + k * sub, sub)
            n = n_s[here, :]
            du = ((t_s[here, :] - first - n * second) * inverse * slope_s[here, :].astype(F32)).astype(BF16)
            pieces.append(du)
            grad = matmul(du, cn_s[...])
            if has_partial:
                grad = grad + parts[turn, rows, :].astype(F32)
            gu_ref[rows, :] = grad.astype(BF16)
        dc_s[...] += matmul(wu[:, pl.ds(base, chunk)], jnp.concatenate(pieces, axis=0))

    @pl.when(step == 3 * steps - 1)
    def _():
        n = (h_s[...] - st[2:3]) * st[3:4]
        t = dc_s[...] * widened(fg[...], width)
        first = jnp.sum(t, axis=0, keepdims=True) * (1.0 / D)
        second = jnp.sum(t * n, axis=0, keepdims=True) * (1.0 / D)
        dh = dyt_s[...].astype(F32) + (t - first - n * second) * st[3:4]
        dh_s[...] = dh
        save(1).start()
        dh_low = dh.astype(BF16)
        n = (o_ref[...].astype(F32) - st[0:1]) * st[1:2]
        t = matmul(wo[...], dh_low) * widened(ig[...], width)
        first = jnp.sum(t, axis=0, keepdims=True) * (1.0 / D)
        second = jnp.sum(t * n, axis=0, keepdims=True) * (1.0 / D)
        do_s[...] = ((t - first - n * second) * st[1:2]).astype(BF16)
        save(2).start()
        grad = matmul(b_s[...], dh_low.T)
        if has_partial:
            pltpu.make_async_copy(part_in[2], part_o, load_sem.at[4]).wait()
            grad = grad + part_o[...].astype(F32)
        go_s[...] = grad.astype(BF16)
        save(3).start()
        for k in range(4):
            save(k).wait()


def feed_both(slot, o_t, tokens, cotangent, gains, weights, partial=None, chunk=1536, sub=256):
    width = BLOCK
    steps = FF // chunk
    has_partial = partial is not None
    anywhere = pl.BlockSpec(memory_space=pl.ANY)
    second = lambda i, slot: (jnp.clip(i - steps, 0, steps - 1), 0)
    third = lambda i, slot: (jnp.clip(i - 2 * steps, 0, steps - 1), 0)
    dma = pltpu.SemaphoreType.DMA
    scratch = [
        pltpu.VMEM((D, width), o_t.dtype),
        pltpu.VMEM((width, D), BF16),
        pltpu.VMEM((width, D), BF16),
        pltpu.VMEM((D, D), BF16),
        pltpu.VMEM((D, FF), BF16),
        pltpu.VMEM((FF, D), BF16),
        pltpu.VMEM((width, D), BF16),
        pltpu.VMEM((D, width), F32),
        pltpu.VMEM((D, width), BF16),
        pltpu.VMEM((D, D), BF16),
        pltpu.VMEM((D, 128), F32),
        pltpu.VMEM((D, 128), F32),
        pltpu.VMEM((FF, 128), F32),
        pltpu.VMEM((D, width), BF16),
        pltpu.VMEM((D, width), F32),
        pltpu.VMEM((D, width), BF16),
        pltpu.VMEM((width, D), BF16),
        pltpu.VMEM((D, width), BF16),
        pltpu.VMEM((FF, width), F32),
        pltpu.VMEM((FF, width), BF16),
        pltpu.VMEM((FF, width), F32),
        pltpu.VMEM((D, width), F32),
        pltpu.VMEM((D, width), F32),
        pltpu.VMEM((8, width), F32),
    ]
    args = [o_t, tokens, cotangent, gains, *weights]
    if has_partial:
        args += list(partial)
        scratch += [pltpu.VMEM((steps, chunk, D), BF16), pltpu.VMEM((D, D), BF16)]
    scratch += [dma((5,)), dma((steps,)), dma((steps,)), dma((2, steps)), dma((4,))]
    return pl.pallas_call(
        functools.partial(feed_kernel, steps, chunk, sub, has_partial),
        grid_spec=pltpu.PrefetchScalarGridSpec(
            num_scalar_prefetch=1,
            grid=(3 * steps,),
            in_specs=[anywhere] * 3
            + [pl.BlockSpec(gains.shape, lambda i, slot: (0, 0), pipeline_mode=pl.Buffered(1))]
            + [anywhere] * (len(args) - 4),
            out_specs=[anywhere] * 4
            + [pl.BlockSpec((chunk, D), second), pl.BlockSpec((chunk, D), third)],
            scratch_shapes=scratch,
        ),
        out_shape=[
            jax.ShapeDtypeStruct((width, D), BF16),
            jax.ShapeDtypeStruct((D, width), F32),
            jax.ShapeDtypeStruct((D, width), BF16),
            jax.ShapeDtypeStruct((D, D), BF16),
            jax.ShapeDtypeStruct((FF, D), BF16),
            jax.ShapeDtypeStruct((FF, D), BF16),
        ],
        compiler_params=pltpu.CompilerParams(vmem_limit_bytes=62 * 2**20),
        cost_estimate=pl.CostEstimate(
            flops=6 * width * D * (D + 2 * FF), bytes_accessed=50 * 2**20, transcendentals=width * FF
        ),
    )(slot, *args)


def long_kernel(*refs):
    x0, x1, x2, x3, w_ref, gain_ref = refs[:6]
    qkv_ref, o_ref, lse_ref, do_ref, a_ref, x_ref, dh_ref = refs[6:13]
    a_out, qkv_out, o_out, lse_out, mine_out, gq_out, dx_out = refs[13:20]
    a_all, qkv, o_own, lse_own, o_low, w, qp, op, lp, dop, ap, xp, dhp, dp, gq, dx = refs[20:36]
    w_near, w_own, load_sem, save_sem, swap_send, swap_recv = refs[36:]
    gain_row = gain_ref[:, 0:D]
    r = lax.axis_index("rows")
    s = lax.axis_index("seq")
    shifted = [(r, (s + shift) % SEQ) for shift in range(SEQ)]
    barrier = pltpu.get_barrier_semaphore()
    for device in shifted[1:]:
        pl.semaphore_signal(barrier, inc=1, device_id=device, device_id_type=MESH)
    pl.semaphore_wait(barrier, SEQ - 1)
    sources = [qkv_ref, o_ref, lse_ref, do_ref, a_ref, x_ref, dh_ref, w_ref]
    targets = [qp, op, lp, dop, ap, xp, dhp, w]
    loads = [
        pltpu.make_async_copy(source, target, load_sem.at[k])
        for k, (source, target) in enumerate(zip(sources, targets))
    ]
    nears = [
        pltpu.make_async_copy(
            w_ref.at[:, pl.ds(pl.multiple_of(part * D + (3 * s // 2) * 128, 128), 256)],
            w_near.at[part],
            load_sem.at[8 + part],
        )
        for part in range(3)
    ]
    for load in nears + loads:
        load.start()
    saves = [
        pltpu.make_async_copy(source, target, save_sem.at[k])
        for k, (source, target) in enumerate(
            [(a_all, a_out), (qkv, qkv_out), (o_own, o_out), (lse_own, lse_out)]
            + [(gq, gq_out), (dx, dx_out)]
        )
    ]

    def o_copy(h, shift):
        part = o_low.at[(s + shift) % SEQ, pl.ds(h * HEAD_DIM, HEAD_DIM), :]
        place = pl.ds(pl.multiple_of(s * (HEADS_OWN * HEAD_DIM) + h * HEAD_DIM, 16), HEAD_DIM)
        target = mine_out.at[place, :]
        if shift == 0:
            return pltpu.make_async_copy(part, target, save_sem.at[6 + h])
        return pltpu.make_async_remote_copy(
            src_ref=part,
            dst_ref=target,
            send_sem=swap_send.at[h, shift],
            recv_sem=swap_recv.at[h, shift],
            device_id=shifted[shift],
            device_id_type=MESH,
        )

    for part in range(3):
        nears[part].wait()

        @pl.when(s % 2 == 0)
        def _():
            w_own[part] = w_near[part, :, 0:192]

        @pl.when(s % 2 == 1)
        def _():
            w_own[part] = w_near[part, :, 64:256]

    for shift, x in enumerate((x0, x1, x2, x3)):
        start = pl.multiple_of(((s - shift) % SEQ) * BLOCK, BLOCK)
        a = norm_in(x[...].astype(F32), gain_row)
        a_all[pl.ds(start, BLOCK), :] = a
        a_t = a.T
        for part in range(3):
            qkv[part, :, pl.ds(start, BLOCK)] = left_t(w_own[part], a_t).astype(BF16)
    saves[0].start()
    saves[1].start()
    for h in range(HEADS_OWN):
        rows = slice(h * HEAD_DIM, (h + 1) * HEAD_DIM)

        def write(query_block, here, o, lse):
            o_own[rows, here] = o
            lse_own[h, 0:1, here] = lse
            o_low[query_block, rows, :] = o.astype(BF16)

        attend_head(lambda part, columns: qkv[part, rows, columns], write, SEQ)
        for shift in range(SEQ):
            o_copy(h, shift).start()
    saves[2].start()
    saves[3].start()
    for load in loads:
        load.wait()

    def back(h, carry):
        rows = pl.ds(pl.multiple_of(h * HEAD_DIM, HEAD_DIM), HEAD_DIM)
        queries_t = (qp[0, rows, :].astype(F32) * 0.125).astype(BF16)
        keys_t = qp[1, rows, :]
        do_t = dop[rows, :]
        lse = lp[pl.ds(pl.multiple_of(h * 8, 8), 8), :][0:1]
        delta = jnp.sum(do_t.astype(F32) * op[rows, :], axis=0, keepdims=True)
        probs = jnp.exp(matmul(keys_t.T, queries_t) - lse)
        probs = jnp.where(causal_mask(0, BLOCK, BLOCK), probs, 0.0)
        dprobs = matmul(qp[2, rows, :].T, do_t)
        dlogits = (probs * (dprobs - delta)).astype(BF16)
        dp[0, rows, :] = (matmul(keys_t, dlogits) * 0.125).astype(BF16)
        dp[1, rows, :] = matmul(dlogits, queries_t.T).T.astype(BF16)
        dp[2, rows, :] = matmul(probs.astype(BF16), do_t.T).T.astype(BF16)
        return carry

    lax.fori_loop(0, HEADS, back, 0)
    for part in range(3):
        gq[part * D : (part + 1) * D, :] = matmul(dp[part], ap[...]).astype(BF16)
    saves[4].start()
    dx[...] = first_norm_back(xp[...], dhp[...], w, dp, gain_row)
    saves[5].start()
    for save in saves:
        save.wait()
    for h in range(HEADS_OWN):
        for shift in range(SEQ):
            o_copy(h, shift).wait()


def first_norm_back(x, dh_t, w, dqkv, gain):
    x_t = x.T.astype(F32)
    average, inverse = column_stats(x_t)
    n = (x_t - average) * inverse
    t = matmul(w[:, 0:D], dqkv[0])
    for part in range(1, 3):
        t = t + matmul(w[:, part * D : (part + 1) * D], dqkv[part])
    t = t * widened(jnp.broadcast_to(gain, (128, D)).T, BLOCK)
    first = jnp.sum(t, axis=0, keepdims=True) * (1.0 / D)
    second = jnp.sum(t * n, axis=0, keepdims=True) * (1.0 / D)
    return (dh_t + (t - first - n * second) * inverse).astype(BF16).T


def long_forward(x_blocks, weight, gains, pack, collective_id):
    own_rows = HEADS_OWN * HEAD_DIM
    length = SEQ * BLOCK
    dma = pltpu.SemaphoreType.DMA
    anywhere = pl.BlockSpec(memory_space=pl.ANY)
    resident = pl.BlockSpec(memory_space=pltpu.VMEM)
    return pl.pallas_call(
        long_kernel,
        in_specs=[resident] * 4 + [anywhere] + [resident] + [anywhere] * 7,
        out_specs=[anywhere] * 7,
        out_shape=[
            jax.ShapeDtypeStruct((length, D), BF16),
            jax.ShapeDtypeStruct((3, own_rows, length), BF16),
            jax.ShapeDtypeStruct((own_rows, length), F32),
            jax.ShapeDtypeStruct((HEADS_OWN, 8, length), F32),
            jax.ShapeDtypeStruct((D, BLOCK), BF16),
            jax.ShapeDtypeStruct((3 * D, D), BF16),
            jax.ShapeDtypeStruct((BLOCK, D), BF16),
        ],
        scratch_shapes=[
            pltpu.VMEM((length, D), BF16),
            pltpu.VMEM((3, own_rows, length), BF16),
            pltpu.VMEM((own_rows, length), F32),
            pltpu.VMEM((HEADS_OWN, 8, length), F32),
            pltpu.VMEM((SEQ, own_rows, BLOCK), BF16),
            pltpu.VMEM((D, 3 * D), BF16),
            pltpu.VMEM((3, D, BLOCK), BF16),
            pltpu.VMEM((D, BLOCK), F32),
            pltpu.VMEM((HEADS * 8, BLOCK), F32),
            pltpu.VMEM((D, BLOCK), BF16),
            pltpu.VMEM((BLOCK, D), BF16),
            pltpu.VMEM((BLOCK, D), BF16),
            pltpu.VMEM((D, BLOCK), F32),
            pltpu.VMEM((3, D, BLOCK), BF16),
            pltpu.VMEM((3 * D, D), BF16),
            pltpu.VMEM((BLOCK, D), BF16),
            pltpu.VMEM((3, D, 256), BF16),
            pltpu.VMEM((3, D, own_rows), BF16),
            dma((11,)),
            dma((6 + HEADS_OWN,)),
            dma((HEADS_OWN, SEQ)),
            dma((HEADS_OWN, SEQ)),
        ],
        compiler_params=pltpu.CompilerParams(
            collective_id=collective_id, has_side_effects=True, vmem_limit_bytes=VMEM_LIMIT
        ),
        cost_estimate=pl.CostEstimate(
            flops=20 * 10**9, bytes_accessed=40 * 2**20, transcendentals=10**7
        ),
    )(*x_blocks, weight, gains, *pack)


PIECE = 768
HALF = PIECE // 2
COLS = D // 2
FEED_PIECES = (2 * FF + D) // PIECE
QKV_PIECES = 3 * D // PIECE
PIECES = FEED_PIECES + QKV_PIECES
ATTEND_TICK = 2
QKV_TICK = 5
BACK_TICK = 3
BACKS = 1


def sum_kernel(*refs):
    gd, gu, go, gq, do_ref, qkv_ref, o_ref, lse_ref, a_ref, total_ref, back_ref = refs[:11]
    own, r0, r1, r2, r3, r4, fin, qkv, o_own, lse_own, a_all, gq_own, do_own, d_own = refs[11:25]
    dk_acc, dv_acc, own_sem, send_sem, recv_sem, fin_sem, in_sem, swap_send, swap_recv = refs[25:]
    r = lax.axis_index("rows")
    s = lax.axis_index("seq")
    core, xb, yb = r % 2, (r // 2) % 2, r // 4
    inside = (s == 1) | (s == 2)
    outside = (s == 0) | (s == 3)
    to_core = (r + 1 - 2 * core, s)
    to_x = (r + 2 - 4 * xb, s)
    to_y = (r + 4 - 8 * yb, s)
    to_pair = (r, s + 1 - 2 * (s % 2))
    to_middle = (r, 3 - s)
    shifted = [(r, (s + shift) % SEQ) for shift in range(SEQ)]
    barrier = pltpu.get_barrier_semaphore()
    for device in (to_core, to_x, to_y, *shifted[1:]):
        pl.semaphore_signal(barrier, inc=1, device_id=device, device_id_type=MESH)
    pl.semaphore_wait(barrier, 6)
    bits = [(xb, yb), (yb, xb)]
    partners = [(to_x, to_y), (to_y, to_x)]

    def rows_at(start, count):
        return pl.ds(pl.multiple_of(start, 16), count)

    def remote(source, target, send, recv, device):
        return pltpu.make_async_remote_copy(
            src_ref=source,
            dst_ref=target,
            send_sem=send,
            recv_sem=recv,
            device_id=device,
            device_id_type=MESH,
        )

    def numbered(source, target, kind, p, device):
        return remote(source, target, send_sem.at[kind, p], recv_sem.at[kind, p], device)

    def columns(o):
        return slice(o * COLS, (o + 1) * COLS)

    def base(o):
        return bits[o][0] * 192 + bits[o][1] * 96

    def core_copy(ref, q, p):
        part = ref.at[rows_at(q * PIECE + (1 - core) * HALF, HALF), :]
        return numbered(part, r0.at[p], 0, p, to_core)

    def own_copy(ref, q, p):
        part = ref.at[rows_at(q * PIECE + core * HALF, HALF), :]
        return pltpu.make_async_copy(part, own.at[p], own_sem.at[p])

    def first_copy(p, o):
        part = own.at[p, rows_at((1 - bits[o][0]) * 192, 192), columns(o)]
        return numbered(part, r1.at[p, o], 1 + o, p, partners[o][0])

    def second_copy(p, o):
        part = own.at[p, rows_at(bits[o][0] * 192 + (1 - bits[o][1]) * 96, 96), columns(o)]
        return numbered(part, r2.at[p, o], 3 + o, p, partners[o][1])

    def pair_copy(p, o):
        part = own.at[p, rows_at(base(o), 96), columns(o)]
        return numbered(part, r3.at[p, o], 5 + o, p, to_pair)

    def middle_copy(p, o):
        part = own.at[p, rows_at(base(o), 96), columns(o)]
        return numbered(part, r4.at[p, o], 7 + o, p, to_middle)

    def region(p, start, count, o):
        return total_ref.at[rows_at(p * PIECE + core * HALF + start, count), columns(o)]

    def fin_copy(p, o):
        return pltpu.make_async_copy(fin.at[p, o], region(p, base(o), 96, o), fin_sem.at[o, p])

    def pair_back(p, o):
        return numbered(fin.at[p, o], region(p, base(o), 96, o), 9 + o, p, to_pair)

    def second_back(p, o):
        part = region(p, base(o), 96, o)
        return numbered(part, part, 11 + o, p, partners[o][1])

    def first_back(p, o):
        part = region(p, bits[o][0] * 192, 192, o)
        return numbered(part, part, 13 + o, p, partners[o][0])

    def core_back(p):
        part = total_ref.at[rows_at(p * PIECE + core * HALF, HALF), :]
        return numbered(part, part, 15, p, to_core)

    def do_copy(shift):
        part = do_ref.at[(s + shift) % SEQ]
        if shift == 0:
            return pltpu.make_async_copy(part, do_own.at[s], in_sem.at[5])
        return remote(
            part, do_own.at[s], swap_send.at[0, shift], swap_recv.at[0, shift], shifted[shift]
        )

    def back_copy(h, shift):
        part = d_own.at[(s + shift) % SEQ, :, rows_at(h * HEAD_DIM, HEAD_DIM), :]
        target = back_ref.at[
            :, rows_at(s * (HEADS_OWN * HEAD_DIM) + h * HEAD_DIM, HEAD_DIM), :
        ]
        if shift == 0:
            return pltpu.make_async_copy(part, target, in_sem.at[6 + h])
        return remote(
            part, target, swap_send.at[1 + h, shift], swap_recv.at[1 + h, shift], shifted[shift]
        )

    loads = [
        pltpu.make_async_copy(qkv_ref, qkv, in_sem.at[0]),
        pltpu.make_async_copy(o_ref, o_own, in_sem.at[1]),
        pltpu.make_async_copy(lse_ref, lse_own, in_sem.at[2]),
        pltpu.make_async_copy(a_ref, a_all, in_sem.at[3]),
        pltpu.make_async_copy(gq, gq_own, in_sem.at[4]),
    ]
    for shift in range(1, SEQ):
        do_copy(shift).start()
    offset = 0
    for ref in (gd, gu, go):

        def begin(q, carry, ref=ref, offset=offset):
            core_copy(ref, q, q + offset).start()
            own_copy(ref, q, q + offset).start()
            return carry

        lax.fori_loop(0, ref.shape[0] // PIECE, begin, 0)
        offset += ref.shape[0] // PIECE
    do_copy(0).start()
    for load in loads:
        load.start()

    def added(index, other):
        own[index] = (own[index].astype(F32) + other.astype(F32)).astype(BF16)

    def after_core(p):
        own_copy(gd, 0, p).wait()
        core_copy(gd, 0, p).wait()
        own[p] = (own[p].astype(F32) + r0[p].astype(F32)).astype(BF16)
        for o in range(2):
            first_copy(p, o).start()

    def after_first(p):
        for o in range(2):
            first_copy(p, o).wait()
            added((p, rows_at(bits[o][0] * 192, 192), columns(o)), r1[p, o])
            second_copy(p, o).start()

    def after_second(p):
        for o in range(2):
            second_copy(p, o).wait()
            added((p, rows_at(base(o), 96), columns(o)), r2[p, o])

            @pl.when(outside)
            def _():
                pair_copy(p, o).start()

    def after_pair(p):
        for o in range(2):

            @pl.when(outside)
            def _():
                pair_copy(p, o).wait_send()

            @pl.when(inside)
            def _():
                pair_copy(p, o).wait_recv()
                added((p, rows_at(base(o), 96), columns(o)), r3[p, o])
                middle_copy(p, o).start()

    def after_middle(p):
        for o in range(2):

            @pl.when(inside)
            def _():
                middle_copy(p, o).wait()
                mine = own[p, rows_at(base(o), 96), columns(o)].astype(F32)
                fin[p, o] = (mine + r4[p, o].astype(F32)).astype(BF16)
                pair_back(p, o).start()
                fin_copy(p, o).start()

    def after_pair_back(p):
        for o in range(2):

            @pl.when(inside)
            def _():
                fin_copy(p, o).wait()
                pair_back(p, o).wait_send()

            @pl.when(outside)
            def _():
                pair_back(p, o).wait_recv()

            second_back(p, o).start()

    def after_second_back(p):
        for o in range(2):
            second_back(p, o).wait()
            first_back(p, o).start()

    def after_first_back(p):
        for o in range(2):
            first_back(p, o).wait()
        core_back(p).start()

    def after_core_back(p):
        core_back(p).wait()

    stages = [
        after_core,
        after_first,
        after_second,
        after_pair,
        after_middle,
        after_pair_back,
        after_second_back,
        after_first_back,
        after_core_back,
    ]

    def head_rows(h):
        return rows_at(h * HEAD_DIM, HEAD_DIM)

    def attend(h, query_block):
        rows = head_rows(h)
        here = slice(query_block * BLOCK, (query_block + 1) * BLOCK)
        queries_t = (qkv[0, rows, here].astype(F32) * 0.125).astype(BF16)
        queries = queries_t.T
        do_t = do_own[query_block, rows, :]
        do_rows = do_t.T
        lse = lse_own[h, 0:1, here]
        delta = jnp.sum(do_t.astype(F32) * o_own[rows, here], axis=0, keepdims=True)
        dq = jnp.zeros((HEAD_DIM, BLOCK), F32)
        for key_block in range(query_block + 1):
            there = slice(key_block * BLOCK, (key_block + 1) * BLOCK)
            keys_t = qkv[1, rows, there]
            probs = jnp.exp(matmul(keys_t.T, queries_t) - lse)
            if key_block == query_block:
                probs = jnp.where(causal_mask(0, BLOCK, BLOCK), probs, 0.0)
            dprobs = matmul(qkv[2, rows, there].T, do_t)
            dlogits = (probs * (dprobs - delta)).astype(BF16)
            dq = dq + matmul(keys_t, dlogits)
            dv_acc[there, :] += matmul(probs.astype(BF16), do_rows)
            dk_acc[there, :] += matmul(dlogits, queries)
        d_own[query_block, 0, rows, :] = (dq * 0.125).astype(BF16)

    def finish_head(h):
        rows = head_rows(h)
        total = jnp.zeros((3 * HEAD_DIM, D), F32)
        for block in range(SEQ):
            here = slice(block * BLOCK, (block + 1) * BLOCK)
            d_own[block, 1, rows, :] = dk_acc[here, :].T.astype(BF16)
            d_own[block, 2, rows, :] = dv_acc[here, :].T.astype(BF16)
            joined = d_own[block, :, rows, :].reshape(3 * HEAD_DIM, BLOCK)
            total = total + matmul(joined, a_all[here, :])
        for part in range(3):
            place = rows_at(part * D + s * (HEADS_OWN * HEAD_DIM) + h * HEAD_DIM, HEAD_DIM)
            term = total[part * HEAD_DIM : (part + 1) * HEAD_DIM, :]
            gq_own[place, :] = (gq_own[place, :].astype(F32) + term).astype(BF16)
        back_copy(h, 0).start()

    def tick(t, carry):
        for lag, stage in enumerate(stages):
            for sub in range(2):
                p = 2 * (t - lag) + sub

                @pl.when((p >= 0) & (p < FEED_PIECES))
                def _():
                    stage(p)

                q = 2 * (t - lag - QKV_TICK) + sub

                @pl.when((q >= 0) & (q < QKV_PIECES))
                def _():
                    stage(FEED_PIECES + q)

        @pl.when(t == ATTEND_TICK)
        def _():
            for load in loads:
                load.wait()
            for shift in range(SEQ):
                do_copy(shift).wait()

        h = t - ATTEND_TICK

        @pl.when((h >= 0) & (h < HEADS_OWN))
        def _():
            dk_acc[...] = jnp.zeros_like(dk_acc)
            dv_acc[...] = jnp.zeros_like(dv_acc)
            for query_block in range(SEQ):
                attend(h, query_block)
            finish_head(h)

        @pl.when(h == HEADS_OWN - 1)
        def _():
            for q in range(QKV_PIECES):
                core_copy(gq_own, q, FEED_PIECES + q).start()
                own_copy(gq_own, q, FEED_PIECES + q).start()

        for unit in range(3 * HEADS_OWN):

            @pl.when(t == BACK_TICK + unit // BACKS)
            def _():
                back_copy(unit // 3, unit % 3 + 1).start()

        return carry

    last = QKV_TICK + (QKV_PIECES - 1) // 2 + len(stages)
    lax.fori_loop(0, last, tick, 0)
    for h in range(HEADS_OWN):
        for shift in range(SEQ):
            back_copy(h, shift).wait()


def summed_everywhere(gd, gu, go, gq, do_pieces, qkv_own, o_own, lse, a_all, collective_id):
    n = PIECES
    length = SEQ * BLOCK
    own_rows = HEADS_OWN * HEAD_DIM
    dma = pltpu.SemaphoreType.DMA
    anywhere = pl.BlockSpec(memory_space=pl.ANY)
    return pl.pallas_call(
        sum_kernel,
        out_shape=[
            jax.ShapeDtypeStruct((n * PIECE, D), BF16),
            jax.ShapeDtypeStruct((3, D, BLOCK), BF16),
        ],
        in_specs=[anywhere] * 9,
        out_specs=[anywhere] * 2,
        scratch_shapes=[
            pltpu.VMEM((n, HALF, D), BF16),
            pltpu.VMEM((n, HALF, D), BF16),
            pltpu.VMEM((n, 2, 192, COLS), BF16),
            pltpu.VMEM((n, 2, 96, COLS), BF16),
            pltpu.VMEM((n, 2, 96, COLS), BF16),
            pltpu.VMEM((n, 2, 96, COLS), BF16),
            pltpu.VMEM((n, 2, 96, COLS), BF16),
            pltpu.VMEM((3, own_rows, length), BF16),
            pltpu.VMEM((own_rows, length), F32),
            pltpu.VMEM((HEADS_OWN, 8, length), F32),
            pltpu.VMEM((length, D), BF16),
            pltpu.VMEM((3 * D, D), BF16),
            pltpu.VMEM((SEQ, own_rows, BLOCK), BF16),
            pltpu.VMEM((SEQ, 3, own_rows, BLOCK), BF16),
            pltpu.VMEM((length, HEAD_DIM), F32),
            pltpu.VMEM((length, HEAD_DIM), F32),
            dma((n,)),
            dma((16, n)),
            dma((16, n)),
            dma((2, n)),
            dma((6 + HEADS_OWN,)),
            dma((1 + HEADS_OWN, SEQ)),
            dma((1 + HEADS_OWN, SEQ)),
        ],
        compiler_params=pltpu.CompilerParams(
            collective_id=collective_id, has_side_effects=True, vmem_limit_bytes=VMEM_LIMIT
        ),
        cost_estimate=pl.CostEstimate(flops=0, bytes_accessed=n * PIECE * D * 64, transcendentals=0),
    )(gd, gu, go, gq, do_pieces, qkv_own, o_own, lse, a_all)


def shifted_by(value, shift):
    return lax.ppermute(value, "seq", [(i, (i + shift) % SEQ) for i in range(SEQ)])


def finish_kernel(slots, *refs):
    total, wd, wu, wo, wq, gain_ref = refs[:6]
    dqkv_ref, dh_ref, tokens, out_pack, out_long, dx_pack = refs[6:12]
    gd, gu, go, gq, si, sf, sh, sa, output, grad_out = refs[12:22]
    acc, dqkv, dh_t, x_long, dx, rows, load_sem, copy_sem = refs[22:]
    step = pl.program_id(0)
    sources = [dqkv_ref, dh_ref, tokens.at[slots[0]]]
    targets = [dqkv, dh_t, x_long]
    loads = [
        pltpu.make_async_copy(source, target, load_sem.at[k])
        for k, (source, target) in enumerate(zip(sources, targets))
    ]
    fetches = [
        pltpu.make_async_copy(source, rows.at[k], load_sem.at[3 + k])
        for k, source in enumerate((out_long, out_pack, dx_pack))
    ]
    copies = [
        pltpu.make_async_copy(rows.at[0], output.at[slots[0]], copy_sem.at[0]),
        pltpu.make_async_copy(rows.at[1], output.at[slots[1]], copy_sem.at[1]),
        pltpu.make_async_copy(rows.at[2], grad_out.at[slots[1]], copy_sem.at[2]),
    ]
    last = pltpu.make_async_copy(dx, grad_out.at[slots[0]], copy_sem.at[3])

    def lanes(values):
        folded = values[:, 0:128]
        for k in range(1, D // 128):
            folded = folded + values[:, k * 128 : (k + 1) * 128]
        return folded

    def as_row(folded, start):
        gain = gain_ref[:, pl.ds(pl.multiple_of(start, D), D)]
        return (jnp.sum(folded.T, axis=0, keepdims=True) / gain)[0]

    @pl.when(step == 0)
    def _():
        for copy in loads + fetches:
            copy.start()

    @pl.when(step == 4)
    def _():
        for fetch, copy in zip(fetches, copies):
            fetch.wait()
            copy.start()

    @pl.when(step < 4)
    def _():
        grad = total[...].astype(F32)
        gd[...] = grad
        rows_here = pl.ds(pl.multiple_of(step * D, D), D)
        sh[rows_here] = as_row(lanes(grad * wd[...].astype(F32)), (3 + step) * D)

    @pl.when((step >= 4) & (step < 8))
    def _():
        grad = total[...].T.astype(F32)
        gu[...] = grad
        acc[0] = lanes(grad * wu[...].astype(F32)) + jnp.where(step == 4, 0.0, acc[0])

    @pl.when(step == 8)
    def _():
        sf[...] = as_row(acc[0], 2 * D)
        grad = total[...].astype(F32)
        go[...] = grad
        si[...] = as_row(lanes(grad * wo[...].astype(F32)), D)

    @pl.when(step == 6)
    def _():
        for load in loads:
            load.wait()
        dx[...] = first_norm_back(x_long[...], dh_t[...], wq, dqkv, gain_ref[:, 0:D])
        last.start()

    @pl.when(step >= 9)
    def _():
        grad = total[...].T.astype(F32)
        gq[...] = grad
        columns = pl.ds(pl.multiple_of((step - 9) * D, D), D)
        acc[1] = lanes(grad * wq[:, columns].astype(F32)) + jnp.where(step == 9, 0.0, acc[1])

    @pl.when(step == 11)
    def _():
        sa[...] = as_row(acc[1], 0)
        for copy in copies:
            copy.wait()
        last.wait()


def finished(slots, total, weights, gains, rows):
    down_weight, up_weight, out_weight, query_key_value = weights
    square = lambda index: pl.BlockSpec((D, D), index)
    row = lambda index: pl.BlockSpec((D,), index)
    at_down = lambda i, slots: (jnp.clip(i, 0, 3), 0)
    at_up = lambda i, slots: (0, jnp.clip(i - 4, 0, 3))
    at_qkv = lambda i, slots: (0, jnp.clip(i - 9, 0, 2))
    still = lambda i, slots: (0, 0)
    only = lambda i, slots: (0,)
    once = lambda *shape: pl.BlockSpec(shape, still, pipeline_mode=pl.Buffered(1))
    anywhere = pl.BlockSpec(memory_space=pl.ANY)
    shapes = [(FF, D), (D, FF), (D, D), (D, 3 * D), (D,), (D,), (FF,), (D,)]
    pair = jax.ShapeDtypeStruct((2, BLOCK, D), BF16)
    dma = pltpu.SemaphoreType.DMA
    return pl.pallas_call(
        finish_kernel,
        grid_spec=pltpu.PrefetchScalarGridSpec(
            num_scalar_prefetch=1,
            grid=(PIECES,),
            in_specs=[square(lambda i, slots: (i, 0)), square(at_down), square(at_up)]
            + [once(D, D), once(D, 3 * D), once(1, 3 * D + FF)]
            + [anywhere] * 6,
            out_specs=[square(at_down), square(at_up), square(still), square(at_qkv)]
            + [row(only), row(only), pl.BlockSpec((FF,), only), row(only)]
            + [anywhere] * 2,
            scratch_shapes=[
                pltpu.VMEM((2, D, 128), F32),
                pltpu.VMEM((3, D, BLOCK), BF16),
                pltpu.VMEM((D, BLOCK), F32),
                pltpu.VMEM((BLOCK, D), BF16),
                pltpu.VMEM((BLOCK, D), BF16),
                pltpu.VMEM((3, BLOCK, D), BF16),
                dma((6,)),
                dma((4,)),
            ],
        ),
        out_shape=[jax.ShapeDtypeStruct(shape, F32) for shape in shapes] + [pair, pair],
        compiler_params=pltpu.CompilerParams(vmem_limit_bytes=VMEM_LIMIT),
        cost_estimate=pl.CostEstimate(
            flops=2 * 10**9, bytes_accessed=56 * 2**20, transcendentals=0
        ),
    )(
        slots,
        total,
        down_weight,
        up_weight,
        out_weight,
        query_key_value,
        gains,
        *rows,
    )


def split_layer(
    tokens,
    segment_ids,
    cotangent,
    query_key_value,
    out_weight,
    up_weight,
    down_weight,
    attend_gain,
    inner_gain,
    feed_gain,
    hidden_gain,
):
    long_first = segment_ids[0, -1] == 0
    x_long = jnp.where(long_first, tokens[0], tokens[1])
    x_blocks = [x_long] + [shifted_by(x_long, shift) for shift in range(1, SEQ)]
    long_slot = jnp.where(long_first, 0, 1).astype(jnp.int32)
    slots = jnp.stack([long_slot, 1 - long_slot])
    gains = jnp.concatenate([attend_gain, inner_gain, feed_gain, hidden_gain])[None]
    weights = (out_weight, up_weight, down_weight)
    a_pack, qkv_pack, o_pack, lse_pack, x_pack = pack_forward(
        slots[1:], tokens, query_key_value, gains
    )
    out_pack, dh_pack, do_pack, go_pack, gd_pack, gu_pack = feed_both(
        slots[1:], o_pack, tokens, cotangent, gains, weights
    )
    *x_blocks, do_pack = lax.optimization_barrier((*x_blocks, do_pack))
    a_all, qkv_long, o_long, lse_long, o_mine, gq_pack, dx_pack = long_forward(
        x_blocks,
        query_key_value,
        gains,
        (qkv_pack, o_pack, lse_pack, do_pack, a_pack, x_pack, dh_pack),
        1,
    )
    out_long, dh_long, do_long, go, gd, gu = feed_both(
        slots[:1], o_mine, tokens, cotangent, gains, weights, (gd_pack, gu_pack, go_pack)
    )
    total, dqkv_long = summed_everywhere(
        gd,
        gu,
        go,
        gq_pack,
        do_long.reshape(SEQ, HEADS_OWN * HEAD_DIM, BLOCK),
        qkv_long,
        o_long,
        lse_long,
        a_all,
        0,
    )
    down_grad, up_grad, out_grad, qkv_grad, *sums, output, tokens_grad = finished(
        slots,
        total,
        (down_weight, up_weight, out_weight, query_key_value),
        gains,
        (dqkv_long, dh_long, tokens, out_pack, out_long, dx_pack),
    )
    inner_total, feed_total, hidden_total, attend_total = sums
    return (
        output,
        tokens_grad,
        qkv_grad,
        out_grad,
        up_grad,
        down_grad,
        attend_total,
        inner_total,
        feed_total,
        hidden_total,
    )


def per_device(tokens, *others):
    split = lax.axis_size("seq") == SEQ and lax.axis_size("rows") == 8
    if split and tokens.shape == (2, BLOCK, D):
        return split_layer(tokens, *others)
    return ring_layer(tokens, *others)


def solution(mesh):
    return jax.shard_map(
        per_device,
        mesh=mesh,
        in_specs=(
            P("rows", "seq", None),
            P("rows", None),
            P("rows", "seq", None),
            P(),
            P(),
            P(),
            P(),
            P(),
            P(),
            P(),
            P(),
        ),
        out_specs=(
            P("rows", "seq", None),
            P("rows", "seq", None),
            P(),
            P(),
            P(),
            P(),
            P(),
            P(),
            P(),
            P(),
        ),
        check_vma=False,
    )
```

```python
import functools
import math

import jax
import jax.numpy as jnp
from jax import lax
from jax.experimental import pallas as pl
from jax.experimental.pallas import tpu as pltpu
from jax.sharding import PartitionSpec as P

D = 768
HEADS = 12
HEAD_DIM = 64


EPSILON = 1e-05
MASKED = -1e30


def passed_along(value, axis, steps):
    count = lax.axis_size(axis)
    initial, last = (max(0, -steps), min(count, count - steps))
    return lax.ppermute(value, axis, [(source, source + steps) for source in range(initial, last)])


def from_behind(value, axis, steps):
    count = lax.axis_size(axis)
    pairs = [(source, (source + steps) % count) for source in range(count)]
    return lax.ppermute(value, axis, pairs)


def layer_norm(values, gain):
    average = jnp.mean(values, axis=-1, keepdims=True)
    centred = values - average
    inverse = lax.rsqrt(jnp.mean(centred * centred, axis=-1, keepdims=True) + EPSILON)
    normed = centred * inverse
    return (normed * gain, normed, inverse)


def norm_back(upstream, normed, inverse, gain):
    scaled = upstream * gain
    spread = (
        scaled
        - jnp.mean(scaled, axis=-1, keepdims=True)
        - normed * jnp.mean(scaled * normed, axis=-1, keepdims=True)
    )
    return (spread * inverse, jnp.sum(upstream * normed, axis=0))


def gelu_exact(values):
    return jax.nn.gelu(values, approximate=False)


def matmul(left, right):
    return jnp.dot(left, right, preferred_element_type=jnp.float32)


def left_t(left, right):
    return lax.dot_general(
        left, right, (((0,), (0,)), ((), ())), preferred_element_type=jnp.float32
    )


def right_t(left, right):
    return lax.dot_general(
        left, right, (((1,), (1,)), ((), ())), preferred_element_type=jnp.float32
    )


def split_heads(values):
    return values.reshape(values.shape[0], values.shape[1], HEADS, HEAD_DIM)


def allowed_pairs(query_pos, query_seg, key_pos, key_seg):
    causal = key_pos[None, None, None, :] <= query_pos[None, None, :, None]
    same_doc = key_seg[:, None, None, :] == query_seg[:, None, :, None]
    return causal & same_doc


def scores(queries, key_rows):
    return jnp.einsum(
        "rqhd,rkhd->rhqk",
        split_heads(queries),
        split_heads(key_rows),
        preferred_element_type=jnp.float32,
    ) * HEAD_DIM ** (-0.5)


def fold_keys(carry, piece, queries, query_pos, query_seg, segment_ids):
    key_rows, value_rows = piece
    row_count = key_rows.shape[0]
    key_count = key_rows.shape[1]
    block_width = math.gcd(key_count, queries.shape[1])
    block_count = key_count // block_width
    key_blocks = key_rows.reshape(row_count, block_count, block_width, D).transpose(1, 0, 2, 3)
    value_blocks = value_rows.reshape(row_count, block_count, block_width, D).transpose(1, 0, 2, 3)

    def one_block(state, block_item):
        accum, running, softmax_total = state
        key_block, value_block, offset = block_item
        key_start = offset * block_width
        key_pos = key_start + jnp.arange(block_width, dtype=jnp.int32)
        key_seg = lax.dynamic_slice_in_dim(segment_ids, key_start, block_width, 1)
        allowed = allowed_pairs(query_pos, query_seg, key_pos, key_seg)
        logits = jnp.where(allowed, scores(queries, key_block), MASKED)
        new_peak = jnp.maximum(running, jnp.max(logits, axis=-1))
        weights = jnp.where(allowed, jnp.exp(logits - new_peak[..., None]), 0.0)
        factor = jnp.exp(running - new_peak)
        softmax_total = softmax_total * factor + jnp.sum(weights, axis=-1)
        accum = accum * factor[..., None] + jnp.einsum(
            "rhqk,rkhd->rhqd",
            weights.astype(jnp.bfloat16),
            split_heads(value_block),
            preferred_element_type=jnp.float32,
        )
        return ((accum, new_peak, softmax_total), None)

    carry, unused = lax.scan(
        one_block, carry, (key_blocks, value_blocks, jnp.arange(block_count, dtype=jnp.int32))
    )
    return carry


def back_block(queries, grad_rows, log_total, delta, key_rows, value_rows, allowed):
    logits = jnp.where(allowed, scores(queries, key_rows), MASKED)
    probs = jnp.where(allowed, jnp.exp(logits - log_total[..., None]), 0.0)
    dprobs = jnp.einsum(
        "rqhd,rkhd->rhqk",
        split_heads(grad_rows),
        split_heads(value_rows),
        preferred_element_type=jnp.float32,
    )
    dlogits = (probs * (dprobs - delta[..., None])).astype(jnp.bfloat16)
    factor = HEAD_DIM ** (-0.5)
    query_part = (
        jnp.einsum(
            "rhqk,rkhd->rqhd", dlogits, split_heads(key_rows), preferred_element_type=jnp.float32
        )
        * factor
    )
    key_part = (
        jnp.einsum(
            "rhqk,rqhd->rkhd", dlogits, split_heads(queries), preferred_element_type=jnp.float32
        )
        * factor
    )
    value_part = jnp.einsum(
        "rhqk,rqhd->rkhd",
        probs.astype(jnp.bfloat16),
        split_heads(grad_rows),
        preferred_element_type=jnp.float32,
    )
    return (
        query_part.reshape(queries.shape),
        key_part.reshape(key_rows.shape),
        value_part.reshape(value_rows.shape),
    )


def ring_layer(
    tokens,
    segment_ids,
    cotangent,
    query_key_value,
    out_weight,
    up_weight,
    down_weight,
    attend_gain,
    inner_gain,
    feed_gain,
    hidden_gain,
):
    row_count = tokens.shape[0]
    width_q = tokens.shape[1]
    model_width = tokens.shape[2]
    token_count = row_count * width_q
    seq_index = lax.axis_index("seq")
    seq_size = lax.axis_size("seq")
    local_pos = seq_index * width_q + jnp.arange(width_q, dtype=jnp.int32)
    local_seg = lax.dynamic_slice_in_dim(segment_ids, seq_index * width_q, width_q, 1)
    residual = tokens.reshape(token_count, model_width).astype(jnp.float32)
    attend_out, attend_normed, attend_inverse = layer_norm(residual, attend_gain)
    attend_low = attend_out.astype(jnp.bfloat16)
    projected = matmul(attend_low, query_key_value).astype(jnp.bfloat16)
    queries = projected[:, :model_width].reshape(row_count, width_q, model_width)
    key_rows = projected[:, model_width : 2 * model_width].reshape(row_count, width_q, model_width)
    value_rows = projected[:, 2 * model_width :].reshape(row_count, width_q, model_width)
    start_state = (
        jnp.zeros((row_count, HEADS, width_q, HEAD_DIM), jnp.float32),
        jnp.full((row_count, HEADS, width_q), MASKED, jnp.float32),
        jnp.zeros((row_count, HEADS, width_q), jnp.float32),
    )
    accum, running, softmax_total = fold_keys(
        start_state,
        (
            lax.all_gather(key_rows, "seq", axis=1, tiled=True),
            lax.all_gather(value_rows, "seq", axis=1, tiled=True),
        ),
        queries,
        local_pos,
        local_seg,
        segment_ids,
    )
    log_total = running + jnp.log(softmax_total)
    attended = (accum / softmax_total[..., None]).transpose(0, 2, 1, 3)
    attended_flat = attended.reshape(token_count, model_width)
    inner_out, inner_normed, inner_inverse = layer_norm(attended_flat, inner_gain)
    inner_low = inner_out.astype(jnp.bfloat16)
    state = residual + matmul(inner_low, out_weight)
    feed_out, feed_normed, feed_inverse = layer_norm(state, feed_gain)
    feed_low = feed_out.astype(jnp.bfloat16)
    pre_act = matmul(feed_low, up_weight)
    hidden, gelu_back = jax.vjp(gelu_exact, pre_act)
    hidden_out, hidden_normed, hidden_inverse = layer_norm(hidden, hidden_gain)
    hidden_low = hidden_out.astype(jnp.bfloat16)
    result = state + matmul(hidden_low, down_weight)
    output = result.astype(jnp.bfloat16).reshape(tokens.shape)
    upstream_low = cotangent.reshape(token_count, model_width)
    upstream = upstream_low.astype(jnp.float32)
    down_term = left_t(hidden_low, upstream_low)
    hidden_grad, hidden_gain_term = norm_back(
        right_t(upstream_low, down_weight), hidden_normed, hidden_inverse, hidden_gain
    )
    pre_grad = gelu_back(hidden_grad)[0]
    pre_low = pre_grad.astype(jnp.bfloat16)
    up_term = left_t(feed_low, pre_low)
    feed_grad, feed_gain_term = norm_back(
        right_t(pre_low, up_weight), feed_normed, feed_inverse, feed_gain
    )
    state_grad = upstream + feed_grad
    state_low = state_grad.astype(jnp.bfloat16)
    out_term = left_t(inner_low, state_low)
    inner_grad, inner_gain_term = norm_back(
        right_t(state_low, out_weight), inner_normed, inner_inverse, inner_gain
    )
    attend_grad_low = inner_grad.astype(jnp.bfloat16).reshape(row_count, width_q, model_width)
    delta = jnp.sum(split_heads(attend_grad_low).astype(jnp.float32) * attended, axis=-1).transpose(
        0, 2, 1
    )
    zero_rows = jnp.zeros((row_count, width_q, model_width), jnp.float32)

    def key_step(step_count, cycle_state):
        moving_keys, moving_values, moving_dkeys, moving_dvalues, query_acc = cycle_state
        source = jnp.remainder(seq_index - step_count, seq_size)
        key_start = source * width_q
        key_pos = key_start + jnp.arange(width_q, dtype=jnp.int32)
        key_seg = lax.dynamic_slice_in_dim(segment_ids, key_start, width_q, 1)
        allowed = allowed_pairs(local_pos, local_seg, key_pos, key_seg)
        query_part, key_part, value_part = back_block(
            queries, attend_grad_low, log_total, delta, moving_keys, moving_values, allowed
        )
        moving_keys, moving_values = passed_along((moving_keys, moving_values), "seq", 1)
        moving_dkeys, moving_dvalues = (
            from_behind((moving_dkeys + key_part).astype(jnp.bfloat16), "seq", 1).astype(
                jnp.float32
            ),
            from_behind((moving_dvalues + value_part).astype(jnp.bfloat16), "seq", 1).astype(
                jnp.float32
            ),
        )
        return (moving_keys, moving_values, moving_dkeys, moving_dvalues, query_acc + query_part)

    cycle_out = lax.fori_loop(
        0, seq_size, key_step, (key_rows, value_rows, zero_rows, zero_rows, zero_rows)
    )
    key_grad, value_grad, query_grad = (cycle_out[2], cycle_out[3], cycle_out[4])
    joined_grad = jnp.concatenate(
        [
            query_grad.astype(jnp.bfloat16),
            key_grad.astype(jnp.bfloat16),
            value_grad.astype(jnp.bfloat16),
        ],
        axis=-1,
    ).reshape(token_count, 3 * model_width)
    qkv_term = left_t(attend_low, joined_grad)
    attend_back, attend_gain_term = norm_back(
        right_t(joined_grad, query_key_value), attend_normed, attend_inverse, attend_gain
    )
    tokens_grad = (state_grad + attend_back).astype(jnp.bfloat16).reshape(tokens.shape)
    all_sectioned = (
        lax.psum_scatter(
            qkv_term.astype(jnp.bfloat16), "rows", scatter_dimension=0, tiled=True
        ).astype(jnp.float32),
        lax.psum_scatter(
            out_term.astype(jnp.bfloat16), "rows", scatter_dimension=0, tiled=True
        ).astype(jnp.float32),
        lax.psum_scatter(
            up_term.astype(jnp.bfloat16), "rows", scatter_dimension=0, tiled=True
        ).astype(jnp.float32),
        lax.psum_scatter(
            down_term.astype(jnp.bfloat16), "rows", scatter_dimension=0, tiled=True
        ).astype(jnp.float32),
    )
    seq_sectioned = (
        lax.psum_scatter(
            all_sectioned[0].astype(jnp.bfloat16), "seq", scatter_dimension=1, tiled=True
        ).astype(jnp.float32),
        lax.psum_scatter(
            all_sectioned[1].astype(jnp.bfloat16), "seq", scatter_dimension=1, tiled=True
        ).astype(jnp.float32),
        lax.psum_scatter(
            all_sectioned[2].astype(jnp.bfloat16), "seq", scatter_dimension=1, tiled=True
        ).astype(jnp.float32),
        lax.psum_scatter(
            all_sectioned[3].astype(jnp.bfloat16), "seq", scatter_dimension=1, tiled=True
        ).astype(jnp.float32),
    )
    seq_whole = (
        lax.all_gather(seq_sectioned[0].astype(jnp.bfloat16), "seq", axis=1, tiled=True).astype(
            jnp.float32
        ),
        lax.all_gather(seq_sectioned[1].astype(jnp.bfloat16), "seq", axis=1, tiled=True).astype(
            jnp.float32
        ),
        lax.all_gather(seq_sectioned[2].astype(jnp.bfloat16), "seq", axis=1, tiled=True).astype(
            jnp.float32
        ),
        lax.all_gather(seq_sectioned[3].astype(jnp.bfloat16), "seq", axis=1, tiled=True).astype(
            jnp.float32
        ),
    )
    qkv_grad, out_grad, up_grad, down_grad = (
        lax.all_gather(seq_whole[0].astype(jnp.bfloat16), "rows", axis=0, tiled=True).astype(
            jnp.float32
        ),
        lax.all_gather(seq_whole[1].astype(jnp.bfloat16), "rows", axis=0, tiled=True).astype(
            jnp.float32
        ),
        lax.all_gather(seq_whole[2].astype(jnp.bfloat16), "rows", axis=0, tiled=True).astype(
            jnp.float32
        ),
        lax.all_gather(seq_whole[3].astype(jnp.bfloat16), "rows", axis=0, tiled=True).astype(
            jnp.float32
        ),
    )
    attend_total, inner_total, feed_total, hidden_total = lax.psum(
        (attend_gain_term, inner_gain_term, feed_gain_term, hidden_gain_term), ("rows", "seq")
    )
    return (
        output,
        tokens_grad,
        qkv_grad,
        out_grad,
        up_grad,
        down_grad,
        attend_total,
        inner_total,
        feed_total,
        hidden_total,
    )


FF = 3072
SEQ = 4
BLOCK = 512
SPLIT = BLOCK // 2
HEADS_OWN = HEADS // SEQ
GROUP = HEADS_OWN * 3 * HEAD_DIM
MESH = pl.DeviceIdType.MESH
F32 = jnp.float32
BF16 = jnp.bfloat16
VMEM_LIMIT = 56 * 2**20


def causal_mask(key_start, key_count, query_count):
    key_pos = lax.broadcasted_iota(jnp.int32, (key_count, query_count), 0) + key_start
    query_pos = lax.broadcasted_iota(jnp.int32, (key_count, query_count), 1)
    return key_pos <= query_pos


def attend_head(read, write, block_count):
    for query_block in range(block_count):
        here = slice(query_block * BLOCK, (query_block + 1) * BLOCK)
        queries = (read(0, here).astype(F32) * 0.125).astype(BF16)
        peak = jnp.full((1, BLOCK), MASKED, F32)
        total = jnp.zeros((1, BLOCK), F32)
        accum = jnp.zeros((HEAD_DIM, BLOCK), F32)
        for key_block in range(query_block):
            there = slice(key_block * BLOCK, (key_block + 1) * BLOCK)
            logits = matmul(read(1, there).T, queries)
            new_peak = jnp.maximum(peak, jnp.max(logits, axis=0, keepdims=True))
            weights = jnp.exp(logits - new_peak)
            factor = jnp.exp(peak - new_peak)
            total = total * factor + jnp.sum(weights, axis=0, keepdims=True)
            accum = accum * factor + matmul(read(2, there), weights.astype(BF16))
            peak = new_peak
        keys = read(1, here).T
        values = read(2, here)
        logits = jnp.where(
            causal_mask(0, SPLIT, BLOCK), matmul(keys[:SPLIT], queries), MASKED
        )
        corner = jnp.where(
            causal_mask(0, SPLIT, SPLIT), matmul(keys[SPLIT:], queries[:, SPLIT:]), MASKED
        )
        new_peak = jnp.maximum(peak, jnp.max(logits, axis=0, keepdims=True))
        late_peak = jnp.maximum(new_peak[:, SPLIT:], jnp.max(corner, axis=0, keepdims=True))
        new_peak = jnp.concatenate([new_peak[:, :SPLIT], late_peak], axis=1)
        weights = jnp.exp(logits - new_peak)
        corner = jnp.exp(corner - late_peak)
        factor = jnp.exp(peak - new_peak)
        total = total * factor + jnp.sum(weights, axis=0, keepdims=True)
        accum = accum * factor + matmul(values[:, :SPLIT], weights.astype(BF16))
        corner_total = jnp.sum(corner, axis=0, keepdims=True)
        corner_accum = matmul(values[:, SPLIT:], corner.astype(BF16))
        total = jnp.concatenate([total[:, :SPLIT], total[:, SPLIT:] + corner_total], axis=1)
        accum = jnp.concatenate([accum[:, :SPLIT], accum[:, SPLIT:] + corner_accum], axis=1)
        write(query_block, here, accum / total, new_peak + jnp.log(total))


def norm_in(x, gain):
    average = jnp.mean(x, axis=-1, keepdims=True)
    centred = x - average
    inverse = lax.rsqrt(jnp.mean(centred * centred, axis=-1, keepdims=True) + EPSILON)
    return (centred * inverse * gain).astype(BF16)


def pack_kernel(slot_ref, x_ref, w_ref, gain_ref, a_ref, qkv_ref, o_ref, lse_ref, x_out, at):
    h = pl.program_id(0)

    @pl.when(h == 0)
    def _():
        x_out[...] = x_ref[0]
        a = norm_in(x_ref[0].astype(F32), gain_ref[:, 0:D])
        a_ref[...] = a
        at[...] = a.T
        for part in range(3):
            for k in range(0, D, 256):
                columns = slice(part * D + k, part * D + k + 256)
                qkv_ref[part, k : k + 256, :] = left_t(w_ref[:, columns], at[...]).astype(BF16)

    rows = pl.ds(pl.multiple_of(h * HEAD_DIM, HEAD_DIM), HEAD_DIM)

    def write(query_block, here, o, lse):
        o_ref[...] = o
        lse_ref[0:1, :] = lse

    attend_head(lambda part, columns: qkv_ref[part, rows, :], write, 1)


def pack_forward(slot, tokens, weight, gain):
    still = lambda *shape: pl.BlockSpec(shape, lambda h, slot: (0,) * len(shape))
    once = lambda *shape: pl.BlockSpec(
        shape, lambda h, slot: (0,) * len(shape), pipeline_mode=pl.Buffered(1)
    )
    by_head = lambda rows: pl.BlockSpec((rows, BLOCK), lambda h, slot: (h, 0))
    return pl.pallas_call(
        pack_kernel,
        grid_spec=pltpu.PrefetchScalarGridSpec(
            num_scalar_prefetch=1,
            grid=(HEADS,),
            in_specs=[
                pl.BlockSpec((1, BLOCK, D), lambda h, slot: (slot[0], 0, 0)),
                once(D, 3 * D),
                once(1, 3 * D + FF),
            ],
            out_specs=[still(BLOCK, D), still(3, D, BLOCK), by_head(HEAD_DIM), by_head(8)]
            + [still(BLOCK, D)],
            scratch_shapes=[pltpu.VMEM((D, BLOCK), BF16)],
        ),
        out_shape=[
            jax.ShapeDtypeStruct((BLOCK, D), BF16),
            jax.ShapeDtypeStruct((3, D, BLOCK), BF16),
            jax.ShapeDtypeStruct((D, BLOCK), F32),
            jax.ShapeDtypeStruct((HEADS * 8, BLOCK), F32),
            jax.ShapeDtypeStruct((BLOCK, D), BF16),
        ],
        compiler_params=pltpu.CompilerParams(vmem_limit_bytes=VMEM_LIMIT),
        cost_estimate=pl.CostEstimate(
            flops=8 * 10**9, bytes_accessed=10 * 2**20, transcendentals=HEADS * BLOCK * BLOCK
        ),
    )(slot, tokens, weight, gain)


def widened(gain, width):
    return jnp.concatenate([gain] * (width // 128), axis=1)


def column_stats(values):
    size = values.shape[0]
    average = jnp.sum(values, axis=0, keepdims=True) * (1.0 / size)
    centred = values - average
    spread = jnp.sum(centred * centred, axis=0, keepdims=True) * (1.0 / size)
    return average, lax.rsqrt(spread + EPSILON)


def gelu_both(values):
    t = 1.0 / (1.0 + (0.3275911 * 0.7071067811865476) * jnp.abs(values))
    density = jnp.exp(-0.5 * (values * values))
    tail = 0.5 * -1.453152027 + t * (0.5 * 1.061405429)
    tail = 0.5 * 1.421413741 + t * tail
    tail = 0.5 * -0.284496736 + t * tail
    tail = 0.5 * 0.254829592 + t * tail
    tail = tail * t * density
    below = jnp.where(values >= 0, 1.0 - tail, tail)
    return values * below, below + values * (density * 0.3989422804014327)


def feed_kernel(steps, chunk, sub, has_partial, slot, *refs):
    names = iter(refs)
    take = lambda count: [next(names) for _ in range(count)]
    o_in, x_in, dy_in, gain_ref, wo_in, wu_in, wd_in = take(7)
    part_in = take(3) if has_partial else []
    if has_partial:
        take(1)
    out_to, dh_to, do_to, go_to, gd_ref, gu_ref = take(6)
    o_ref, x_ref, dy_ref, wo, wu, wd, out_s, dh_s, do_s, go_s = take(10)
    ig, fg, hg, b_s, h_s, c_s, cn_s, dyt_s, n_s, slope_s, t_s, sum_s, dc_s, st = take(14)
    parts, part_o = take(2) if has_partial else (None, None)
    load_sem, wu_sem, wd_sem, part_sem, save_sem = take(5)
    width = BLOCK
    step = pl.program_id(0)
    o_load = pltpu.make_async_copy(o_in, o_ref, load_sem.at[0])
    wo_load = pltpu.make_async_copy(wo_in, wo, load_sem.at[1])
    x_load = pltpu.make_async_copy(x_in.at[slot[0]], x_ref, load_sem.at[2])
    dy_load = pltpu.make_async_copy(dy_in.at[slot[0]], dy_ref, load_sem.at[3])

    def span(k):
        return pl.ds(pl.multiple_of(k * chunk, chunk), chunk)

    def wu_load(k):
        return pltpu.make_async_copy(wu_in.at[:, span(k)], wu.at[:, span(k)], wu_sem.at[k])

    def wd_load(k):
        return pltpu.make_async_copy(wd_in.at[span(k), :], wd.at[span(k), :], wd_sem.at[k])

    def part_load(which, k):
        return pltpu.make_async_copy(
            part_in[which].at[span(k), :], parts.at[k], part_sem.at[which, k]
        )

    def save(k):
        source, target = [(out_s, out_to.at[slot[0]]), (dh_s, dh_to), (do_s, do_to), (go_s, go_to)][k]
        return pltpu.make_async_copy(source, target, save_sem.at[k])

    @pl.when(step == 0)
    def _():
        for load in (o_load, wo_load, x_load):
            load.start()
        ig[...] = jnp.broadcast_to(gain_ref[:, D : 2 * D], (128, D)).T
        fg[...] = jnp.broadcast_to(gain_ref[:, 2 * D : 3 * D], (128, D)).T
        hg[...] = jnp.broadcast_to(gain_ref[:, 3 * D :], (128, FF)).T
        o_load.wait()
        o = o_ref[...].astype(F32)
        average, inverse = column_stats(o)
        b = ((o - average) * inverse * widened(ig[...], width)).astype(BF16)
        b_s[...] = b
        st[0:1] = average
        st[1:2] = inverse
        wo_load.wait()
        x_load.wait()
        wu_load(0).start()
        dy_load.start()
        h = x_ref[...].T.astype(F32) + left_t(wo[...], b)
        h_s[...] = h
        average, inverse = column_stats(h)
        st[2:3] = average
        st[3:4] = inverse
        c = ((h - average) * inverse * widened(fg[...], width)).astype(BF16)
        c_s[...] = c
        cn_s[...] = c.T
        dy_load.wait()
        dyt_s[...] = dy_ref[...].T
        for k in range(1, steps):
            wu_load(k).start()
        for k in range(steps):
            wd_load(k).start()
        if has_partial:
            for k in range(steps):
                part_load(0, k).start()
            pltpu.make_async_copy(part_in[2], part_o, load_sem.at[4]).start()

    @pl.when(step < steps)
    def _():
        wu_load(step).wait()
        base = pl.multiple_of(step * chunk, chunk)
        for k in range(chunk // sub):
            u = left_t(wu[:, pl.ds(base + k * sub, sub)], c_s[...])
            z, slope = gelu_both(u)
            n_s[pl.ds(base + k * sub, sub), :] = z
            slope_s[pl.ds(base + k * sub, sub), :] = slope.astype(BF16)

    @pl.when(step == steps - 1)
    def _():
        total = jnp.zeros((1, width), F32)
        for k in range(FF // sub):
            total = total + jnp.sum(n_s[k * sub : (k + 1) * sub, :], axis=0, keepdims=True)
        average = total * (1.0 / FF)
        total = jnp.zeros((1, width), F32)
        for k in range(FF // sub):
            centred = n_s[k * sub : (k + 1) * sub, :] - average
            total = total + jnp.sum(centred * centred, axis=0, keepdims=True)
        st[4:5] = average
        st[5:6] = lax.rsqrt(total * (1.0 / FF) + EPSILON)
        st[6:8] = jnp.zeros((2, width), F32)
        sum_s[...] = h_s[...]

    @pl.when((step >= steps) & (step < 2 * steps))
    def _():
        turn = step - steps
        wd_load(turn).wait()
        if has_partial:
            part_load(0, turn).wait()
        base = pl.multiple_of(turn * chunk, chunk)
        average = st[4:5]
        inverse = st[5:6]
        first = jnp.zeros((1, width), F32)
        second = jnp.zeros((1, width), F32)
        pieces = []
        for k in range(chunk // sub):
            rows = slice(k * sub, (k + 1) * sub)
            here = pl.ds(base + k * sub, sub)
            n = (n_s[here, :] - average) * inverse
            n_s[here, :] = n
            gain = widened(hg[here, :], width)
            e = (n * gain).astype(BF16)
            pieces.append(e)
            t = matmul(wd[here, :], dyt_s[...]) * gain
            t_s[here, :] = t
            first = first + jnp.sum(t, axis=0, keepdims=True)
            second = second + jnp.sum(t * n, axis=0, keepdims=True)
            grad = matmul(e, dy_ref[...])
            if has_partial:
                grad = grad + parts[turn, rows, :].astype(F32)
            gd_ref[rows, :] = grad.astype(BF16)
        sum_s[...] += left_t(wd[pl.ds(base, chunk), :], jnp.concatenate(pieces, axis=0))
        st[6:7] += first
        st[7:8] += second
        if has_partial:
            part_load(1, turn).start()

    @pl.when(step == 2 * steps - 1)
    def _():
        out_s[...] = sum_s[...].astype(BF16).T
        save(0).start()
        st[6:8] = st[6:8] * (1.0 / FF)
        dc_s[...] = jnp.zeros_like(dc_s)

    @pl.when(step >= 2 * steps)
    def _():
        turn = step - 2 * steps
        if has_partial:
            part_load(1, turn).wait()
        base = pl.multiple_of(turn * chunk, chunk)
        inverse = st[5:6]
        first = st[6:7]
        second = st[7:8]
        pieces = []
        for k in range(chunk // sub):
            rows = slice(k * sub, (k + 1) * sub)
            here = pl.ds(base + k * sub, sub)
            n = n_s[here, :]
            du = ((t_s[here, :] - first - n * second) * inverse * slope_s[here, :].astype(F32)).astype(BF16)
            pieces.append(du)
            grad = matmul(du, cn_s[...])
            if has_partial:
                grad = grad + parts[turn, rows, :].astype(F32)
            gu_ref[rows, :] = grad.astype(BF16)
        dc_s[...] += matmul(wu[:, pl.ds(base, chunk)], jnp.concatenate(pieces, axis=0))

    @pl.when(step == 3 * steps - 1)
    def _():
        n = (h_s[...] - st[2:3]) * st[3:4]
        t = dc_s[...] * widened(fg[...], width)
        first = jnp.sum(t, axis=0, keepdims=True) * (1.0 / D)
        second = jnp.sum(t * n, axis=0, keepdims=True) * (1.0 / D)
        dh = dyt_s[...].astype(F32) + (t - first - n * second) * st[3:4]
        dh_s[...] = dh
        save(1).start()
        dh_low = dh.astype(BF16)
        n = (o_ref[...].astype(F32) - st[0:1]) * st[1:2]
        t = matmul(wo[...], dh_low) * widened(ig[...], width)
        first = jnp.sum(t, axis=0, keepdims=True) * (1.0 / D)
        second = jnp.sum(t * n, axis=0, keepdims=True) * (1.0 / D)
        do_s[...] = ((t - first - n * second) * st[1:2]).astype(BF16)
        save(2).start()
        grad = matmul(b_s[...], dh_low.T)
        if has_partial:
            pltpu.make_async_copy(part_in[2], part_o, load_sem.at[4]).wait()
            grad = grad + part_o[...].astype(F32)
        go_s[...] = grad.astype(BF16)
        save(3).start()
        for k in range(4):
            save(k).wait()


def feed_both(slot, o_t, tokens, cotangent, gains, weights, partial=None, output=None, chunk=1536, sub=256):
    width = BLOCK
    steps = FF // chunk
    has_partial = partial is not None
    anywhere = pl.BlockSpec(memory_space=pl.ANY)
    second = lambda i, slot: (jnp.clip(i - steps, 0, steps - 1), 0)
    third = lambda i, slot: (jnp.clip(i - 2 * steps, 0, steps - 1), 0)
    dma = pltpu.SemaphoreType.DMA
    scratch = [
        pltpu.VMEM((D, width), o_t.dtype),
        pltpu.VMEM((width, D), BF16),
        pltpu.VMEM((width, D), BF16),
        pltpu.VMEM((D, D), BF16),
        pltpu.VMEM((D, FF), BF16),
        pltpu.VMEM((FF, D), BF16),
        pltpu.VMEM((width, D), BF16),
        pltpu.VMEM((D, width), F32),
        pltpu.VMEM((D, width), BF16),
        pltpu.VMEM((D, D), BF16),
        pltpu.VMEM((D, 128), F32),
        pltpu.VMEM((D, 128), F32),
        pltpu.VMEM((FF, 128), F32),
        pltpu.VMEM((D, width), BF16),
        pltpu.VMEM((D, width), F32),
        pltpu.VMEM((D, width), BF16),
        pltpu.VMEM((width, D), BF16),
        pltpu.VMEM((D, width), BF16),
        pltpu.VMEM((FF, width), F32),
        pltpu.VMEM((FF, width), BF16),
        pltpu.VMEM((FF, width), F32),
        pltpu.VMEM((D, width), F32),
        pltpu.VMEM((D, width), F32),
        pltpu.VMEM((8, width), F32),
    ]
    args = [o_t, tokens, cotangent, gains, *weights]
    if has_partial:
        args += [*partial, output]
        scratch += [pltpu.VMEM((steps, chunk, D), BF16), pltpu.VMEM((D, D), BF16)]
    scratch += [dma((5,)), dma((steps,)), dma((steps,)), dma((2, steps)), dma((4,))]
    return pl.pallas_call(
        functools.partial(feed_kernel, steps, chunk, sub, has_partial),
        grid_spec=pltpu.PrefetchScalarGridSpec(
            num_scalar_prefetch=1,
            grid=(3 * steps,),
            in_specs=[anywhere] * 3
            + [pl.BlockSpec(gains.shape, lambda i, slot: (0, 0), pipeline_mode=pl.Buffered(1))]
            + [anywhere] * (len(args) - 4),
            out_specs=[anywhere] * 4
            + [pl.BlockSpec((chunk, D), second), pl.BlockSpec((chunk, D), third)],
            scratch_shapes=scratch,
        ),
        input_output_aliases={len(args): 0} if has_partial else {},
        out_shape=[
            jax.ShapeDtypeStruct((2, width, D), BF16),
            jax.ShapeDtypeStruct((D, width), F32),
            jax.ShapeDtypeStruct((D, width), BF16),
            jax.ShapeDtypeStruct((D, D), BF16),
            jax.ShapeDtypeStruct((FF, D), BF16),
            jax.ShapeDtypeStruct((FF, D), BF16),
        ],
        compiler_params=pltpu.CompilerParams(vmem_limit_bytes=62 * 2**20),
        cost_estimate=pl.CostEstimate(
            flops=6 * width * D * (D + 2 * FF), bytes_accessed=50 * 2**20, transcendentals=width * FF
        ),
    )(slot, *args)


def long_kernel(*refs):
    own_x, left, right, left_two, right_two, across, w_ref, gain_ref = refs[:8]
    qkv_ref, o_ref, lse_ref, do_ref, a_ref, x_ref, dh_ref = refs[8:15]
    a_out, qkv_out, o_out, lse_out, mine_out, gq_out, dx_out = refs[15:22]
    a_all, qkv, o_own, lse_own, o_low, w, qp, op, lp, dop, ap, xp, dhp, dp, gq, dx = refs[22:38]
    x_all, w_near, w_own, load_sem, save_sem, swap_send, swap_recv = refs[38:]
    gain_row = gain_ref[:, 0:D]
    r = lax.axis_index("rows")
    s = lax.axis_index("seq")
    shifted = [(r, (s + shift) % SEQ) for shift in range(SEQ)]
    barrier = pltpu.get_barrier_semaphore()
    for device in shifted[1:]:
        pl.semaphore_signal(barrier, inc=1, device_id=device, device_id_type=MESH)
    pl.semaphore_wait(barrier, SEQ - 1)
    sources = [qkv_ref, o_ref, lse_ref, do_ref, a_ref, x_ref, dh_ref, w_ref]
    targets = [qp, op, lp, dop, ap, xp, dhp, w]
    loads = [
        pltpu.make_async_copy(source, target, load_sem.at[k])
        for k, (source, target) in enumerate(zip(sources, targets))
    ]
    nears = [
        pltpu.make_async_copy(
            w_ref.at[:, pl.ds(pl.multiple_of(part * D + (3 * s // 2) * 128, 128), 256)],
            w_near.at[part],
            load_sem.at[8 + part],
        )
        for part in range(3)
    ]
    x_from = [
        [own_x, right, right_two, across],
        [left, own_x, right, right_two],
        [left_two, left, own_x, right],
        [across, left_two, left, own_x],
    ]

    def x_load(k, j):
        return pltpu.make_async_copy(x_from[k][j], x_all.at[j], load_sem.at[11 + j])

    for k in range(SEQ):

        @pl.when(s == k)
        def _():
            for j in range(SEQ):
                x_load(k, j).start()

    for load in nears + loads:
        load.start()
    saves = [
        pltpu.make_async_copy(source, target, save_sem.at[k])
        for k, (source, target) in enumerate(
            [(a_all, a_out), (qkv, qkv_out), (o_own, o_out), (lse_own, lse_out)]
            + [(gq, gq_out), (dx, dx_out)]
        )
    ]

    def o_copy(h, shift):
        part = o_low.at[(s + shift) % SEQ, pl.ds(h * HEAD_DIM, HEAD_DIM), :]
        place = pl.ds(pl.multiple_of(s * (HEADS_OWN * HEAD_DIM) + h * HEAD_DIM, 16), HEAD_DIM)
        target = mine_out.at[place, :]
        if shift == 0:
            return pltpu.make_async_copy(part, target, save_sem.at[6 + h])
        return pltpu.make_async_remote_copy(
            src_ref=part,
            dst_ref=target,
            send_sem=swap_send.at[h, shift],
            recv_sem=swap_recv.at[h, shift],
            device_id=shifted[shift],
            device_id_type=MESH,
        )

    for part in range(3):
        nears[part].wait()

        @pl.when(s % 2 == 0)
        def _():
            w_own[part] = w_near[part, :, 0:192]

        @pl.when(s % 2 == 1)
        def _():
            w_own[part] = w_near[part, :, 64:256]

    for j in range(SEQ):
        start = j * BLOCK
        x_load(0, j).wait()
        a = norm_in(x_all[j].astype(F32), gain_row)
        a_all[start : start + BLOCK, :] = a
        a_t = a.T
        for part in range(3):
            qkv[part, :, start : start + BLOCK] = left_t(w_own[part], a_t).astype(BF16)
    saves[0].start()
    saves[1].start()
    for h in range(HEADS_OWN):
        rows = slice(h * HEAD_DIM, (h + 1) * HEAD_DIM)

        def write(query_block, here, o, lse):
            o_own[rows, here] = o
            lse_own[h, 0:1, here] = lse
            o_low[query_block, rows, :] = o.astype(BF16)

        attend_head(lambda part, columns: qkv[part, rows, columns], write, SEQ)
        for shift in range(SEQ):
            o_copy(h, shift).start()
    saves[2].start()
    saves[3].start()
    for load in loads:
        load.wait()

    def back(h, carry):
        rows = pl.ds(pl.multiple_of(h * HEAD_DIM, HEAD_DIM), HEAD_DIM)
        queries_t = (qp[0, rows, :].astype(F32) * 0.125).astype(BF16)
        keys_t = qp[1, rows, :]
        do_t = dop[rows, :]
        lse = lp[pl.ds(pl.multiple_of(h * 8, 8), 8), :][0:1]
        delta = jnp.sum(do_t.astype(F32) * op[rows, :], axis=0, keepdims=True)
        keys = keys_t.T
        values = qp[2, rows, :].T
        queries = queries_t.T
        do_rows = do_t.T
        probs = jnp.exp(matmul(keys[:SPLIT], queries_t) - lse)
        probs = jnp.where(causal_mask(0, SPLIT, BLOCK), probs, 0.0)
        dprobs = matmul(values[:SPLIT], do_t)
        dlogits = (probs * (dprobs - delta)).astype(BF16)
        late = slice(SPLIT, BLOCK)
        corner = jnp.exp(matmul(keys[SPLIT:], queries_t[:, late]) - lse[:, late])
        corner = jnp.where(causal_mask(0, SPLIT, SPLIT), corner, 0.0)
        dcorner = matmul(values[SPLIT:], do_t[:, late])
        dcorner = (corner * (dcorner - delta[:, late])).astype(BF16)
        dq = matmul(keys_t[:, :SPLIT], dlogits)
        dq_late = dq[:, late] + matmul(keys_t[:, late], dcorner)
        dp[0, rows, :SPLIT] = (dq[:, :SPLIT] * 0.125).astype(BF16)
        dp[0, rows, late] = (dq_late * 0.125).astype(BF16)
        dp[1, rows, :SPLIT] = matmul(dlogits, queries).T.astype(BF16)
        dp[1, rows, late] = matmul(dcorner, queries[late]).T.astype(BF16)
        dp[2, rows, :SPLIT] = matmul(probs.astype(BF16), do_rows).T.astype(BF16)
        dp[2, rows, late] = matmul(corner.astype(BF16), do_rows[late]).T.astype(BF16)
        return carry

    lax.fori_loop(0, HEADS, back, 0)
    for part in range(3):
        gq[part * D : (part + 1) * D, :] = matmul(dp[part], ap[...]).astype(BF16)
    saves[4].start()
    dx[...] = first_norm_back(xp[...], dhp[...], w, dp, gain_row)
    saves[5].start()
    for save in saves:
        save.wait()
    for h in range(HEADS_OWN):
        for shift in range(SEQ):
            o_copy(h, shift).wait()


def first_norm_back(x, dh_t, w, dqkv, gain):
    x_t = x.T.astype(F32)
    average, inverse = column_stats(x_t)
    n = (x_t - average) * inverse
    t = matmul(w[:, 0:D], dqkv[0])
    for part in range(1, 3):
        t = t + matmul(w[:, part * D : (part + 1) * D], dqkv[part])
    t = t * widened(jnp.broadcast_to(gain, (128, D)).T, BLOCK)
    first = jnp.sum(t, axis=0, keepdims=True) * (1.0 / D)
    second = jnp.sum(t * n, axis=0, keepdims=True) * (1.0 / D)
    return (dh_t + (t - first - n * second) * inverse).astype(BF16).T


def long_forward(x_blocks, weight, gains, pack, collective_id):
    own_rows = HEADS_OWN * HEAD_DIM
    length = SEQ * BLOCK
    dma = pltpu.SemaphoreType.DMA
    anywhere = pl.BlockSpec(memory_space=pl.ANY)
    resident = pl.BlockSpec(memory_space=pltpu.VMEM)
    return pl.pallas_call(
        long_kernel,
        in_specs=[anywhere] * 7 + [resident] + [anywhere] * 7,
        out_specs=[anywhere] * 7,
        out_shape=[
            jax.ShapeDtypeStruct((length, D), BF16),
            jax.ShapeDtypeStruct((3, own_rows, length), BF16),
            jax.ShapeDtypeStruct((own_rows, length), F32),
            jax.ShapeDtypeStruct((HEADS_OWN, 8, length), F32),
            jax.ShapeDtypeStruct((D, BLOCK), BF16),
            jax.ShapeDtypeStruct((3 * D, D), BF16),
            jax.ShapeDtypeStruct((BLOCK, D), BF16),
        ],
        scratch_shapes=[
            pltpu.VMEM((length, D), BF16),
            pltpu.VMEM((3, own_rows, length), BF16),
            pltpu.VMEM((own_rows, length), F32),
            pltpu.VMEM((HEADS_OWN, 8, length), F32),
            pltpu.VMEM((SEQ, own_rows, BLOCK), BF16),
            pltpu.VMEM((D, 3 * D), BF16),
            pltpu.VMEM((3, D, BLOCK), BF16),
            pltpu.VMEM((D, BLOCK), F32),
            pltpu.VMEM((HEADS * 8, BLOCK), F32),
            pltpu.VMEM((D, BLOCK), BF16),
            pltpu.VMEM((BLOCK, D), BF16),
            pltpu.VMEM((BLOCK, D), BF16),
            pltpu.VMEM((D, BLOCK), F32),
            pltpu.VMEM((3, D, BLOCK), BF16),
            pltpu.VMEM((3 * D, D), BF16),
            pltpu.VMEM((BLOCK, D), BF16),
            pltpu.VMEM((SEQ, BLOCK, D), BF16),
            pltpu.VMEM((3, D, 256), BF16),
            pltpu.VMEM((3, D, own_rows), BF16),
            dma((11 + SEQ,)),
            dma((6 + HEADS_OWN,)),
            dma((HEADS_OWN, SEQ)),
            dma((HEADS_OWN, SEQ)),
        ],
        compiler_params=pltpu.CompilerParams(
            collective_id=collective_id, has_side_effects=True, vmem_limit_bytes=VMEM_LIMIT
        ),
        cost_estimate=pl.CostEstimate(
            flops=20 * 10**9, bytes_accessed=40 * 2**20, transcendentals=10**7
        ),
    )(*x_blocks, weight, gains, *pack)


PIECE = 768
HALF = PIECE // 2
COLS = D // 2
FEED_PIECES = (2 * FF + D) // PIECE
QKV_PIECES = 3 * D // PIECE
PIECES = FEED_PIECES + QKV_PIECES
ATTEND_TICK = 2
QKV_TICK = 5
BACK_TICK = 3
BACKS = 1
DX_TICK = 13


def sum_kernel(*refs):
    gd, gu, go, gq, do_ref, qkv_ref, o_ref, lse_ref, a_ref, gain_ref = refs[:10]
    x_ref, dh_ref, wd_ref, wu_ref, wo_ref, wq_ref, total_ref, dx_ref, sums_ref = refs[10:19]
    own, r0, r1, r2, r3, r4, fin, qkv, o_own, lse_own, a_all, gq_own, do_own, d_own = refs[19:33]
    dk_acc, dv_acc, back_ref, x_own, dh_own, wq, dx, grads, factors, sums = refs[33:43]
    own_sem, send_sem, recv_sem, fin_sem, in_sem, swap_send, swap_recv, gain_sem = refs[43:]
    r = lax.axis_index("rows")
    s = lax.axis_index("seq")
    core, xb, yb = r % 2, (r // 2) % 2, r // 4
    inside = (s == 1) | (s == 2)
    outside = (s == 0) | (s == 3)
    to_core = (r + 1 - 2 * core, s)
    to_x = (r + 2 - 4 * xb, s)
    to_y = (r + 4 - 8 * yb, s)
    to_pair = (r, s + 1 - 2 * (s % 2))
    to_middle = (r, 3 - s)
    shifted = [(r, (s + shift) % SEQ) for shift in range(SEQ)]
    barrier = pltpu.get_barrier_semaphore()
    for device in (to_core, to_x, to_y, *shifted[1:]):
        pl.semaphore_signal(barrier, inc=1, device_id=device, device_id_type=MESH)
    pl.semaphore_wait(barrier, 6)
    bits = [(xb, yb), (yb, xb)]
    partners = [(to_x, to_y), (to_y, to_x)]

    def rows_at(start, count):
        return pl.ds(pl.multiple_of(start, 16), count)

    def remote(source, target, send, recv, device):
        return pltpu.make_async_remote_copy(
            src_ref=source,
            dst_ref=target,
            send_sem=send,
            recv_sem=recv,
            device_id=device,
            device_id_type=MESH,
        )

    def numbered(source, target, kind, p, device):
        return remote(source, target, send_sem.at[kind, p], recv_sem.at[kind, p], device)

    def columns(o):
        return slice(o * COLS, (o + 1) * COLS)

    def base(o):
        return bits[o][0] * 192 + bits[o][1] * 96

    def core_copy(ref, q, p):
        part = ref.at[rows_at(q * PIECE + (1 - core) * HALF, HALF), :]
        return numbered(part, r0.at[p], 0, p, to_core)

    def own_copy(ref, q, p):
        part = ref.at[rows_at(q * PIECE + core * HALF, HALF), :]
        return pltpu.make_async_copy(part, own.at[p], own_sem.at[p])

    def first_copy(p, o):
        part = own.at[p, rows_at((1 - bits[o][0]) * 192, 192), columns(o)]
        return numbered(part, r1.at[p, o], 1 + o, p, partners[o][0])

    def second_copy(p, o):
        part = own.at[p, rows_at(bits[o][0] * 192 + (1 - bits[o][1]) * 96, 96), columns(o)]
        return numbered(part, r2.at[p, o], 3 + o, p, partners[o][1])

    def pair_copy(p, o):
        part = own.at[p, rows_at(base(o), 96), columns(o)]
        return numbered(part, r3.at[p, o], 5 + o, p, to_pair)

    def middle_copy(p, o):
        part = own.at[p, rows_at(base(o), 96), columns(o)]
        return numbered(part, r4.at[p, o], 7 + o, p, to_middle)

    def region(p, start, count, o):
        return total_ref.at[rows_at(p * PIECE + core * HALF + start, count), columns(o)]

    def fin_copy(p, o):
        return pltpu.make_async_copy(fin.at[p, o], region(p, base(o), 96, o), fin_sem.at[o, p])

    def pair_back(p, o):
        return numbered(fin.at[p, o], region(p, base(o), 96, o), 9 + o, p, to_pair)

    def second_back(p, o):
        part = region(p, base(o), 96, o)
        return numbered(part, part, 11 + o, p, partners[o][1])

    def first_back(p, o):
        part = region(p, bits[o][0] * 192, 192, o)
        return numbered(part, part, 13 + o, p, partners[o][0])

    def core_back(p):
        part = total_ref.at[rows_at(p * PIECE + core * HALF, HALF), :]
        return numbered(part, part, 15, p, to_core)

    def do_copy(shift):
        part = do_ref.at[(s + shift) % SEQ]
        if shift == 0:
            return pltpu.make_async_copy(part, do_own.at[s], in_sem.at[5])
        return remote(
            part, do_own.at[s], swap_send.at[0, shift], swap_recv.at[0, shift], shifted[shift]
        )

    def back_copy(h, shift):
        part = d_own.at[(s + shift) % SEQ, :, rows_at(h * HEAD_DIM, HEAD_DIM), :]
        target = back_ref.at[
            :, rows_at(s * (HEADS_OWN * HEAD_DIM) + h * HEAD_DIM, HEAD_DIM), :
        ]
        if shift == 0:
            return pltpu.make_async_copy(part, target, in_sem.at[6 + h])
        return remote(
            part, target, swap_send.at[1 + h, shift], swap_recv.at[1 + h, shift], shifted[shift]
        )

    loads = [
        pltpu.make_async_copy(qkv_ref, qkv, in_sem.at[0]),
        pltpu.make_async_copy(o_ref, o_own, in_sem.at[1]),
        pltpu.make_async_copy(lse_ref, lse_own, in_sem.at[2]),
        pltpu.make_async_copy(a_ref, a_all, in_sem.at[3]),
        pltpu.make_async_copy(gq, gq_own, in_sem.at[4]),
    ]
    late = [
        pltpu.make_async_copy(x_ref, x_own, in_sem.at[6 + HEADS_OWN]),
        pltpu.make_async_copy(dh_ref, dh_own, in_sem.at[7 + HEADS_OWN]),
        pltpu.make_async_copy(wq_ref, wq, in_sem.at[8 + HEADS_OWN]),
    ]
    dx_save = pltpu.make_async_copy(dx, dx_ref, in_sem.at[9 + HEADS_OWN])
    sums_save = pltpu.make_async_copy(sums, sums_ref, in_sem.at[10 + HEADS_OWN])
    for shift in range(1, SEQ):
        do_copy(shift).start()
    offset = 0
    for ref in (gd, gu, go):

        def begin(q, carry, ref=ref, offset=offset):
            core_copy(ref, q, q + offset).start()
            own_copy(ref, q, q + offset).start()
            return carry

        lax.fori_loop(0, ref.shape[0] // PIECE, begin, 0)
        offset += ref.shape[0] // PIECE
    do_copy(0).start()
    for load in loads:
        load.start()

    def added(index, other):
        own[index] = (own[index].astype(F32) + other.astype(F32)).astype(BF16)

    def after_core(p):
        own_copy(gd, 0, p).wait()
        core_copy(gd, 0, p).wait()
        own[p] = (own[p].astype(F32) + r0[p].astype(F32)).astype(BF16)
        for o in range(2):
            first_copy(p, o).start()

    def after_first(p):
        for o in range(2):
            first_copy(p, o).wait()
            added((p, rows_at(bits[o][0] * 192, 192), columns(o)), r1[p, o])
            second_copy(p, o).start()

    def after_second(p):
        for o in range(2):
            second_copy(p, o).wait()
            added((p, rows_at(base(o), 96), columns(o)), r2[p, o])

            @pl.when(outside)
            def _():
                pair_copy(p, o).start()

    def after_pair(p):
        for o in range(2):

            @pl.when(outside)
            def _():
                pair_copy(p, o).wait_send()

            @pl.when(inside)
            def _():
                pair_copy(p, o).wait_recv()
                added((p, rows_at(base(o), 96), columns(o)), r3[p, o])
                middle_copy(p, o).start()

    def after_middle(p):
        for o in range(2):

            @pl.when(inside)
            def _():
                middle_copy(p, o).wait()
                mine = own[p, rows_at(base(o), 96), columns(o)].astype(F32)
                fin[p, o] = (mine + r4[p, o].astype(F32)).astype(BF16)
                pair_back(p, o).start()
                fin_copy(p, o).start()

    def after_pair_back(p):
        for o in range(2):

            @pl.when(inside)
            def _():
                fin_copy(p, o).wait()
                pair_back(p, o).wait_send()

            @pl.when(outside)
            def _():
                pair_back(p, o).wait_recv()

            second_back(p, o).start()

    def after_second_back(p):
        for o in range(2):
            second_back(p, o).wait()
            first_back(p, o).start()

    def after_first_back(p):
        for o in range(2):
            first_back(p, o).wait()
        core_back(p).start()

    def after_core_back(p):
        core_back(p).wait()

    stages = [
        after_core,
        after_first,
        after_second,
        after_pair,
        after_middle,
        after_pair_back,
        after_second_back,
        after_first_back,
    ]

    def square(ref, p):
        return ref.at[rows_at(p * PIECE, PIECE), :]

    def grad_load(p):
        return pltpu.make_async_copy(square(total_ref, p), grads.at[p % 2], gain_sem.at[0, p % 2])

    def factor_load(ref, p):
        return pltpu.make_async_copy(ref, factors.at[p % 2], gain_sem.at[1, p % 2])

    def fetch(p):
        grad_load(p).start()

        @pl.when(p < 4)
        def _():
            factor_load(square(wd_ref, p), p).start()

        @pl.when((p >= 4) & (p < 8))
        def _():
            columns = pl.ds(pl.multiple_of((p - 4) * PIECE, PIECE), PIECE)
            factor_load(wu_ref.at[:, columns], p).start()

        @pl.when(p == 8)
        def _():
            factor_load(wo_ref, p).start()

    def row_sums(values):
        folded = values[:, 0:128]
        for k in range(1, D // 128):
            folded = folded + values[:, k * 128 : (k + 1) * 128]
        return jnp.sum(folded.T, axis=0, keepdims=True)

    def weigh(p):
        grad_load(p).wait()
        factor_load(wo_ref, p).wait()
        grad = grads[p % 2].astype(F32)

        @pl.when(p < 4)
        def _():
            place = pl.ds(pl.multiple_of(p * PIECE, PIECE), PIECE)
            sums[0:1, place] = row_sums(grad * factors[p % 2].astype(F32))

        @pl.when((p >= 4) & (p < 8))
        def _():
            term = jnp.sum(grad * factors[p % 2].T.astype(F32), axis=0, keepdims=True)
            sums[1:2, 0:D] = jnp.where(p == 4, 0.0, sums[1:2, 0:D]) + term

        @pl.when(p == 8)
        def _():
            sums[2:3, 0:D] = row_sums(grad * factors[p % 2].astype(F32))

    def head_rows(h):
        return rows_at(h * HEAD_DIM, HEAD_DIM)

    def attend(h, query_block):
        rows = head_rows(h)
        here = slice(query_block * BLOCK, (query_block + 1) * BLOCK)
        queries_t = (qkv[0, rows, here].astype(F32) * 0.125).astype(BF16)
        queries = queries_t.T
        do_t = do_own[query_block, rows, :]
        do_rows = do_t.T
        lse = lse_own[h, 0:1, here]
        delta = jnp.sum(do_t.astype(F32) * o_own[rows, here], axis=0, keepdims=True)
        dq = jnp.zeros((HEAD_DIM, BLOCK), F32)
        for key_block in range(query_block + 1):
            there = slice(key_block * BLOCK, (key_block + 1) * BLOCK)
            keys_t = qkv[1, rows, there]
            probs = jnp.exp(matmul(keys_t.T, queries_t) - lse)
            if key_block == query_block:
                probs = jnp.where(causal_mask(0, BLOCK, BLOCK), probs, 0.0)
            dprobs = matmul(qkv[2, rows, there].T, do_t)
            dlogits = (probs * (dprobs - delta)).astype(BF16)
            dq = dq + matmul(keys_t, dlogits)
            dv_acc[there, :] += matmul(probs.astype(BF16), do_rows)
            dk_acc[there, :] += matmul(dlogits, queries)
        d_own[query_block, 0, rows, :] = (dq * 0.125).astype(BF16)

    def finish_head(h):
        rows = head_rows(h)
        total = jnp.zeros((3 * HEAD_DIM, D), F32)
        for block in range(SEQ):
            here = slice(block * BLOCK, (block + 1) * BLOCK)
            d_own[block, 1, rows, :] = dk_acc[here, :].T.astype(BF16)
            d_own[block, 2, rows, :] = dv_acc[here, :].T.astype(BF16)
            joined = d_own[block, :, rows, :].reshape(3 * HEAD_DIM, BLOCK)
            total = total + matmul(joined, a_all[here, :])
        for part in range(3):
            place = rows_at(part * D + s * (HEADS_OWN * HEAD_DIM) + h * HEAD_DIM, HEAD_DIM)
            term = total[part * HEAD_DIM : (part + 1) * HEAD_DIM, :]
            gq_own[place, :] = (gq_own[place, :].astype(F32) + term).astype(BF16)
        back_copy(h, 0).start()

    def tick(t, carry):
        for lag, stage in enumerate(stages):
            for sub in range(2):
                p = 2 * (t - lag) + sub

                @pl.when((p >= 0) & (p < FEED_PIECES))
                def _():
                    stage(p)

                q = 2 * (t - lag - QKV_TICK) + sub

                @pl.when((q >= 0) & (q < QKV_PIECES))
                def _():
                    stage(FEED_PIECES + q)

        @pl.when(t == ATTEND_TICK)
        def _():
            for load in loads:
                load.wait()
            for load in late:
                load.start()
            for shift in range(SEQ):
                do_copy(shift).wait()

        h = t - ATTEND_TICK

        @pl.when((h >= 0) & (h < HEADS_OWN))
        def _():
            dk_acc[...] = jnp.zeros_like(dk_acc)
            dv_acc[...] = jnp.zeros_like(dv_acc)
            for query_block in range(SEQ):
                attend(h, query_block)
            finish_head(h)

        @pl.when(h == HEADS_OWN - 1)
        def _():
            for q in range(QKV_PIECES):
                core_copy(gq_own, q, FEED_PIECES + q).start()
                own_copy(gq_own, q, FEED_PIECES + q).start()

        for unit in range(3 * HEADS_OWN):

            @pl.when(t == BACK_TICK + unit // BACKS)
            def _():
                back_copy(unit // 3, unit % 3 + 1).start()

        for sub in range(2):
            p = 2 * (t - len(stages) - 1) + sub

            @pl.when((p >= 0) & (p < FEED_PIECES))
            def _():
                weigh(p)

        for sub in range(2):
            p = 2 * (t - len(stages)) + sub

            @pl.when((p >= 0) & (p < FEED_PIECES))
            def _():
                after_core_back(p)
                fetch(p)

            q = p - 2 * QKV_TICK

            @pl.when((q >= 0) & (q < QKV_PIECES))
            def _():
                after_core_back(FEED_PIECES + q)

        @pl.when(t == DX_TICK)
        def _():
            for load in late:
                load.wait()
            for h in range(HEADS_OWN):
                for shift in range(SEQ):
                    back_copy(h, shift).wait()
            dx[...] = first_norm_back(x_own[...], dh_own[...], wq, back_ref, gain_ref[:, 0:D])
            dx_save.start()

        return carry

    last = QKV_TICK + (QKV_PIECES - 1) // 2 + len(stages) + 1
    lax.fori_loop(0, last, tick, 0)
    sums_save.start()
    dx_save.wait()
    sums_save.wait()


def summed_everywhere(*args, collective_id):
    n = PIECES
    length = SEQ * BLOCK
    own_rows = HEADS_OWN * HEAD_DIM
    dma = pltpu.SemaphoreType.DMA
    anywhere = pl.BlockSpec(memory_space=pl.ANY)
    return pl.pallas_call(
        sum_kernel,
        out_shape=[
            jax.ShapeDtypeStruct((n * PIECE, D), BF16),
            jax.ShapeDtypeStruct((BLOCK, D), BF16),
            jax.ShapeDtypeStruct((8, FF), F32),
        ],
        in_specs=[anywhere] * 9 + [pl.BlockSpec(memory_space=pltpu.VMEM)] + [anywhere] * 6,
        out_specs=[anywhere] * 3,
        scratch_shapes=[
            pltpu.VMEM((n, HALF, D), BF16),
            pltpu.VMEM((n, HALF, D), BF16),
            pltpu.VMEM((n, 2, 192, COLS), BF16),
            pltpu.VMEM((n, 2, 96, COLS), BF16),
            pltpu.VMEM((n, 2, 96, COLS), BF16),
            pltpu.VMEM((n, 2, 96, COLS), BF16),
            pltpu.VMEM((n, 2, 96, COLS), BF16),
            pltpu.VMEM((3, own_rows, length), BF16),
            pltpu.VMEM((own_rows, length), F32),
            pltpu.VMEM((HEADS_OWN, 8, length), F32),
            pltpu.VMEM((length, D), BF16),
            pltpu.VMEM((3 * D, D), BF16),
            pltpu.VMEM((SEQ, own_rows, BLOCK), BF16),
            pltpu.VMEM((SEQ, 3, own_rows, BLOCK), BF16),
            pltpu.VMEM((length, HEAD_DIM), F32),
            pltpu.VMEM((length, HEAD_DIM), F32),
            pltpu.VMEM((3, D, BLOCK), BF16),
            pltpu.VMEM((BLOCK, D), BF16),
            pltpu.VMEM((D, BLOCK), F32),
            pltpu.VMEM((D, 3 * D), BF16),
            pltpu.VMEM((BLOCK, D), BF16),
            pltpu.VMEM((2, PIECE, D), BF16),
            pltpu.VMEM((2, PIECE, D), BF16),
            pltpu.VMEM((8, FF), F32),
            dma((n,)),
            dma((16, n)),
            dma((16, n)),
            dma((2, n)),
            dma((11 + HEADS_OWN,)),
            dma((1 + HEADS_OWN, SEQ)),
            dma((1 + HEADS_OWN, SEQ)),
            dma((2, 2)),
        ],
        compiler_params=pltpu.CompilerParams(
            collective_id=collective_id, has_side_effects=True, vmem_limit_bytes=60 * 2**20
        ),
        cost_estimate=pl.CostEstimate(flops=0, bytes_accessed=n * PIECE * D * 64, transcendentals=0),
    )(*args)


def sent(value, *pairs):
    return lax.ppermute(value, "seq", pairs)


def finish_kernel(slots, total, wq, gain_ref, sums, dx_long, dx_pack, *refs):
    gd, gu, go, gq, si, sf, sh, sa, grad_out, acc, dx, load_sem, copy_sem = refs
    step = pl.program_id(0)
    loads = [
        pltpu.make_async_copy(source, dx.at[k], load_sem.at[k])
        for k, source in enumerate((dx_long, dx_pack))
    ]
    copies = [
        pltpu.make_async_copy(dx.at[k], grad_out.at[slots[k]], copy_sem.at[k]) for k in range(2)
    ]

    @pl.when(step == 0)
    def _():
        for load in loads:
            load.start()
        si[...] = (sums[2:3, 0:D] / gain_ref[:, D : 2 * D])[0]
        sf[...] = (sums[1:2, 0:D] / gain_ref[:, 2 * D : 3 * D])[0]
        sh[...] = (sums[0:1, :] / gain_ref[:, 3 * D :])[0]

    @pl.when(step == 2)
    def _():
        for load, copy in zip(loads, copies):
            load.wait()
            copy.start()

    @pl.when(step < 4)
    def _():
        gd[...] = total[...].astype(F32)

    @pl.when((step >= 4) & (step < 8))
    def _():
        gu[...] = total[...].T.astype(F32)

    @pl.when(step == 8)
    def _():
        go[...] = total[...].astype(F32)

    @pl.when(step >= 9)
    def _():
        grad = total[...].T.astype(F32)
        gq[...] = grad
        product = grad * wq[...].astype(F32)
        folded = product[:, 0:128]
        for k in range(1, D // 128):
            folded = folded + product[:, k * 128 : (k + 1) * 128]
        acc[...] = folded + jnp.where(step == 9, 0.0, acc[...])

    @pl.when(step == 11)
    def _():
        sa[...] = (jnp.sum(acc[...].T, axis=0, keepdims=True) / gain_ref[:, 0:D])[0]
        for copy in copies:
            copy.wait()


def finished(slots, total, weight, gains, sums, dx_long, dx_pack):
    square = lambda index: pl.BlockSpec((D, D), index)
    at_down = lambda i, slots: (jnp.clip(i, 0, 3), 0)
    at_up = lambda i, slots: (0, jnp.clip(i - 4, 0, 3))
    at_qkv = lambda i, slots: (0, jnp.clip(i - 9, 0, 2))
    still = lambda i, slots: (0, 0)
    once = lambda *shape: pl.BlockSpec(shape, still, pipeline_mode=pl.Buffered(1))
    row = lambda size: pl.BlockSpec((size,), lambda i, slots: (0,))
    anywhere = pl.BlockSpec(memory_space=pl.ANY)
    shapes = [(FF, D), (D, FF), (D, D), (D, 3 * D), (D,), (D,), (FF,), (D,)]
    dma = pltpu.SemaphoreType.DMA
    return pl.pallas_call(
        finish_kernel,
        grid_spec=pltpu.PrefetchScalarGridSpec(
            num_scalar_prefetch=1,
            grid=(PIECES,),
            in_specs=[square(lambda i, slots: (i, 0)), square(at_qkv)]
            + [once(1, 3 * D + FF), once(8, FF)]
            + [anywhere] * 2,
            out_specs=[square(at_down), square(at_up), square(still), square(at_qkv)]
            + [row(D), row(D), row(FF), row(D)]
            + [anywhere],
            scratch_shapes=[
                pltpu.VMEM((D, 128), F32),
                pltpu.VMEM((2, BLOCK, D), BF16),
                dma((2,)),
                dma((2,)),
            ],
        ),
        out_shape=[jax.ShapeDtypeStruct(shape, F32) for shape in shapes]
        + [jax.ShapeDtypeStruct((2, BLOCK, D), BF16)],
        compiler_params=pltpu.CompilerParams(vmem_limit_bytes=VMEM_LIMIT),
        cost_estimate=pl.CostEstimate(
            flops=2 * 10**7, bytes_accessed=46 * 2**20, transcendentals=0
        ),
    )(slots, total, weight, gains, sums, dx_long, dx_pack)


def split_layer(
    tokens,
    segment_ids,
    cotangent,
    query_key_value,
    out_weight,
    up_weight,
    down_weight,
    attend_gain,
    inner_gain,
    feed_gain,
    hidden_gain,
):
    long_first = segment_ids[0, -1] == 0
    x_long = jnp.where(long_first, tokens[0], tokens[1])
    left = sent(x_long, (0, 1), (1, 2), (2, 3))
    right = sent(x_long, (1, 0), (2, 1), (3, 2))
    long_slot = jnp.where(long_first, 0, 1).astype(jnp.int32)
    slots = jnp.stack([long_slot, 1 - long_slot])
    gains = jnp.concatenate([attend_gain, inner_gain, feed_gain, hidden_gain])[None]
    weights = (out_weight, up_weight, down_weight)
    a_pack, qkv_pack, o_pack, lse_pack, x_pack = pack_forward(
        slots[1:], tokens, query_key_value, gains
    )
    o_pack, left, right = lax.optimization_barrier((o_pack, left, right))
    left_two = sent(left, (1, 2), (2, 3))
    right_two = sent(right, (1, 0), (2, 1))
    across = sent(jnp.where(lax.axis_index("seq") == 1, left, right), (1, 3), (2, 0))
    output, dh_pack, do_pack, go_pack, gd_pack, gu_pack = feed_both(
        slots[1:], o_pack, tokens, cotangent, gains, weights
    )
    *x_far, do_pack = lax.optimization_barrier((left_two, right_two, across, do_pack))
    a_all, qkv_long, o_long, lse_long, o_mine, gq_pack, dx_pack = long_forward(
        (x_long, left, right, *x_far),
        query_key_value,
        gains,
        (qkv_pack, o_pack, lse_pack, do_pack, a_pack, x_pack, dh_pack),
        1,
    )
    output, dh_long, do_long, go, gd, gu = feed_both(
        slots[:1],
        o_mine,
        tokens,
        cotangent,
        gains,
        weights,
        (gd_pack, gu_pack, go_pack),
        output,
    )
    total, dx_long, sums = summed_everywhere(
        gd,
        gu,
        go,
        gq_pack,
        do_long.reshape(SEQ, HEADS_OWN * HEAD_DIM, BLOCK),
        qkv_long,
        o_long,
        lse_long,
        a_all,
        gains,
        x_long,
        dh_long,
        down_weight,
        up_weight,
        out_weight,
        query_key_value,
        collective_id=0,
    )
    down_grad, up_grad, out_grad, qkv_grad, *sums, tokens_grad = finished(
        slots, total, query_key_value, gains, sums, dx_long, dx_pack
    )
    inner_total, feed_total, hidden_total, attend_total = sums
    return (
        output,
        tokens_grad,
        qkv_grad,
        out_grad,
        up_grad,
        down_grad,
        attend_total,
        inner_total,
        feed_total,
        hidden_total,
    )


def per_device(tokens, *others):
    split = lax.axis_size("seq") == SEQ and lax.axis_size("rows") == 8
    if split and tokens.shape == (2, BLOCK, D):
        return split_layer(tokens, *others)
    return ring_layer(tokens, *others)


def solution(mesh):
    return jax.shard_map(
        per_device,
        mesh=mesh,
        in_specs=(
            P("rows", "seq", None),
            P("rows", None),
            P("rows", "seq", None),
            P(),
            P(),
            P(),
            P(),
            P(),
            P(),
            P(),
            P(),
        ),
        out_specs=(
            P("rows", "seq", None),
            P("rows", "seq", None),
            P(),
            P(),
            P(),
            P(),
            P(),
            P(),
            P(),
            P(),
        ),
        check_vma=False,
    )
```

```python
import functools
import math

import jax
import jax.numpy as jnp
from jax import lax
from jax.experimental import pallas as pl
from jax.experimental.pallas import tpu as pltpu
from jax.sharding import PartitionSpec as P

D = 768
HEADS = 12
HEAD_DIM = 64


EPSILON = 1e-05
MASKED = -1e30


def passed_along(value, axis, steps):
    count = lax.axis_size(axis)
    initial, last = (max(0, -steps), min(count, count - steps))
    return lax.ppermute(value, axis, [(source, source + steps) for source in range(initial, last)])


def from_behind(value, axis, steps):
    count = lax.axis_size(axis)
    pairs = [(source, (source + steps) % count) for source in range(count)]
    return lax.ppermute(value, axis, pairs)


def layer_norm(values, gain):
    average = jnp.mean(values, axis=-1, keepdims=True)
    centred = values - average
    inverse = lax.rsqrt(jnp.mean(centred * centred, axis=-1, keepdims=True) + EPSILON)
    normed = centred * inverse
    return (normed * gain, normed, inverse)


def norm_back(upstream, normed, inverse, gain):
    scaled = upstream * gain
    spread = (
        scaled
        - jnp.mean(scaled, axis=-1, keepdims=True)
        - normed * jnp.mean(scaled * normed, axis=-1, keepdims=True)
    )
    return (spread * inverse, jnp.sum(upstream * normed, axis=0))


def gelu_exact(values):
    return jax.nn.gelu(values, approximate=False)


def matmul(left, right):
    return jnp.dot(left, right, preferred_element_type=jnp.float32)


def left_t(left, right):
    return lax.dot_general(
        left, right, (((0,), (0,)), ((), ())), preferred_element_type=jnp.float32
    )


def right_t(left, right):
    return lax.dot_general(
        left, right, (((1,), (1,)), ((), ())), preferred_element_type=jnp.float32
    )


def split_heads(values):
    return values.reshape(values.shape[0], values.shape[1], HEADS, HEAD_DIM)


def allowed_pairs(query_pos, query_seg, key_pos, key_seg):
    causal = key_pos[None, None, None, :] <= query_pos[None, None, :, None]
    same_doc = key_seg[:, None, None, :] == query_seg[:, None, :, None]
    return causal & same_doc


def scores(queries, key_rows):
    return jnp.einsum(
        "rqhd,rkhd->rhqk",
        split_heads(queries),
        split_heads(key_rows),
        preferred_element_type=jnp.float32,
    ) * HEAD_DIM ** (-0.5)


def fold_keys(carry, piece, queries, query_pos, query_seg, segment_ids):
    key_rows, value_rows = piece
    row_count = key_rows.shape[0]
    key_count = key_rows.shape[1]
    block_width = math.gcd(key_count, queries.shape[1])
    block_count = key_count // block_width
    key_blocks = key_rows.reshape(row_count, block_count, block_width, D).transpose(1, 0, 2, 3)
    value_blocks = value_rows.reshape(row_count, block_count, block_width, D).transpose(1, 0, 2, 3)

    def one_block(state, block_item):
        accum, running, softmax_total = state
        key_block, value_block, offset = block_item
        key_start = offset * block_width
        key_pos = key_start + jnp.arange(block_width, dtype=jnp.int32)
        key_seg = lax.dynamic_slice_in_dim(segment_ids, key_start, block_width, 1)
        allowed = allowed_pairs(query_pos, query_seg, key_pos, key_seg)
        logits = jnp.where(allowed, scores(queries, key_block), MASKED)
        new_peak = jnp.maximum(running, jnp.max(logits, axis=-1))
        weights = jnp.where(allowed, jnp.exp(logits - new_peak[..., None]), 0.0)
        factor = jnp.exp(running - new_peak)
        softmax_total = softmax_total * factor + jnp.sum(weights, axis=-1)
        accum = accum * factor[..., None] + jnp.einsum(
            "rhqk,rkhd->rhqd",
            weights.astype(jnp.bfloat16),
            split_heads(value_block),
            preferred_element_type=jnp.float32,
        )
        return ((accum, new_peak, softmax_total), None)

    carry, unused = lax.scan(
        one_block, carry, (key_blocks, value_blocks, jnp.arange(block_count, dtype=jnp.int32))
    )
    return carry


def back_block(queries, grad_rows, log_total, delta, key_rows, value_rows, allowed):
    logits = jnp.where(allowed, scores(queries, key_rows), MASKED)
    probs = jnp.where(allowed, jnp.exp(logits - log_total[..., None]), 0.0)
    dprobs = jnp.einsum(
        "rqhd,rkhd->rhqk",
        split_heads(grad_rows),
        split_heads(value_rows),
        preferred_element_type=jnp.float32,
    )
    dlogits = (probs * (dprobs - delta[..., None])).astype(jnp.bfloat16)
    factor = HEAD_DIM ** (-0.5)
    query_part = (
        jnp.einsum(
            "rhqk,rkhd->rqhd", dlogits, split_heads(key_rows), preferred_element_type=jnp.float32
        )
        * factor
    )
    key_part = (
        jnp.einsum(
            "rhqk,rqhd->rkhd", dlogits, split_heads(queries), preferred_element_type=jnp.float32
        )
        * factor
    )
    value_part = jnp.einsum(
        "rhqk,rqhd->rkhd",
        probs.astype(jnp.bfloat16),
        split_heads(grad_rows),
        preferred_element_type=jnp.float32,
    )
    return (
        query_part.reshape(queries.shape),
        key_part.reshape(key_rows.shape),
        value_part.reshape(value_rows.shape),
    )


def ring_layer(
    tokens,
    segment_ids,
    cotangent,
    query_key_value,
    out_weight,
    up_weight,
    down_weight,
    attend_gain,
    inner_gain,
    feed_gain,
    hidden_gain,
):
    row_count = tokens.shape[0]
    width_q = tokens.shape[1]
    model_width = tokens.shape[2]
    token_count = row_count * width_q
    seq_index = lax.axis_index("seq")
    seq_size = lax.axis_size("seq")
    local_pos = seq_index * width_q + jnp.arange(width_q, dtype=jnp.int32)
    local_seg = lax.dynamic_slice_in_dim(segment_ids, seq_index * width_q, width_q, 1)
    residual = tokens.reshape(token_count, model_width).astype(jnp.float32)
    attend_out, attend_normed, attend_inverse = layer_norm(residual, attend_gain)
    attend_low = attend_out.astype(jnp.bfloat16)
    projected = matmul(attend_low, query_key_value).astype(jnp.bfloat16)
    queries = projected[:, :model_width].reshape(row_count, width_q, model_width)
    key_rows = projected[:, model_width : 2 * model_width].reshape(row_count, width_q, model_width)
    value_rows = projected[:, 2 * model_width :].reshape(row_count, width_q, model_width)
    start_state = (
        jnp.zeros((row_count, HEADS, width_q, HEAD_DIM), jnp.float32),
        jnp.full((row_count, HEADS, width_q), MASKED, jnp.float32),
        jnp.zeros((row_count, HEADS, width_q), jnp.float32),
    )
    accum, running, softmax_total = fold_keys(
        start_state,
        (
            lax.all_gather(key_rows, "seq", axis=1, tiled=True),
            lax.all_gather(value_rows, "seq", axis=1, tiled=True),
        ),
        queries,
        local_pos,
        local_seg,
        segment_ids,
    )
    log_total = running + jnp.log(softmax_total)
    attended = (accum / softmax_total[..., None]).transpose(0, 2, 1, 3)
    attended_flat = attended.reshape(token_count, model_width)
    inner_out, inner_normed, inner_inverse = layer_norm(attended_flat, inner_gain)
    inner_low = inner_out.astype(jnp.bfloat16)
    state = residual + matmul(inner_low, out_weight)
    feed_out, feed_normed, feed_inverse = layer_norm(state, feed_gain)
    feed_low = feed_out.astype(jnp.bfloat16)
    pre_act = matmul(feed_low, up_weight)
    hidden, gelu_back = jax.vjp(gelu_exact, pre_act)
    hidden_out, hidden_normed, hidden_inverse = layer_norm(hidden, hidden_gain)
    hidden_low = hidden_out.astype(jnp.bfloat16)
    result = state + matmul(hidden_low, down_weight)
    output = result.astype(jnp.bfloat16).reshape(tokens.shape)
    upstream_low = cotangent.reshape(token_count, model_width)
    upstream = upstream_low.astype(jnp.float32)
    down_term = left_t(hidden_low, upstream_low)
    hidden_grad, hidden_gain_term = norm_back(
        right_t(upstream_low, down_weight), hidden_normed, hidden_inverse, hidden_gain
    )
    pre_grad = gelu_back(hidden_grad)[0]
    pre_low = pre_grad.astype(jnp.bfloat16)
    up_term = left_t(feed_low, pre_low)
    feed_grad, feed_gain_term = norm_back(
        right_t(pre_low, up_weight), feed_normed, feed_inverse, feed_gain
    )
    state_grad = upstream + feed_grad
    state_low = state_grad.astype(jnp.bfloat16)
    out_term = left_t(inner_low, state_low)
    inner_grad, inner_gain_term = norm_back(
        right_t(state_low, out_weight), inner_normed, inner_inverse, inner_gain
    )
    attend_grad_low = inner_grad.astype(jnp.bfloat16).reshape(row_count, width_q, model_width)
    delta = jnp.sum(split_heads(attend_grad_low).astype(jnp.float32) * attended, axis=-1).transpose(
        0, 2, 1
    )
    zero_rows = jnp.zeros((row_count, width_q, model_width), jnp.float32)

    def key_step(step_count, cycle_state):
        moving_keys, moving_values, moving_dkeys, moving_dvalues, query_acc = cycle_state
        source = jnp.remainder(seq_index - step_count, seq_size)
        key_start = source * width_q
        key_pos = key_start + jnp.arange(width_q, dtype=jnp.int32)
        key_seg = lax.dynamic_slice_in_dim(segment_ids, key_start, width_q, 1)
        allowed = allowed_pairs(local_pos, local_seg, key_pos, key_seg)
        query_part, key_part, value_part = back_block(
            queries, attend_grad_low, log_total, delta, moving_keys, moving_values, allowed
        )
        moving_keys, moving_values = passed_along((moving_keys, moving_values), "seq", 1)
        moving_dkeys, moving_dvalues = (
            from_behind((moving_dkeys + key_part).astype(jnp.bfloat16), "seq", 1).astype(
                jnp.float32
            ),
            from_behind((moving_dvalues + value_part).astype(jnp.bfloat16), "seq", 1).astype(
                jnp.float32
            ),
        )
        return (moving_keys, moving_values, moving_dkeys, moving_dvalues, query_acc + query_part)

    cycle_out = lax.fori_loop(
        0, seq_size, key_step, (key_rows, value_rows, zero_rows, zero_rows, zero_rows)
    )
    key_grad, value_grad, query_grad = (cycle_out[2], cycle_out[3], cycle_out[4])
    joined_grad = jnp.concatenate(
        [
            query_grad.astype(jnp.bfloat16),
            key_grad.astype(jnp.bfloat16),
            value_grad.astype(jnp.bfloat16),
        ],
        axis=-1,
    ).reshape(token_count, 3 * model_width)
    qkv_term = left_t(attend_low, joined_grad)
    attend_back, attend_gain_term = norm_back(
        right_t(joined_grad, query_key_value), attend_normed, attend_inverse, attend_gain
    )
    tokens_grad = (state_grad + attend_back).astype(jnp.bfloat16).reshape(tokens.shape)
    all_sectioned = (
        lax.psum_scatter(
            qkv_term.astype(jnp.bfloat16), "rows", scatter_dimension=0, tiled=True
        ).astype(jnp.float32),
        lax.psum_scatter(
            out_term.astype(jnp.bfloat16), "rows", scatter_dimension=0, tiled=True
        ).astype(jnp.float32),
        lax.psum_scatter(
            up_term.astype(jnp.bfloat16), "rows", scatter_dimension=0, tiled=True
        ).astype(jnp.float32),
        lax.psum_scatter(
            down_term.astype(jnp.bfloat16), "rows", scatter_dimension=0, tiled=True
        ).astype(jnp.float32),
    )
    seq_sectioned = (
        lax.psum_scatter(
            all_sectioned[0].astype(jnp.bfloat16), "seq", scatter_dimension=1, tiled=True
        ).astype(jnp.float32),
        lax.psum_scatter(
            all_sectioned[1].astype(jnp.bfloat16), "seq", scatter_dimension=1, tiled=True
        ).astype(jnp.float32),
        lax.psum_scatter(
            all_sectioned[2].astype(jnp.bfloat16), "seq", scatter_dimension=1, tiled=True
        ).astype(jnp.float32),
        lax.psum_scatter(
            all_sectioned[3].astype(jnp.bfloat16), "seq", scatter_dimension=1, tiled=True
        ).astype(jnp.float32),
    )
    seq_whole = (
        lax.all_gather(seq_sectioned[0].astype(jnp.bfloat16), "seq", axis=1, tiled=True).astype(
            jnp.float32
        ),
        lax.all_gather(seq_sectioned[1].astype(jnp.bfloat16), "seq", axis=1, tiled=True).astype(
            jnp.float32
        ),
        lax.all_gather(seq_sectioned[2].astype(jnp.bfloat16), "seq", axis=1, tiled=True).astype(
            jnp.float32
        ),
        lax.all_gather(seq_sectioned[3].astype(jnp.bfloat16), "seq", axis=1, tiled=True).astype(
            jnp.float32
        ),
    )
    qkv_grad, out_grad, up_grad, down_grad = (
        lax.all_gather(seq_whole[0].astype(jnp.bfloat16), "rows", axis=0, tiled=True).astype(
            jnp.float32
        ),
        lax.all_gather(seq_whole[1].astype(jnp.bfloat16), "rows", axis=0, tiled=True).astype(
            jnp.float32
        ),
        lax.all_gather(seq_whole[2].astype(jnp.bfloat16), "rows", axis=0, tiled=True).astype(
            jnp.float32
        ),
        lax.all_gather(seq_whole[3].astype(jnp.bfloat16), "rows", axis=0, tiled=True).astype(
            jnp.float32
        ),
    )
    attend_total, inner_total, feed_total, hidden_total = lax.psum(
        (attend_gain_term, inner_gain_term, feed_gain_term, hidden_gain_term), ("rows", "seq")
    )
    return (
        output,
        tokens_grad,
        qkv_grad,
        out_grad,
        up_grad,
        down_grad,
        attend_total,
        inner_total,
        feed_total,
        hidden_total,
    )


FF = 3072
SEQ = 4
BLOCK = 512
SPLIT = BLOCK // 2
TOGETHER = 2
HEADS_OWN = HEADS // SEQ
GROUP = HEADS_OWN * 3 * HEAD_DIM
MESH = pl.DeviceIdType.MESH
F32 = jnp.float32
BF16 = jnp.bfloat16
VMEM_LIMIT = 56 * 2**20


def causal_mask(key_start, key_count, query_count):
    key_pos = lax.broadcasted_iota(jnp.int32, (key_count, query_count), 0) + key_start
    query_pos = lax.broadcasted_iota(jnp.int32, (key_count, query_count), 1)
    return key_pos <= query_pos


def attend_head(read, write, block_count):
    for query_block in range(block_count):
        here = slice(query_block * BLOCK, (query_block + 1) * BLOCK)
        queries = (read(0, here).astype(F32) * 0.125).astype(BF16)
        peak = jnp.full((1, BLOCK), MASKED, F32)
        total = jnp.zeros((1, BLOCK), F32)
        accum = jnp.zeros((HEAD_DIM, BLOCK), F32)
        for key_block in range(query_block):
            there = slice(key_block * BLOCK, (key_block + 1) * BLOCK)
            logits = matmul(read(1, there).T, queries)
            new_peak = jnp.maximum(peak, jnp.max(logits, axis=0, keepdims=True))
            weights = jnp.exp(logits - new_peak)
            factor = jnp.exp(peak - new_peak)
            total = total * factor + jnp.sum(weights, axis=0, keepdims=True)
            accum = accum * factor + matmul(read(2, there), weights.astype(BF16))
            peak = new_peak
        keys = read(1, here).T
        values = read(2, here)
        logits = jnp.where(
            causal_mask(0, SPLIT, BLOCK), matmul(keys[:SPLIT], queries), MASKED
        )
        corner = jnp.where(
            causal_mask(0, SPLIT, SPLIT), matmul(keys[SPLIT:], queries[:, SPLIT:]), MASKED
        )
        new_peak = jnp.maximum(peak, jnp.max(logits, axis=0, keepdims=True))
        late_peak = jnp.maximum(new_peak[:, SPLIT:], jnp.max(corner, axis=0, keepdims=True))
        new_peak = jnp.concatenate([new_peak[:, :SPLIT], late_peak], axis=1)
        weights = jnp.exp(logits - new_peak)
        corner = jnp.exp(corner - late_peak)
        factor = jnp.exp(peak - new_peak)
        total = total * factor + jnp.sum(weights, axis=0, keepdims=True)
        accum = accum * factor + matmul(values[:, :SPLIT], weights.astype(BF16))
        corner_total = jnp.sum(corner, axis=0, keepdims=True)
        corner_accum = matmul(values[:, SPLIT:], corner.astype(BF16))
        total = jnp.concatenate([total[:, :SPLIT], total[:, SPLIT:] + corner_total], axis=1)
        accum = jnp.concatenate([accum[:, :SPLIT], accum[:, SPLIT:] + corner_accum], axis=1)
        write(query_block, here, accum / total, new_peak + jnp.log(total))


def norm_in(x, gain):
    average = jnp.mean(x, axis=-1, keepdims=True)
    centred = x - average
    inverse = lax.rsqrt(jnp.mean(centred * centred, axis=-1, keepdims=True) + EPSILON)
    return (centred * inverse * gain).astype(BF16)


def pack_kernel(slot_ref, x_ref, w_ref, gain_ref, a_ref, qkv_ref, o_ref, lse_ref, x_out, at):
    h = pl.program_id(0)

    @pl.when(h == 0)
    def _():
        x_out[...] = x_ref[0]
        a = norm_in(x_ref[0].astype(F32), gain_ref[:, 0:D])
        a_ref[...] = a
        at[...] = a.T
        for part in range(3):
            for k in range(0, D, 256):
                columns = slice(part * D + k, part * D + k + 256)
                qkv_ref[part, k : k + 256, :] = left_t(w_ref[:, columns], at[...]).astype(BF16)

    for sub in range(TOGETHER):
        start = (h * TOGETHER + sub) * HEAD_DIM
        rows = pl.ds(pl.multiple_of(start, HEAD_DIM), HEAD_DIM)

        def write(query_block, here, o, lse):
            o_ref[sub * HEAD_DIM : (sub + 1) * HEAD_DIM, :] = o
            lse_ref[8 * sub : 8 * sub + 1, :] = lse

        attend_head(lambda part, columns: qkv_ref[part, rows, :], write, 1)


def pack_forward(slot, tokens, weight, gain):
    still = lambda *shape: pl.BlockSpec(shape, lambda h, slot: (0,) * len(shape))
    once = lambda *shape: pl.BlockSpec(
        shape, lambda h, slot: (0,) * len(shape), pipeline_mode=pl.Buffered(1)
    )
    by_head = lambda rows: pl.BlockSpec((TOGETHER * rows, BLOCK), lambda h, slot: (h, 0))
    return pl.pallas_call(
        pack_kernel,
        grid_spec=pltpu.PrefetchScalarGridSpec(
            num_scalar_prefetch=1,
            grid=(HEADS // TOGETHER,),
            in_specs=[
                pl.BlockSpec((1, BLOCK, D), lambda h, slot: (slot[0], 0, 0)),
                once(D, 3 * D),
                once(1, 3 * D + FF),
            ],
            out_specs=[still(BLOCK, D), still(3, D, BLOCK), by_head(HEAD_DIM), by_head(8)]
            + [still(BLOCK, D)],
            scratch_shapes=[pltpu.VMEM((D, BLOCK), BF16)],
        ),
        out_shape=[
            jax.ShapeDtypeStruct((BLOCK, D), BF16),
            jax.ShapeDtypeStruct((3, D, BLOCK), BF16),
            jax.ShapeDtypeStruct((D, BLOCK), F32),
            jax.ShapeDtypeStruct((HEADS * 8, BLOCK), F32),
            jax.ShapeDtypeStruct((BLOCK, D), BF16),
        ],
        compiler_params=pltpu.CompilerParams(vmem_limit_bytes=VMEM_LIMIT),
        cost_estimate=pl.CostEstimate(
            flops=8 * 10**9, bytes_accessed=10 * 2**20, transcendentals=HEADS * BLOCK * BLOCK
        ),
    )(slot, tokens, weight, gain)


def widened(gain, width):
    return jnp.concatenate([gain] * (width // 128), axis=1)


def column_stats(values):
    size = values.shape[0]
    average = jnp.sum(values, axis=0, keepdims=True) * (1.0 / size)
    centred = values - average
    spread = jnp.sum(centred * centred, axis=0, keepdims=True) * (1.0 / size)
    return average, lax.rsqrt(spread + EPSILON)


def gelu_both(values):
    t = 1.0 / (1.0 + (0.3275911 * 0.7071067811865476) * jnp.abs(values))
    density = jnp.exp(-0.5 * (values * values))
    tail = 0.5 * -1.453152027 + t * (0.5 * 1.061405429)
    tail = 0.5 * 1.421413741 + t * tail
    tail = 0.5 * -0.284496736 + t * tail
    tail = 0.5 * 0.254829592 + t * tail
    tail = tail * t * density
    below = jnp.where(values >= 0, 1.0 - tail, tail)
    return values * below, below + values * (density * 0.3989422804014327)


def feed_kernel(steps, chunk, sub, has_partial, slot, *refs):
    names = iter(refs)
    take = lambda count: [next(names) for _ in range(count)]
    o_in, x_in, dy_in, gain_ref, wo_in, wu_in, wd_in = take(7)
    part_in = take(3) if has_partial else []
    if has_partial:
        take(1)
    out_to, dh_to, do_to, go_to, gd_ref, gu_ref = take(6)
    o_ref, x_ref, dy_ref, wo, wu, wd, out_s, dh_s, do_s, go_s = take(10)
    ig, fg, hg, b_s, h_s, c_s, cn_s, dyt_s, n_s, slope_s, t_s, sum_s, dc_s, st = take(14)
    parts, part_o = take(2) if has_partial else (None, None)
    load_sem, wu_sem, wd_sem, part_sem, save_sem = take(5)
    width = BLOCK
    step = pl.program_id(0)
    o_load = pltpu.make_async_copy(o_in, o_ref, load_sem.at[0])
    wo_load = pltpu.make_async_copy(wo_in, wo, load_sem.at[1])
    x_load = pltpu.make_async_copy(x_in.at[slot[0]], x_ref, load_sem.at[2])
    dy_load = pltpu.make_async_copy(dy_in.at[slot[0]], dy_ref, load_sem.at[3])

    def span(k):
        return pl.ds(pl.multiple_of(k * chunk, chunk), chunk)

    def wu_load(k):
        return pltpu.make_async_copy(wu_in.at[:, span(k)], wu.at[:, span(k)], wu_sem.at[k])

    def wd_load(k):
        return pltpu.make_async_copy(wd_in.at[span(k), :], wd.at[span(k), :], wd_sem.at[k])

    def part_load(which, k):
        return pltpu.make_async_copy(
            part_in[which].at[span(k), :], parts.at[k], part_sem.at[which, k]
        )

    def save(k):
        source, target = [(out_s, out_to.at[slot[0]]), (dh_s, dh_to), (do_s, do_to), (go_s, go_to)][k]
        return pltpu.make_async_copy(source, target, save_sem.at[k])

    @pl.when(step == 0)
    def _():
        for load in (o_load, wo_load, x_load):
            load.start()
        ig[...] = jnp.broadcast_to(gain_ref[:, D : 2 * D], (128, D)).T
        fg[...] = jnp.broadcast_to(gain_ref[:, 2 * D : 3 * D], (128, D)).T
        hg[...] = jnp.broadcast_to(gain_ref[:, 3 * D :], (128, FF)).T
        o_load.wait()
        o = o_ref[...].astype(F32)
        average, inverse = column_stats(o)
        b = ((o - average) * inverse * widened(ig[...], width)).astype(BF16)
        b_s[...] = b
        st[0:1] = average
        st[1:2] = inverse
        wo_load.wait()
        x_load.wait()
        wu_load(0).start()
        dy_load.start()
        h = x_ref[...].T.astype(F32) + left_t(wo[...], b)
        h_s[...] = h
        average, inverse = column_stats(h)
        st[2:3] = average
        st[3:4] = inverse
        c = ((h - average) * inverse * widened(fg[...], width)).astype(BF16)
        c_s[...] = c
        cn_s[...] = c.T
        dy_load.wait()
        dyt_s[...] = dy_ref[...].T
        for k in range(1, steps):
            wu_load(k).start()
        for k in range(steps):
            wd_load(k).start()
        if has_partial:
            for k in range(steps):
                part_load(0, k).start()
            pltpu.make_async_copy(part_in[2], part_o, load_sem.at[4]).start()

    @pl.when(step < steps)
    def _():
        wu_load(step).wait()
        base = pl.multiple_of(step * chunk, chunk)
        for k in range(chunk // sub):
            u = left_t(wu[:, pl.ds(base + k * sub, sub)], c_s[...])
            z, slope = gelu_both(u)
            n_s[pl.ds(base + k * sub, sub), :] = z
            slope_s[pl.ds(base + k * sub, sub), :] = slope.astype(BF16)

    @pl.when(step == steps - 1)
    def _():
        total = jnp.zeros((1, width), F32)
        for k in range(FF // sub):
            total = total + jnp.sum(n_s[k * sub : (k + 1) * sub, :], axis=0, keepdims=True)
        average = total * (1.0 / FF)
        total = jnp.zeros((1, width), F32)
        for k in range(FF // sub):
            centred = n_s[k * sub : (k + 1) * sub, :] - average
            total = total + jnp.sum(centred * centred, axis=0, keepdims=True)
        st[4:5] = average
        st[5:6] = lax.rsqrt(total * (1.0 / FF) + EPSILON)
        st[6:8] = jnp.zeros((2, width), F32)
        sum_s[...] = h_s[...]

    @pl.when((step >= steps) & (step < 2 * steps))
    def _():
        turn = step - steps
        wd_load(turn).wait()
        if has_partial:
            part_load(0, turn).wait()
        base = pl.multiple_of(turn * chunk, chunk)
        average = st[4:5]
        inverse = st[5:6]
        first = jnp.zeros((1, width), F32)
        second = jnp.zeros((1, width), F32)
        pieces = []
        for k in range(chunk // sub):
            rows = slice(k * sub, (k + 1) * sub)
            here = pl.ds(base + k * sub, sub)
            n = (n_s[here, :] - average) * inverse
            n_s[here, :] = n
            gain = widened(hg[here, :], width)
            e = (n * gain).astype(BF16)
            pieces.append(e)
            t = matmul(wd[here, :], dyt_s[...]) * gain
            t_s[here, :] = t
            first = first + jnp.sum(t, axis=0, keepdims=True)
            second = second + jnp.sum(t * n, axis=0, keepdims=True)
            grad = matmul(e, dy_ref[...])
            if has_partial:
                grad = grad + parts[turn, rows, :].astype(F32)
            gd_ref[rows, :] = grad.astype(BF16)
        sum_s[...] += left_t(wd[pl.ds(base, chunk), :], jnp.concatenate(pieces, axis=0))
        st[6:7] += first
        st[7:8] += second
        if has_partial:
            part_load(1, turn).start()

    @pl.when(step == 2 * steps - 1)
    def _():
        out_s[...] = sum_s[...].astype(BF16).T
        save(0).start()
        st[6:8] = st[6:8] * (1.0 / FF)
        dc_s[...] = jnp.zeros_like(dc_s)

    @pl.when(step >= 2 * steps)
    def _():
        turn = step - 2 * steps
        if has_partial:
            part_load(1, turn).wait()
        base = pl.multiple_of(turn * chunk, chunk)
        inverse = st[5:6]
        first = st[6:7]
        second = st[7:8]
        pieces = []
        for k in range(chunk // sub):
            rows = slice(k * sub, (k + 1) * sub)
            here = pl.ds(base + k * sub, sub)
            n = n_s[here, :]
            du = ((t_s[here, :] - first - n * second) * inverse * slope_s[here, :].astype(F32)).astype(BF16)
            pieces.append(du)
            grad = matmul(du, cn_s[...])
            if has_partial:
                grad = grad + parts[turn, rows, :].astype(F32)
            gu_ref[rows, :] = grad.astype(BF16)
        dc_s[...] += matmul(wu[:, pl.ds(base, chunk)], jnp.concatenate(pieces, axis=0))

    @pl.when(step == 3 * steps - 1)
    def _():
        n = (h_s[...] - st[2:3]) * st[3:4]
        t = dc_s[...] * widened(fg[...], width)
        first = jnp.sum(t, axis=0, keepdims=True) * (1.0 / D)
        second = jnp.sum(t * n, axis=0, keepdims=True) * (1.0 / D)
        dh = dyt_s[...].astype(F32) + (t - first - n * second) * st[3:4]
        dh_s[...] = dh
        save(1).start()
        dh_low = dh.astype(BF16)
        n = (o_ref[...].astype(F32) - st[0:1]) * st[1:2]
        t = matmul(wo[...], dh_low) * widened(ig[...], width)
        first = jnp.sum(t, axis=0, keepdims=True) * (1.0 / D)
        second = jnp.sum(t * n, axis=0, keepdims=True) * (1.0 / D)
        do_s[...] = ((t - first - n * second) * st[1:2]).astype(BF16)
        save(2).start()
        grad = matmul(b_s[...], dh_low.T)
        if has_partial:
            pltpu.make_async_copy(part_in[2], part_o, load_sem.at[4]).wait()
            grad = grad + part_o[...].astype(F32)
        go_s[...] = grad.astype(BF16)
        save(3).start()
        for k in range(4):
            save(k).wait()


def feed_both(slot, o_t, tokens, cotangent, gains, weights, partial=None, output=None, chunk=1536, sub=256):
    width = BLOCK
    steps = FF // chunk
    has_partial = partial is not None
    anywhere = pl.BlockSpec(memory_space=pl.ANY)
    second = lambda i, slot: (jnp.clip(i - steps, 0, steps - 1), 0)
    third = lambda i, slot: (jnp.clip(i - 2 * steps, 0, steps - 1), 0)
    dma = pltpu.SemaphoreType.DMA
    scratch = [
        pltpu.VMEM((D, width), o_t.dtype),
        pltpu.VMEM((width, D), BF16),
        pltpu.VMEM((width, D), BF16),
        pltpu.VMEM((D, D), BF16),
        pltpu.VMEM((D, FF), BF16),
        pltpu.VMEM((FF, D), BF16),
        pltpu.VMEM((width, D), BF16),
        pltpu.VMEM((D, width), F32),
        pltpu.VMEM((D, width), BF16),
        pltpu.VMEM((D, D), BF16),
        pltpu.VMEM((D, 128), F32),
        pltpu.VMEM((D, 128), F32),
        pltpu.VMEM((FF, 128), F32),
        pltpu.VMEM((D, width), BF16),
        pltpu.VMEM((D, width), F32),
        pltpu.VMEM((D, width), BF16),
        pltpu.VMEM((width, D), BF16),
        pltpu.VMEM((D, width), BF16),
        pltpu.VMEM((FF, width), F32),
        pltpu.VMEM((FF, width), BF16),
        pltpu.VMEM((FF, width), F32),
        pltpu.VMEM((D, width), F32),
        pltpu.VMEM((D, width), F32),
        pltpu.VMEM((8, width), F32),
    ]
    args = [o_t, tokens, cotangent, gains, *weights]
    if has_partial:
        args += [*partial, output]
        scratch += [pltpu.VMEM((steps, chunk, D), BF16), pltpu.VMEM((D, D), BF16)]
    scratch += [dma((5,)), dma((steps,)), dma((steps,)), dma((2, steps)), dma((4,))]
    return pl.pallas_call(
        functools.partial(feed_kernel, steps, chunk, sub, has_partial),
        grid_spec=pltpu.PrefetchScalarGridSpec(
            num_scalar_prefetch=1,
            grid=(3 * steps,),
            in_specs=[anywhere] * 3
            + [pl.BlockSpec(gains.shape, lambda i, slot: (0, 0), pipeline_mode=pl.Buffered(1))]
            + [anywhere] * (len(args) - 4),
            out_specs=[anywhere] * 4
            + [pl.BlockSpec((chunk, D), second), pl.BlockSpec((chunk, D), third)],
            scratch_shapes=scratch,
        ),
        input_output_aliases={len(args): 0} if has_partial else {},
        out_shape=[
            jax.ShapeDtypeStruct((2, width, D), BF16),
            jax.ShapeDtypeStruct((D, width), F32),
            jax.ShapeDtypeStruct((D, width), BF16),
            jax.ShapeDtypeStruct((D, D), BF16),
            jax.ShapeDtypeStruct((FF, D), BF16),
            jax.ShapeDtypeStruct((FF, D), BF16),
        ],
        compiler_params=pltpu.CompilerParams(vmem_limit_bytes=62 * 2**20),
        cost_estimate=pl.CostEstimate(
            flops=6 * width * D * (D + 2 * FF), bytes_accessed=50 * 2**20, transcendentals=width * FF
        ),
    )(slot, *args)


def long_kernel(*refs):
    own_x, left, right, left_two, right_two, across, w_ref, gain_ref = refs[:8]
    qkv_ref, o_ref, lse_ref, do_ref, a_ref, x_ref, dh_ref = refs[8:15]
    a_out, qkv_out, o_out, lse_out, mine_out, gq_out, dx_out = refs[15:22]
    a_all, qkv, o_own, lse_own, o_low, w, qp, op, lp, dop, ap, xp, dhp, dp, gq, dx = refs[22:38]
    x_all, w_near, w_own, load_sem, save_sem, swap_send, swap_recv = refs[38:]
    gain_row = gain_ref[:, 0:D]
    r = lax.axis_index("rows")
    s = lax.axis_index("seq")
    shifted = [(r, (s + shift) % SEQ) for shift in range(SEQ)]
    barrier = pltpu.get_barrier_semaphore()
    for device in shifted[1:]:
        pl.semaphore_signal(barrier, inc=1, device_id=device, device_id_type=MESH)
    pl.semaphore_wait(barrier, SEQ - 1)
    sources = [qkv_ref, o_ref, lse_ref, do_ref, a_ref, x_ref, dh_ref, w_ref]
    targets = [qp, op, lp, dop, ap, xp, dhp, w]
    loads = [
        pltpu.make_async_copy(source, target, load_sem.at[k])
        for k, (source, target) in enumerate(zip(sources, targets))
    ]
    nears = [
        pltpu.make_async_copy(
            w_ref.at[:, pl.ds(pl.multiple_of(part * D + (3 * s // 2) * 128, 128), 256)],
            w_near.at[part],
            load_sem.at[8 + part],
        )
        for part in range(3)
    ]
    x_from = [
        [own_x, right, right_two, across],
        [left, own_x, right, right_two],
        [left_two, left, own_x, right],
        [across, left_two, left, own_x],
    ]

    def x_load(k, j):
        return pltpu.make_async_copy(x_from[k][j], x_all.at[j], load_sem.at[11 + j])

    for k in range(SEQ):

        @pl.when(s == k)
        def _():
            for j in range(SEQ):
                x_load(k, j).start()

    for load in nears + loads:
        load.start()
    saves = [
        pltpu.make_async_copy(source, target, save_sem.at[k])
        for k, (source, target) in enumerate(
            [(a_all, a_out), (qkv, qkv_out), (o_own, o_out), (lse_own, lse_out)]
            + [(gq, gq_out), (dx, dx_out)]
        )
    ]

    def o_copy(h, shift):
        part = o_low.at[(s + shift) % SEQ, pl.ds(h * HEAD_DIM, HEAD_DIM), :]
        place = pl.ds(pl.multiple_of(s * (HEADS_OWN * HEAD_DIM) + h * HEAD_DIM, 16), HEAD_DIM)
        target = mine_out.at[place, :]
        if shift == 0:
            return pltpu.make_async_copy(part, target, save_sem.at[6 + h])
        return pltpu.make_async_remote_copy(
            src_ref=part,
            dst_ref=target,
            send_sem=swap_send.at[h, shift],
            recv_sem=swap_recv.at[h, shift],
            device_id=shifted[shift],
            device_id_type=MESH,
        )

    for part in range(3):
        nears[part].wait()

        @pl.when(s % 2 == 0)
        def _():
            w_own[part] = w_near[part, :, 0:192]

        @pl.when(s % 2 == 1)
        def _():
            w_own[part] = w_near[part, :, 64:256]

    for j in range(SEQ):
        start = j * BLOCK
        x_load(0, j).wait()
        a = norm_in(x_all[j].astype(F32), gain_row)
        a_all[start : start + BLOCK, :] = a
        a_t = a.T
        for part in range(3):
            qkv[part, :, start : start + BLOCK] = left_t(w_own[part], a_t).astype(BF16)
    saves[0].start()
    saves[1].start()
    for h in range(HEADS_OWN):
        rows = slice(h * HEAD_DIM, (h + 1) * HEAD_DIM)

        def write(query_block, here, o, lse):
            o_own[rows, here] = o
            lse_own[h, 0:1, here] = lse
            o_low[query_block, rows, :] = o.astype(BF16)

        attend_head(lambda part, columns: qkv[part, rows, columns], write, SEQ)
        for shift in range(SEQ):
            o_copy(h, shift).start()
    saves[2].start()
    saves[3].start()
    for load in loads:
        load.wait()

    def back_head(h):
        rows = pl.ds(pl.multiple_of(h * HEAD_DIM, HEAD_DIM), HEAD_DIM)
        queries_t = (qp[0, rows, :].astype(F32) * 0.125).astype(BF16)
        keys_t = qp[1, rows, :]
        do_t = dop[rows, :]
        lse = lp[pl.ds(pl.multiple_of(h * 8, 8), 8), :][0:1]
        delta = jnp.sum(do_t.astype(F32) * op[rows, :], axis=0, keepdims=True)
        keys = keys_t.T
        values = qp[2, rows, :].T
        queries = queries_t.T
        do_rows = do_t.T
        probs = jnp.exp(matmul(keys[:SPLIT], queries_t) - lse)
        probs = jnp.where(causal_mask(0, SPLIT, BLOCK), probs, 0.0)
        dprobs = matmul(values[:SPLIT], do_t)
        dlogits = (probs * (dprobs - delta)).astype(BF16)
        late = slice(SPLIT, BLOCK)
        corner = jnp.exp(matmul(keys[SPLIT:], queries_t[:, late]) - lse[:, late])
        corner = jnp.where(causal_mask(0, SPLIT, SPLIT), corner, 0.0)
        dcorner = matmul(values[SPLIT:], do_t[:, late])
        dcorner = (corner * (dcorner - delta[:, late])).astype(BF16)
        dq = matmul(keys_t[:, :SPLIT], dlogits)
        dq_late = dq[:, late] + matmul(keys_t[:, late], dcorner)
        dp[0, rows, :SPLIT] = (dq[:, :SPLIT] * 0.125).astype(BF16)
        dp[0, rows, late] = (dq_late * 0.125).astype(BF16)
        dp[1, rows, :SPLIT] = matmul(dlogits, queries).T.astype(BF16)
        dp[1, rows, late] = matmul(dcorner, queries[late]).T.astype(BF16)
        dp[2, rows, :SPLIT] = matmul(probs.astype(BF16), do_rows).T.astype(BF16)
        dp[2, rows, late] = matmul(corner.astype(BF16), do_rows[late]).T.astype(BF16)

    def back(turn, carry):
        for sub in range(TOGETHER):
            back_head(turn * TOGETHER + sub)
        return carry

    lax.fori_loop(0, HEADS // TOGETHER, back, 0)
    for part in range(3):
        gq[part * D : (part + 1) * D, :] = matmul(dp[part], ap[...]).astype(BF16)
    saves[4].start()
    dx[...] = first_norm_back(xp[...], dhp[...], w, dp, gain_row)
    saves[5].start()
    for save in saves:
        save.wait()
    for h in range(HEADS_OWN):
        for shift in range(SEQ):
            o_copy(h, shift).wait()


def first_norm_back(x, dh_t, w, dqkv, gain):
    x_t = x.T.astype(F32)
    average, inverse = column_stats(x_t)
    n = (x_t - average) * inverse
    t = matmul(w[:, 0:D], dqkv[0])
    for part in range(1, 3):
        t = t + matmul(w[:, part * D : (part + 1) * D], dqkv[part])
    t = t * widened(jnp.broadcast_to(gain, (128, D)).T, BLOCK)
    first = jnp.sum(t, axis=0, keepdims=True) * (1.0 / D)
    second = jnp.sum(t * n, axis=0, keepdims=True) * (1.0 / D)
    return (dh_t + (t - first - n * second) * inverse).astype(BF16).T


def long_forward(x_blocks, weight, gains, pack, collective_id):
    own_rows = HEADS_OWN * HEAD_DIM
    length = SEQ * BLOCK
    dma = pltpu.SemaphoreType.DMA
    anywhere = pl.BlockSpec(memory_space=pl.ANY)
    resident = pl.BlockSpec(memory_space=pltpu.VMEM)
    return pl.pallas_call(
        long_kernel,
        in_specs=[anywhere] * 7 + [resident] + [anywhere] * 7,
        out_specs=[anywhere] * 7,
        out_shape=[
            jax.ShapeDtypeStruct((length, D), BF16),
            jax.ShapeDtypeStruct((3, own_rows, length), BF16),
            jax.ShapeDtypeStruct((own_rows, length), F32),
            jax.ShapeDtypeStruct((HEADS_OWN, 8, length), F32),
            jax.ShapeDtypeStruct((D, BLOCK), BF16),
            jax.ShapeDtypeStruct((3 * D, D), BF16),
            jax.ShapeDtypeStruct((BLOCK, D), BF16),
        ],
        scratch_shapes=[
            pltpu.VMEM((length, D), BF16),
            pltpu.VMEM((3, own_rows, length), BF16),
            pltpu.VMEM((own_rows, length), F32),
            pltpu.VMEM((HEADS_OWN, 8, length), F32),
            pltpu.VMEM((SEQ, own_rows, BLOCK), BF16),
            pltpu.VMEM((D, 3 * D), BF16),
            pltpu.VMEM((3, D, BLOCK), BF16),
            pltpu.VMEM((D, BLOCK), F32),
            pltpu.VMEM((HEADS * 8, BLOCK), F32),
            pltpu.VMEM((D, BLOCK), BF16),
            pltpu.VMEM((BLOCK, D), BF16),
            pltpu.VMEM((BLOCK, D), BF16),
            pltpu.VMEM((D, BLOCK), F32),
            pltpu.VMEM((3, D, BLOCK), BF16),
            pltpu.VMEM((3 * D, D), BF16),
            pltpu.VMEM((BLOCK, D), BF16),
            pltpu.VMEM((SEQ, BLOCK, D), BF16),
            pltpu.VMEM((3, D, 256), BF16),
            pltpu.VMEM((3, D, own_rows), BF16),
            dma((11 + SEQ,)),
            dma((6 + HEADS_OWN,)),
            dma((HEADS_OWN, SEQ)),
            dma((HEADS_OWN, SEQ)),
        ],
        compiler_params=pltpu.CompilerParams(
            collective_id=collective_id, has_side_effects=True, vmem_limit_bytes=VMEM_LIMIT
        ),
        cost_estimate=pl.CostEstimate(
            flops=20 * 10**9, bytes_accessed=40 * 2**20, transcendentals=10**7
        ),
    )(*x_blocks, weight, gains, *pack)


PIECE = 768
HALF = PIECE // 2
COLS = D // 2
FEED_PIECES = (2 * FF + D) // PIECE
QKV_PIECES = 3 * D // PIECE
PIECES = FEED_PIECES + QKV_PIECES
ATTEND_TICK = 2
QKV_TICK = 5
BACK_TICK = 3
BACKS = 1
DX_TICK = 13


def sum_kernel(*refs):
    gd, gu, go, gq, do_ref, qkv_ref, o_ref, lse_ref, a_ref, gain_ref = refs[:10]
    x_ref, dh_ref, wd_ref, wu_ref, wo_ref, wq_ref, total_ref, dx_ref, sums_ref = refs[10:19]
    own, r0, r1, r2, r3, r4, fin, qkv, o_own, lse_own, a_all, gq_own, do_own, d_own = refs[19:33]
    dk_acc, dv_acc, back_ref, x_own, dh_own, wq, dx, grads, factors, sums = refs[33:43]
    own_sem, send_sem, recv_sem, fin_sem, in_sem, swap_send, swap_recv, gain_sem = refs[43:]
    r = lax.axis_index("rows")
    s = lax.axis_index("seq")
    core, xb, yb = r % 2, (r // 2) % 2, r // 4
    inside = (s == 1) | (s == 2)
    outside = (s == 0) | (s == 3)
    to_core = (r + 1 - 2 * core, s)
    to_x = (r + 2 - 4 * xb, s)
    to_y = (r + 4 - 8 * yb, s)
    to_pair = (r, s + 1 - 2 * (s % 2))
    to_middle = (r, 3 - s)
    shifted = [(r, (s + shift) % SEQ) for shift in range(SEQ)]
    barrier = pltpu.get_barrier_semaphore()
    for device in (to_core, to_x, to_y, *shifted[1:]):
        pl.semaphore_signal(barrier, inc=1, device_id=device, device_id_type=MESH)
    pl.semaphore_wait(barrier, 6)
    bits = [(xb, yb), (yb, xb)]
    partners = [(to_x, to_y), (to_y, to_x)]

    def rows_at(start, count):
        return pl.ds(pl.multiple_of(start, 16), count)

    def remote(source, target, send, recv, device):
        return pltpu.make_async_remote_copy(
            src_ref=source,
            dst_ref=target,
            send_sem=send,
            recv_sem=recv,
            device_id=device,
            device_id_type=MESH,
        )

    def numbered(source, target, kind, p, device):
        return remote(source, target, send_sem.at[kind, p], recv_sem.at[kind, p], device)

    def columns(o):
        return slice(o * COLS, (o + 1) * COLS)

    def base(o):
        return bits[o][0] * 192 + bits[o][1] * 96

    def core_copy(ref, q, p):
        part = ref.at[rows_at(q * PIECE + (1 - core) * HALF, HALF), :]
        return numbered(part, r0.at[p], 0, p, to_core)

    def own_copy(ref, q, p):
        part = ref.at[rows_at(q * PIECE + core * HALF, HALF), :]
        return pltpu.make_async_copy(part, own.at[p], own_sem.at[p])

    def first_copy(p, o):
        part = own.at[p, rows_at((1 - bits[o][0]) * 192, 192), columns(o)]
        return numbered(part, r1.at[p, o], 1 + o, p, partners[o][0])

    def second_copy(p, o):
        part = own.at[p, rows_at(bits[o][0] * 192 + (1 - bits[o][1]) * 96, 96), columns(o)]
        return numbered(part, r2.at[p, o], 3 + o, p, partners[o][1])

    def pair_copy(p, o):
        part = own.at[p, rows_at(base(o), 96), columns(o)]
        return numbered(part, r3.at[p, o], 5 + o, p, to_pair)

    def middle_copy(p, o):
        part = own.at[p, rows_at(base(o), 96), columns(o)]
        return numbered(part, r4.at[p, o], 7 + o, p, to_middle)

    def region(p, start, count, o):
        return total_ref.at[rows_at(p * PIECE + core * HALF + start, count), columns(o)]

    def fin_copy(p, o):
        return pltpu.make_async_copy(fin.at[p, o], region(p, base(o), 96, o), fin_sem.at[o, p])

    def pair_back(p, o):
        return numbered(fin.at[p, o], region(p, base(o), 96, o), 9 + o, p, to_pair)

    def second_back(p, o):
        part = region(p, base(o), 96, o)
        return numbered(part, part, 11 + o, p, partners[o][1])

    def first_back(p, o):
        part = region(p, bits[o][0] * 192, 192, o)
        return numbered(part, part, 13 + o, p, partners[o][0])

    def core_back(p):
        part = total_ref.at[rows_at(p * PIECE + core * HALF, HALF), :]
        return numbered(part, part, 15, p, to_core)

    def do_copy(shift):
        part = do_ref.at[(s + shift) % SEQ]
        if shift == 0:
            return pltpu.make_async_copy(part, do_own.at[s], in_sem.at[5])
        return remote(
            part, do_own.at[s], swap_send.at[0, shift], swap_recv.at[0, shift], shifted[shift]
        )

    def back_copy(h, shift):
        part = d_own.at[(s + shift) % SEQ, :, rows_at(h * HEAD_DIM, HEAD_DIM), :]
        target = back_ref.at[
            :, rows_at(s * (HEADS_OWN * HEAD_DIM) + h * HEAD_DIM, HEAD_DIM), :
        ]
        if shift == 0:
            return pltpu.make_async_copy(part, target, in_sem.at[6 + h])
        return remote(
            part, target, swap_send.at[1 + h, shift], swap_recv.at[1 + h, shift], shifted[shift]
        )

    loads = [
        pltpu.make_async_copy(qkv_ref, qkv, in_sem.at[0]),
        pltpu.make_async_copy(o_ref, o_own, in_sem.at[1]),
        pltpu.make_async_copy(lse_ref, lse_own, in_sem.at[2]),
        pltpu.make_async_copy(a_ref, a_all, in_sem.at[3]),
        pltpu.make_async_copy(gq, gq_own, in_sem.at[4]),
    ]
    late = [
        pltpu.make_async_copy(x_ref, x_own, in_sem.at[6 + HEADS_OWN]),
        pltpu.make_async_copy(dh_ref, dh_own, in_sem.at[7 + HEADS_OWN]),
        pltpu.make_async_copy(wq_ref, wq, in_sem.at[8 + HEADS_OWN]),
    ]
    dx_save = pltpu.make_async_copy(dx, dx_ref, in_sem.at[9 + HEADS_OWN])
    sums_save = pltpu.make_async_copy(sums, sums_ref, in_sem.at[10 + HEADS_OWN])
    for shift in range(1, SEQ):
        do_copy(shift).start()
    offset = 0
    for ref in (gd, gu, go):

        def begin(q, carry, ref=ref, offset=offset):
            core_copy(ref, q, q + offset).start()
            own_copy(ref, q, q + offset).start()
            return carry

        lax.fori_loop(0, ref.shape[0] // PIECE, begin, 0)
        offset += ref.shape[0] // PIECE
    do_copy(0).start()
    for load in loads:
        load.start()

    def added(index, other):
        own[index] = (own[index].astype(F32) + other.astype(F32)).astype(BF16)

    def after_core(p):
        own_copy(gd, 0, p).wait()
        core_copy(gd, 0, p).wait()
        own[p] = (own[p].astype(F32) + r0[p].astype(F32)).astype(BF16)
        for o in range(2):
            first_copy(p, o).start()

    def after_first(p):
        for o in range(2):
            first_copy(p, o).wait()
            added((p, rows_at(bits[o][0] * 192, 192), columns(o)), r1[p, o])
            second_copy(p, o).start()

    def after_second(p):
        for o in range(2):
            second_copy(p, o).wait()
            added((p, rows_at(base(o), 96), columns(o)), r2[p, o])

            @pl.when(outside)
            def _():
                pair_copy(p, o).start()

    def after_pair(p):
        for o in range(2):

            @pl.when(outside)
            def _():
                pair_copy(p, o).wait_send()

            @pl.when(inside)
            def _():
                pair_copy(p, o).wait_recv()
                added((p, rows_at(base(o), 96), columns(o)), r3[p, o])
                middle_copy(p, o).start()

    def after_middle(p):
        for o in range(2):

            @pl.when(inside)
            def _():
                middle_copy(p, o).wait()
                mine = own[p, rows_at(base(o), 96), columns(o)].astype(F32)
                fin[p, o] = (mine + r4[p, o].astype(F32)).astype(BF16)
                pair_back(p, o).start()
                fin_copy(p, o).start()

    def after_pair_back(p):
        for o in range(2):

            @pl.when(inside)
            def _():
                fin_copy(p, o).wait()
                pair_back(p, o).wait_send()

            @pl.when(outside)
            def _():
                pair_back(p, o).wait_recv()

            second_back(p, o).start()

    def after_second_back(p):
        for o in range(2):
            second_back(p, o).wait()
            first_back(p, o).start()

    def after_first_back(p):
        for o in range(2):
            first_back(p, o).wait()
        core_back(p).start()

    def after_core_back(p):
        core_back(p).wait()

    stages = [
        after_core,
        after_first,
        after_second,
        after_pair,
        after_middle,
        after_pair_back,
        after_second_back,
        after_first_back,
    ]

    def square(ref, p):
        return ref.at[rows_at(p * PIECE, PIECE), :]

    def grad_load(p):
        return pltpu.make_async_copy(square(total_ref, p), grads.at[p % 2], gain_sem.at[0, p % 2])

    def factor_load(ref, p):
        return pltpu.make_async_copy(ref, factors.at[p % 2], gain_sem.at[1, p % 2])

    def fetch(p):
        grad_load(p).start()

        @pl.when(p < 4)
        def _():
            factor_load(square(wd_ref, p), p).start()

        @pl.when((p >= 4) & (p < 8))
        def _():
            columns = pl.ds(pl.multiple_of((p - 4) * PIECE, PIECE), PIECE)
            factor_load(wu_ref.at[:, columns], p).start()

        @pl.when(p == 8)
        def _():
            factor_load(wo_ref, p).start()

    def row_sums(values):
        folded = values[:, 0:128]
        for k in range(1, D // 128):
            folded = folded + values[:, k * 128 : (k + 1) * 128]
        return jnp.sum(folded.T, axis=0, keepdims=True)

    def weigh(p):
        grad_load(p).wait()
        factor_load(wo_ref, p).wait()
        grad = grads[p % 2].astype(F32)

        @pl.when(p < 4)
        def _():
            place = pl.ds(pl.multiple_of(p * PIECE, PIECE), PIECE)
            sums[0:1, place] = row_sums(grad * factors[p % 2].astype(F32))

        @pl.when((p >= 4) & (p < 8))
        def _():
            term = jnp.sum(grad * factors[p % 2].T.astype(F32), axis=0, keepdims=True)
            sums[1:2, 0:D] = jnp.where(p == 4, 0.0, sums[1:2, 0:D]) + term

        @pl.when(p == 8)
        def _():
            sums[2:3, 0:D] = row_sums(grad * factors[p % 2].astype(F32))

    def head_rows(h):
        return rows_at(h * HEAD_DIM, HEAD_DIM)

    def attend(h, query_block):
        rows = head_rows(h)
        here = slice(query_block * BLOCK, (query_block + 1) * BLOCK)
        queries_t = (qkv[0, rows, here].astype(F32) * 0.125).astype(BF16)
        queries = queries_t.T
        do_t = do_own[query_block, rows, :]
        do_rows = do_t.T
        lse = lse_own[h, 0:1, here]
        delta = jnp.sum(do_t.astype(F32) * o_own[rows, here], axis=0, keepdims=True)
        dq = jnp.zeros((HEAD_DIM, BLOCK), F32)
        for key_block in range(query_block + 1):
            there = slice(key_block * BLOCK, (key_block + 1) * BLOCK)
            keys_t = qkv[1, rows, there]
            probs = jnp.exp(matmul(keys_t.T, queries_t) - lse)
            if key_block == query_block:
                probs = jnp.where(causal_mask(0, BLOCK, BLOCK), probs, 0.0)
            dprobs = matmul(qkv[2, rows, there].T, do_t)
            dlogits = (probs * (dprobs - delta)).astype(BF16)
            dq = dq + matmul(keys_t, dlogits)
            dv_acc[there, :] += matmul(probs.astype(BF16), do_rows)
            dk_acc[there, :] += matmul(dlogits, queries)
        d_own[query_block, 0, rows, :] = (dq * 0.125).astype(BF16)

    def finish_head(h):
        rows = head_rows(h)
        total = jnp.zeros((3 * HEAD_DIM, D), F32)
        for block in range(SEQ):
            here = slice(block * BLOCK, (block + 1) * BLOCK)
            d_own[block, 1, rows, :] = dk_acc[here, :].T.astype(BF16)
            d_own[block, 2, rows, :] = dv_acc[here, :].T.astype(BF16)
            joined = d_own[block, :, rows, :].reshape(3 * HEAD_DIM, BLOCK)
            total = total + matmul(joined, a_all[here, :])
        for part in range(3):
            place = rows_at(part * D + s * (HEADS_OWN * HEAD_DIM) + h * HEAD_DIM, HEAD_DIM)
            term = total[part * HEAD_DIM : (part + 1) * HEAD_DIM, :]
            gq_own[place, :] = (gq_own[place, :].astype(F32) + term).astype(BF16)
        back_copy(h, 0).start()

    def tick(t, carry):
        for lag, stage in enumerate(stages):
            for sub in range(2):
                p = 2 * (t - lag) + sub

                @pl.when((p >= 0) & (p < FEED_PIECES))
                def _():
                    stage(p)

                q = 2 * (t - lag - QKV_TICK) + sub

                @pl.when((q >= 0) & (q < QKV_PIECES))
                def _():
                    stage(FEED_PIECES + q)

        @pl.when(t == ATTEND_TICK)
        def _():
            for load in loads:
                load.wait()
            for load in late:
                load.start()
            for shift in range(SEQ):
                do_copy(shift).wait()

        h = t - ATTEND_TICK

        @pl.when((h >= 0) & (h < HEADS_OWN))
        def _():
            dk_acc[...] = jnp.zeros_like(dk_acc)
            dv_acc[...] = jnp.zeros_like(dv_acc)
            for query_block in range(SEQ):
                attend(h, query_block)
            finish_head(h)

        @pl.when(h == HEADS_OWN - 1)
        def _():
            for q in range(QKV_PIECES):
                core_copy(gq_own, q, FEED_PIECES + q).start()
                own_copy(gq_own, q, FEED_PIECES + q).start()

        for unit in range(3 * HEADS_OWN):

            @pl.when(t == BACK_TICK + unit // BACKS)
            def _():
                back_copy(unit // 3, unit % 3 + 1).start()

        for sub in range(2):
            p = 2 * (t - len(stages) - 1) + sub

            @pl.when((p >= 0) & (p < FEED_PIECES))
            def _():
                weigh(p)

        for sub in range(2):
            p = 2 * (t - len(stages)) + sub

            @pl.when((p >= 0) & (p < FEED_PIECES))
            def _():
                after_core_back(p)
                fetch(p)

            q = p - 2 * QKV_TICK

            @pl.when((q >= 0) & (q < QKV_PIECES))
            def _():
                after_core_back(FEED_PIECES + q)

        @pl.when(t == DX_TICK)
        def _():
            for load in late:
                load.wait()
            for h in range(HEADS_OWN):
                for shift in range(SEQ):
                    back_copy(h, shift).wait()
            dx[...] = first_norm_back(x_own[...], dh_own[...], wq, back_ref, gain_ref[:, 0:D])
            dx_save.start()

        return carry

    last = QKV_TICK + (QKV_PIECES - 1) // 2 + len(stages) + 1
    lax.fori_loop(0, last, tick, 0)
    sums_save.start()
    dx_save.wait()
    sums_save.wait()


def summed_everywhere(*args, collective_id):
    n = PIECES
    length = SEQ * BLOCK
    own_rows = HEADS_OWN * HEAD_DIM
    dma = pltpu.SemaphoreType.DMA
    anywhere = pl.BlockSpec(memory_space=pl.ANY)
    return pl.pallas_call(
        sum_kernel,
        out_shape=[
            jax.ShapeDtypeStruct((n * PIECE, D), BF16),
            jax.ShapeDtypeStruct((BLOCK, D), BF16),
            jax.ShapeDtypeStruct((8, FF), F32),
        ],
        in_specs=[anywhere] * 9 + [pl.BlockSpec(memory_space=pltpu.VMEM)] + [anywhere] * 6,
        out_specs=[anywhere] * 3,
        scratch_shapes=[
            pltpu.VMEM((n, HALF, D), BF16),
            pltpu.VMEM((n, HALF, D), BF16),
            pltpu.VMEM((n, 2, 192, COLS), BF16),
            pltpu.VMEM((n, 2, 96, COLS), BF16),
            pltpu.VMEM((n, 2, 96, COLS), BF16),
            pltpu.VMEM((n, 2, 96, COLS), BF16),
            pltpu.VMEM((n, 2, 96, COLS), BF16),
            pltpu.VMEM((3, own_rows, length), BF16),
            pltpu.VMEM((own_rows, length), F32),
            pltpu.VMEM((HEADS_OWN, 8, length), F32),
            pltpu.VMEM((length, D), BF16),
            pltpu.VMEM((3 * D, D), BF16),
            pltpu.VMEM((SEQ, own_rows, BLOCK), BF16),
            pltpu.VMEM((SEQ, 3, own_rows, BLOCK), BF16),
            pltpu.VMEM((length, HEAD_DIM), F32),
            pltpu.VMEM((length, HEAD_DIM), F32),
            pltpu.VMEM((3, D, BLOCK), BF16),
            pltpu.VMEM((BLOCK, D), BF16),
            pltpu.VMEM((D, BLOCK), F32),
            pltpu.VMEM((D, 3 * D), BF16),
            pltpu.VMEM((BLOCK, D), BF16),
            pltpu.VMEM((2, PIECE, D), BF16),
            pltpu.VMEM((2, PIECE, D), BF16),
            pltpu.VMEM((8, FF), F32),
            dma((n,)),
            dma((16, n)),
            dma((16, n)),
            dma((2, n)),
            dma((11 + HEADS_OWN,)),
            dma((1 + HEADS_OWN, SEQ)),
            dma((1 + HEADS_OWN, SEQ)),
            dma((2, 2)),
        ],
        compiler_params=pltpu.CompilerParams(
            collective_id=collective_id, has_side_effects=True, vmem_limit_bytes=60 * 2**20
        ),
        cost_estimate=pl.CostEstimate(flops=0, bytes_accessed=n * PIECE * D * 64, transcendentals=0),
    )(*args)


def sent(value, *pairs):
    return lax.ppermute(value, "seq", pairs)


def finish_kernel(slots, total, wq, gain_ref, sums, dx_long, dx_pack, *refs):
    gd, gu, go, gq, si, sf, sh, sa, grad_out, acc, dx, load_sem, copy_sem = refs
    step = pl.program_id(0)
    loads = [
        pltpu.make_async_copy(source, dx.at[k], load_sem.at[k])
        for k, source in enumerate((dx_long, dx_pack))
    ]
    copies = [
        pltpu.make_async_copy(dx.at[k], grad_out.at[slots[k]], copy_sem.at[k]) for k in range(2)
    ]

    @pl.when(step == 0)
    def _():
        for load in loads:
            load.start()
        si[...] = (sums[2:3, 0:D] / gain_ref[:, D : 2 * D])[0]
        sf[...] = (sums[1:2, 0:D] / gain_ref[:, 2 * D : 3 * D])[0]
        sh[...] = (sums[0:1, :] / gain_ref[:, 3 * D :])[0]

    @pl.when(step == 2)
    def _():
        for load, copy in zip(loads, copies):
            load.wait()
            copy.start()

    @pl.when(step < 4)
    def _():
        gd[...] = total[...].astype(F32)

    @pl.when((step >= 4) & (step < 8))
    def _():
        gu[...] = total[...].T.astype(F32)

    @pl.when(step == 8)
    def _():
        go[...] = total[...].astype(F32)

    @pl.when(step >= 9)
    def _():
        grad = total[...].T.astype(F32)
        gq[...] = grad
        product = grad * wq[...].astype(F32)
        folded = product[:, 0:128]
        for k in range(1, D // 128):
            folded = folded + product[:, k * 128 : (k + 1) * 128]
        acc[...] = folded + jnp.where(step == 9, 0.0, acc[...])

    @pl.when(step == 11)
    def _():
        sa[...] = (jnp.sum(acc[...].T, axis=0, keepdims=True) / gain_ref[:, 0:D])[0]
        for copy in copies:
            copy.wait()


def finished(slots, total, weight, gains, sums, dx_long, dx_pack):
    square = lambda index: pl.BlockSpec((D, D), index)
    at_down = lambda i, slots: (jnp.clip(i, 0, 3), 0)
    at_up = lambda i, slots: (0, jnp.clip(i - 4, 0, 3))
    at_qkv = lambda i, slots: (0, jnp.clip(i - 9, 0, 2))
    still = lambda i, slots: (0, 0)
    once = lambda *shape: pl.BlockSpec(shape, still, pipeline_mode=pl.Buffered(1))
    row = lambda size: pl.BlockSpec((size,), lambda i, slots: (0,))
    anywhere = pl.BlockSpec(memory_space=pl.ANY)
    shapes = [(FF, D), (D, FF), (D, D), (D, 3 * D), (D,), (D,), (FF,), (D,)]
    dma = pltpu.SemaphoreType.DMA
    return pl.pallas_call(
        finish_kernel,
        grid_spec=pltpu.PrefetchScalarGridSpec(
            num_scalar_prefetch=1,
            grid=(PIECES,),
            in_specs=[square(lambda i, slots: (i, 0)), square(at_qkv)]
            + [once(1, 3 * D + FF), once(8, FF)]
            + [anywhere] * 2,
            out_specs=[square(at_down), square(at_up), square(still), square(at_qkv)]
            + [row(D), row(D), row(FF), row(D)]
            + [anywhere],
            scratch_shapes=[
                pltpu.VMEM((D, 128), F32),
                pltpu.VMEM((2, BLOCK, D), BF16),
                dma((2,)),
                dma((2,)),
            ],
        ),
        out_shape=[jax.ShapeDtypeStruct(shape, F32) for shape in shapes]
        + [jax.ShapeDtypeStruct((2, BLOCK, D), BF16)],
        compiler_params=pltpu.CompilerParams(vmem_limit_bytes=VMEM_LIMIT),
        cost_estimate=pl.CostEstimate(
            flops=2 * 10**7, bytes_accessed=46 * 2**20, transcendentals=0
        ),
    )(slots, total, weight, gains, sums, dx_long, dx_pack)


def split_layer(
    tokens,
    segment_ids,
    cotangent,
    query_key_value,
    out_weight,
    up_weight,
    down_weight,
    attend_gain,
    inner_gain,
    feed_gain,
    hidden_gain,
):
    long_first = segment_ids[0, -1] == 0
    x_long = jnp.where(long_first, tokens[0], tokens[1])
    left = sent(x_long, (0, 1), (1, 2), (2, 3))
    right = sent(x_long, (1, 0), (2, 1), (3, 2))
    long_slot = jnp.where(long_first, 0, 1).astype(jnp.int32)
    slots = jnp.stack([long_slot, 1 - long_slot])
    gains = jnp.concatenate([attend_gain, inner_gain, feed_gain, hidden_gain])[None]
    weights = (out_weight, up_weight, down_weight)
    a_pack, qkv_pack, o_pack, lse_pack, x_pack = pack_forward(
        slots[1:], tokens, query_key_value, gains
    )
    o_pack, left, right = lax.optimization_barrier((o_pack, left, right))
    left_two = sent(left, (1, 2), (2, 3))
    right_two = sent(right, (1, 0), (2, 1))
    across = sent(jnp.where(lax.axis_index("seq") == 1, left, right), (1, 3), (2, 0))
    output, dh_pack, do_pack, go_pack, gd_pack, gu_pack = feed_both(
        slots[1:], o_pack, tokens, cotangent, gains, weights
    )
    *x_far, do_pack = lax.optimization_barrier((left_two, right_two, across, do_pack))
    a_all, qkv_long, o_long, lse_long, o_mine, gq_pack, dx_pack = long_forward(
        (x_long, left, right, *x_far),
        query_key_value,
        gains,
        (qkv_pack, o_pack, lse_pack, do_pack, a_pack, x_pack, dh_pack),
        1,
    )
    output, dh_long, do_long, go, gd, gu = feed_both(
        slots[:1],
        o_mine,
        tokens,
        cotangent,
        gains,
        weights,
        (gd_pack, gu_pack, go_pack),
        output,
    )
    total, dx_long, sums = summed_everywhere(
        gd,
        gu,
        go,
        gq_pack,
        do_long.reshape(SEQ, HEADS_OWN * HEAD_DIM, BLOCK),
        qkv_long,
        o_long,
        lse_long,
        a_all,
        gains,
        x_long,
        dh_long,
        down_weight,
        up_weight,
        out_weight,
        query_key_value,
        collective_id=0,
    )
    down_grad, up_grad, out_grad, qkv_grad, *sums, tokens_grad = finished(
        slots, total, query_key_value, gains, sums, dx_long, dx_pack
    )
    inner_total, feed_total, hidden_total, attend_total = sums
    return (
        output,
        tokens_grad,
        qkv_grad,
        out_grad,
        up_grad,
        down_grad,
        attend_total,
        inner_total,
        feed_total,
        hidden_total,
    )


def per_device(tokens, *others):
    split = lax.axis_size("seq") == SEQ and lax.axis_size("rows") == 8
    if split and tokens.shape == (2, BLOCK, D):
        return split_layer(tokens, *others)
    return ring_layer(tokens, *others)


def solution(mesh):
    return jax.shard_map(
        per_device,
        mesh=mesh,
        in_specs=(
            P("rows", "seq", None),
            P("rows", None),
            P("rows", "seq", None),
            P(),
            P(),
            P(),
            P(),
            P(),
            P(),
            P(),
            P(),
        ),
        out_specs=(
            P("rows", "seq", None),
            P("rows", "seq", None),
            P(),
            P(),
            P(),
            P(),
            P(),
            P(),
            P(),
            P(),
        ),
        check_vma=False,
    )
```

```python
import functools
import math

import jax
import jax.numpy as jnp
from jax import lax
from jax.experimental import pallas as pl
from jax.experimental.pallas import tpu as pltpu
from jax.sharding import PartitionSpec as P

D = 768
HEADS = 12
HEAD_DIM = 64


EPSILON = 1e-05
MASKED = -1e30


def passed_along(value, axis, steps):
    count = lax.axis_size(axis)
    initial, last = (max(0, -steps), min(count, count - steps))
    return lax.ppermute(value, axis, [(source, source + steps) for source in range(initial, last)])


def from_behind(value, axis, steps):
    count = lax.axis_size(axis)
    pairs = [(source, (source + steps) % count) for source in range(count)]
    return lax.ppermute(value, axis, pairs)


def layer_norm(values, gain):
    average = jnp.mean(values, axis=-1, keepdims=True)
    centred = values - average
    inverse = lax.rsqrt(jnp.mean(centred * centred, axis=-1, keepdims=True) + EPSILON)
    normed = centred * inverse
    return (normed * gain, normed, inverse)


def norm_back(upstream, normed, inverse, gain):
    scaled = upstream * gain
    spread = (
        scaled
        - jnp.mean(scaled, axis=-1, keepdims=True)
        - normed * jnp.mean(scaled * normed, axis=-1, keepdims=True)
    )
    return (spread * inverse, jnp.sum(upstream * normed, axis=0))


def gelu_exact(values):
    return jax.nn.gelu(values, approximate=False)


def matmul(left, right):
    return jnp.dot(left, right, preferred_element_type=jnp.float32)


def left_t(left, right):
    return lax.dot_general(
        left, right, (((0,), (0,)), ((), ())), preferred_element_type=jnp.float32
    )


def right_t(left, right):
    return lax.dot_general(
        left, right, (((1,), (1,)), ((), ())), preferred_element_type=jnp.float32
    )


def split_heads(values):
    return values.reshape(values.shape[0], values.shape[1], HEADS, HEAD_DIM)


def allowed_pairs(query_pos, query_seg, key_pos, key_seg):
    causal = key_pos[None, None, None, :] <= query_pos[None, None, :, None]
    same_doc = key_seg[:, None, None, :] == query_seg[:, None, :, None]
    return causal & same_doc


def scores(queries, key_rows):
    return jnp.einsum(
        "rqhd,rkhd->rhqk",
        split_heads(queries),
        split_heads(key_rows),
        preferred_element_type=jnp.float32,
    ) * HEAD_DIM ** (-0.5)


def fold_keys(carry, piece, queries, query_pos, query_seg, segment_ids):
    key_rows, value_rows = piece
    row_count = key_rows.shape[0]
    key_count = key_rows.shape[1]
    block_width = math.gcd(key_count, queries.shape[1])
    block_count = key_count // block_width
    key_blocks = key_rows.reshape(row_count, block_count, block_width, D).transpose(1, 0, 2, 3)
    value_blocks = value_rows.reshape(row_count, block_count, block_width, D).transpose(1, 0, 2, 3)

    def one_block(state, block_item):
        accum, running, softmax_total = state
        key_block, value_block, offset = block_item
        key_start = offset * block_width
        key_pos = key_start + jnp.arange(block_width, dtype=jnp.int32)
        key_seg = lax.dynamic_slice_in_dim(segment_ids, key_start, block_width, 1)
        allowed = allowed_pairs(query_pos, query_seg, key_pos, key_seg)
        logits = jnp.where(allowed, scores(queries, key_block), MASKED)
        new_peak = jnp.maximum(running, jnp.max(logits, axis=-1))
        weights = jnp.where(allowed, jnp.exp(logits - new_peak[..., None]), 0.0)
        factor = jnp.exp(running - new_peak)
        softmax_total = softmax_total * factor + jnp.sum(weights, axis=-1)
        accum = accum * factor[..., None] + jnp.einsum(
            "rhqk,rkhd->rhqd",
            weights.astype(jnp.bfloat16),
            split_heads(value_block),
            preferred_element_type=jnp.float32,
        )
        return ((accum, new_peak, softmax_total), None)

    carry, unused = lax.scan(
        one_block, carry, (key_blocks, value_blocks, jnp.arange(block_count, dtype=jnp.int32))
    )
    return carry


def back_block(queries, grad_rows, log_total, delta, key_rows, value_rows, allowed):
    logits = jnp.where(allowed, scores(queries, key_rows), MASKED)
    probs = jnp.where(allowed, jnp.exp(logits - log_total[..., None]), 0.0)
    dprobs = jnp.einsum(
        "rqhd,rkhd->rhqk",
        split_heads(grad_rows),
        split_heads(value_rows),
        preferred_element_type=jnp.float32,
    )
    dlogits = (probs * (dprobs - delta[..., None])).astype(jnp.bfloat16)
    factor = HEAD_DIM ** (-0.5)
    query_part = (
        jnp.einsum(
            "rhqk,rkhd->rqhd", dlogits, split_heads(key_rows), preferred_element_type=jnp.float32
        )
        * factor
    )
    key_part = (
        jnp.einsum(
            "rhqk,rqhd->rkhd", dlogits, split_heads(queries), preferred_element_type=jnp.float32
        )
        * factor
    )
    value_part = jnp.einsum(
        "rhqk,rqhd->rkhd",
        probs.astype(jnp.bfloat16),
        split_heads(grad_rows),
        preferred_element_type=jnp.float32,
    )
    return (
        query_part.reshape(queries.shape),
        key_part.reshape(key_rows.shape),
        value_part.reshape(value_rows.shape),
    )


def ring_layer(
    tokens,
    segment_ids,
    cotangent,
    query_key_value,
    out_weight,
    up_weight,
    down_weight,
    attend_gain,
    inner_gain,
    feed_gain,
    hidden_gain,
):
    row_count = tokens.shape[0]
    width_q = tokens.shape[1]
    model_width = tokens.shape[2]
    token_count = row_count * width_q
    seq_index = lax.axis_index("seq")
    seq_size = lax.axis_size("seq")
    local_pos = seq_index * width_q + jnp.arange(width_q, dtype=jnp.int32)
    local_seg = lax.dynamic_slice_in_dim(segment_ids, seq_index * width_q, width_q, 1)
    residual = tokens.reshape(token_count, model_width).astype(jnp.float32)
    attend_out, attend_normed, attend_inverse = layer_norm(residual, attend_gain)
    attend_low = attend_out.astype(jnp.bfloat16)
    projected = matmul(attend_low, query_key_value).astype(jnp.bfloat16)
    queries = projected[:, :model_width].reshape(row_count, width_q, model_width)
    key_rows = projected[:, model_width : 2 * model_width].reshape(row_count, width_q, model_width)
    value_rows = projected[:, 2 * model_width :].reshape(row_count, width_q, model_width)
    start_state = (
        jnp.zeros((row_count, HEADS, width_q, HEAD_DIM), jnp.float32),
        jnp.full((row_count, HEADS, width_q), MASKED, jnp.float32),
        jnp.zeros((row_count, HEADS, width_q), jnp.float32),
    )
    accum, running, softmax_total = fold_keys(
        start_state,
        (
            lax.all_gather(key_rows, "seq", axis=1, tiled=True),
            lax.all_gather(value_rows, "seq", axis=1, tiled=True),
        ),
        queries,
        local_pos,
        local_seg,
        segment_ids,
    )
    log_total = running + jnp.log(softmax_total)
    attended = (accum / softmax_total[..., None]).transpose(0, 2, 1, 3)
    attended_flat = attended.reshape(token_count, model_width)
    inner_out, inner_normed, inner_inverse = layer_norm(attended_flat, inner_gain)
    inner_low = inner_out.astype(jnp.bfloat16)
    state = residual + matmul(inner_low, out_weight)
    feed_out, feed_normed, feed_inverse = layer_norm(state, feed_gain)
    feed_low = feed_out.astype(jnp.bfloat16)
    pre_act = matmul(feed_low, up_weight)
    hidden, gelu_back = jax.vjp(gelu_exact, pre_act)
    hidden_out, hidden_normed, hidden_inverse = layer_norm(hidden, hidden_gain)
    hidden_low = hidden_out.astype(jnp.bfloat16)
    result = state + matmul(hidden_low, down_weight)
    output = result.astype(jnp.bfloat16).reshape(tokens.shape)
    upstream_low = cotangent.reshape(token_count, model_width)
    upstream = upstream_low.astype(jnp.float32)
    down_term = left_t(hidden_low, upstream_low)
    hidden_grad, hidden_gain_term = norm_back(
        right_t(upstream_low, down_weight), hidden_normed, hidden_inverse, hidden_gain
    )
    pre_grad = gelu_back(hidden_grad)[0]
    pre_low = pre_grad.astype(jnp.bfloat16)
    up_term = left_t(feed_low, pre_low)
    feed_grad, feed_gain_term = norm_back(
        right_t(pre_low, up_weight), feed_normed, feed_inverse, feed_gain
    )
    state_grad = upstream + feed_grad
    state_low = state_grad.astype(jnp.bfloat16)
    out_term = left_t(inner_low, state_low)
    inner_grad, inner_gain_term = norm_back(
        right_t(state_low, out_weight), inner_normed, inner_inverse, inner_gain
    )
    attend_grad_low = inner_grad.astype(jnp.bfloat16).reshape(row_count, width_q, model_width)
    delta = jnp.sum(split_heads(attend_grad_low).astype(jnp.float32) * attended, axis=-1).transpose(
        0, 2, 1
    )
    zero_rows = jnp.zeros((row_count, width_q, model_width), jnp.float32)

    def key_step(step_count, cycle_state):
        moving_keys, moving_values, moving_dkeys, moving_dvalues, query_acc = cycle_state
        source = jnp.remainder(seq_index - step_count, seq_size)
        key_start = source * width_q
        key_pos = key_start + jnp.arange(width_q, dtype=jnp.int32)
        key_seg = lax.dynamic_slice_in_dim(segment_ids, key_start, width_q, 1)
        allowed = allowed_pairs(local_pos, local_seg, key_pos, key_seg)
        query_part, key_part, value_part = back_block(
            queries, attend_grad_low, log_total, delta, moving_keys, moving_values, allowed
        )
        moving_keys, moving_values = passed_along((moving_keys, moving_values), "seq", 1)
        moving_dkeys, moving_dvalues = (
            from_behind((moving_dkeys + key_part).astype(jnp.bfloat16), "seq", 1).astype(
                jnp.float32
            ),
            from_behind((moving_dvalues + value_part).astype(jnp.bfloat16), "seq", 1).astype(
                jnp.float32
            ),
        )
        return (moving_keys, moving_values, moving_dkeys, moving_dvalues, query_acc + query_part)

    cycle_out = lax.fori_loop(
        0, seq_size, key_step, (key_rows, value_rows, zero_rows, zero_rows, zero_rows)
    )
    key_grad, value_grad, query_grad = (cycle_out[2], cycle_out[3], cycle_out[4])
    joined_grad = jnp.concatenate(
        [
            query_grad.astype(jnp.bfloat16),
            key_grad.astype(jnp.bfloat16),
            value_grad.astype(jnp.bfloat16),
        ],
        axis=-1,
    ).reshape(token_count, 3 * model_width)
    qkv_term = left_t(attend_low, joined_grad)
    attend_back, attend_gain_term = norm_back(
        right_t(joined_grad, query_key_value), attend_normed, attend_inverse, attend_gain
    )
    tokens_grad = (state_grad + attend_back).astype(jnp.bfloat16).reshape(tokens.shape)
    all_sectioned = (
        lax.psum_scatter(
            qkv_term.astype(jnp.bfloat16), "rows", scatter_dimension=0, tiled=True
        ).astype(jnp.float32),
        lax.psum_scatter(
            out_term.astype(jnp.bfloat16), "rows", scatter_dimension=0, tiled=True
        ).astype(jnp.float32),
        lax.psum_scatter(
            up_term.astype(jnp.bfloat16), "rows", scatter_dimension=0, tiled=True
        ).astype(jnp.float32),
        lax.psum_scatter(
            down_term.astype(jnp.bfloat16), "rows", scatter_dimension=0, tiled=True
        ).astype(jnp.float32),
    )
    seq_sectioned = (
        lax.psum_scatter(
            all_sectioned[0].astype(jnp.bfloat16), "seq", scatter_dimension=1, tiled=True
        ).astype(jnp.float32),
        lax.psum_scatter(
            all_sectioned[1].astype(jnp.bfloat16), "seq", scatter_dimension=1, tiled=True
        ).astype(jnp.float32),
        lax.psum_scatter(
            all_sectioned[2].astype(jnp.bfloat16), "seq", scatter_dimension=1, tiled=True
        ).astype(jnp.float32),
        lax.psum_scatter(
            all_sectioned[3].astype(jnp.bfloat16), "seq", scatter_dimension=1, tiled=True
        ).astype(jnp.float32),
    )
    seq_whole = (
        lax.all_gather(seq_sectioned[0].astype(jnp.bfloat16), "seq", axis=1, tiled=True).astype(
            jnp.float32
        ),
        lax.all_gather(seq_sectioned[1].astype(jnp.bfloat16), "seq", axis=1, tiled=True).astype(
            jnp.float32
        ),
        lax.all_gather(seq_sectioned[2].astype(jnp.bfloat16), "seq", axis=1, tiled=True).astype(
            jnp.float32
        ),
        lax.all_gather(seq_sectioned[3].astype(jnp.bfloat16), "seq", axis=1, tiled=True).astype(
            jnp.float32
        ),
    )
    qkv_grad, out_grad, up_grad, down_grad = (
        lax.all_gather(seq_whole[0].astype(jnp.bfloat16), "rows", axis=0, tiled=True).astype(
            jnp.float32
        ),
        lax.all_gather(seq_whole[1].astype(jnp.bfloat16), "rows", axis=0, tiled=True).astype(
            jnp.float32
        ),
        lax.all_gather(seq_whole[2].astype(jnp.bfloat16), "rows", axis=0, tiled=True).astype(
            jnp.float32
        ),
        lax.all_gather(seq_whole[3].astype(jnp.bfloat16), "rows", axis=0, tiled=True).astype(
            jnp.float32
        ),
    )
    attend_total, inner_total, feed_total, hidden_total = lax.psum(
        (attend_gain_term, inner_gain_term, feed_gain_term, hidden_gain_term), ("rows", "seq")
    )
    return (
        output,
        tokens_grad,
        qkv_grad,
        out_grad,
        up_grad,
        down_grad,
        attend_total,
        inner_total,
        feed_total,
        hidden_total,
    )


FF = 3072
SEQ = 4
BLOCK = 512
SPLIT = BLOCK // 2
TOGETHER = 2
HEADS_OWN = HEADS // SEQ
GROUP = HEADS_OWN * 3 * HEAD_DIM
MESH = pl.DeviceIdType.MESH
F32 = jnp.float32
BF16 = jnp.bfloat16
VMEM_LIMIT = 56 * 2**20


def causal_mask(key_start, key_count, query_count):
    key_pos = lax.broadcasted_iota(jnp.int32, (key_count, query_count), 0) + key_start
    query_pos = lax.broadcasted_iota(jnp.int32, (key_count, query_count), 1)
    return key_pos <= query_pos


def attend_head(read, write, block_count):
    for query_block in range(block_count):
        here = slice(query_block * BLOCK, (query_block + 1) * BLOCK)
        queries = (read(0, here).astype(F32) * 0.125).astype(BF16)
        peak = jnp.full((1, BLOCK), MASKED, F32)
        total = jnp.zeros((1, BLOCK), F32)
        accum = jnp.zeros((HEAD_DIM, BLOCK), F32)
        for key_block in range(query_block):
            there = slice(key_block * BLOCK, (key_block + 1) * BLOCK)
            logits = matmul(read(1, there).T, queries)
            new_peak = jnp.maximum(peak, jnp.max(logits, axis=0, keepdims=True))
            weights = jnp.exp(logits - new_peak)
            factor = jnp.exp(peak - new_peak)
            total = total * factor + jnp.sum(weights, axis=0, keepdims=True)
            accum = accum * factor + matmul(read(2, there), weights.astype(BF16))
            peak = new_peak
        keys = read(1, here).T
        values = read(2, here)
        logits = jnp.where(
            causal_mask(0, SPLIT, BLOCK), matmul(keys[:SPLIT], queries), MASKED
        )
        corner = jnp.where(
            causal_mask(0, SPLIT, SPLIT), matmul(keys[SPLIT:], queries[:, SPLIT:]), MASKED
        )
        new_peak = jnp.maximum(peak, jnp.max(logits, axis=0, keepdims=True))
        late_peak = jnp.maximum(new_peak[:, SPLIT:], jnp.max(corner, axis=0, keepdims=True))
        new_peak = jnp.concatenate([new_peak[:, :SPLIT], late_peak], axis=1)
        weights = jnp.exp(logits - new_peak)
        corner = jnp.exp(corner - late_peak)
        factor = jnp.exp(peak - new_peak)
        total = total * factor + jnp.sum(weights, axis=0, keepdims=True)
        accum = accum * factor + matmul(values[:, :SPLIT], weights.astype(BF16))
        corner_total = jnp.sum(corner, axis=0, keepdims=True)
        corner_accum = matmul(values[:, SPLIT:], corner.astype(BF16))
        total = jnp.concatenate([total[:, :SPLIT], total[:, SPLIT:] + corner_total], axis=1)
        accum = jnp.concatenate([accum[:, :SPLIT], accum[:, SPLIT:] + corner_accum], axis=1)
        write(query_block, here, accum / total, new_peak + jnp.log(total))


def norm_in(x, gain):
    average = jnp.mean(x, axis=-1, keepdims=True)
    centred = x - average
    inverse = lax.rsqrt(jnp.mean(centred * centred, axis=-1, keepdims=True) + EPSILON)
    return (centred * inverse * gain).astype(BF16)


def pack_kernel(slot_ref, x_ref, w_ref, gain_ref, a_ref, qkv_ref, o_ref, lse_ref, x_out, at):
    h = pl.program_id(0)

    @pl.when(h == 0)
    def _():
        x_out[...] = x_ref[0]
        a = norm_in(x_ref[0].astype(F32), gain_ref[:, 0:D])
        a_ref[...] = a
        at[...] = a.T
        for part in range(3):
            for k in range(0, D, 256):
                columns = slice(part * D + k, part * D + k + 256)
                qkv_ref[part, k : k + 256, :] = left_t(w_ref[:, columns], at[...]).astype(BF16)

    for sub in range(TOGETHER):
        start = (h * TOGETHER + sub) * HEAD_DIM
        rows = pl.ds(pl.multiple_of(start, HEAD_DIM), HEAD_DIM)

        def write(query_block, here, o, lse):
            o_ref[sub * HEAD_DIM : (sub + 1) * HEAD_DIM, :] = o
            lse_ref[8 * sub : 8 * sub + 1, :] = lse

        attend_head(lambda part, columns: qkv_ref[part, rows, :], write, 1)


def pack_forward(slot, tokens, weight, gain):
    still = lambda *shape: pl.BlockSpec(shape, lambda h, slot: (0,) * len(shape))
    once = lambda *shape: pl.BlockSpec(
        shape, lambda h, slot: (0,) * len(shape), pipeline_mode=pl.Buffered(1)
    )
    by_head = lambda rows: pl.BlockSpec((TOGETHER * rows, BLOCK), lambda h, slot: (h, 0))
    return pl.pallas_call(
        pack_kernel,
        grid_spec=pltpu.PrefetchScalarGridSpec(
            num_scalar_prefetch=1,
            grid=(HEADS // TOGETHER,),
            in_specs=[
                pl.BlockSpec((1, BLOCK, D), lambda h, slot: (slot[0], 0, 0)),
                once(D, 3 * D),
                once(1, 3 * D + FF),
            ],
            out_specs=[still(BLOCK, D), still(3, D, BLOCK), by_head(HEAD_DIM), by_head(8)]
            + [still(BLOCK, D)],
            scratch_shapes=[pltpu.VMEM((D, BLOCK), BF16)],
        ),
        out_shape=[
            jax.ShapeDtypeStruct((BLOCK, D), BF16),
            jax.ShapeDtypeStruct((3, D, BLOCK), BF16),
            jax.ShapeDtypeStruct((D, BLOCK), F32),
            jax.ShapeDtypeStruct((HEADS * 8, BLOCK), F32),
            jax.ShapeDtypeStruct((BLOCK, D), BF16),
        ],
        compiler_params=pltpu.CompilerParams(vmem_limit_bytes=VMEM_LIMIT),
        cost_estimate=pl.CostEstimate(
            flops=8 * 10**9, bytes_accessed=10 * 2**20, transcendentals=HEADS * BLOCK * BLOCK
        ),
    )(slot, tokens, weight, gain)


def widened(gain, width):
    return jnp.concatenate([gain] * (width // 128), axis=1)


def column_stats(values):
    size = values.shape[0]
    average = jnp.sum(values, axis=0, keepdims=True) * (1.0 / size)
    centred = values - average
    spread = jnp.sum(centred * centred, axis=0, keepdims=True) * (1.0 / size)
    return average, lax.rsqrt(spread + EPSILON)


def gelu_both(values):
    t = 1.0 / (1.0 + (0.3275911 * 0.7071067811865476) * jnp.abs(values))
    density = jnp.exp(-0.5 * (values * values))
    tail = 0.5 * -1.453152027 + t * (0.5 * 1.061405429)
    tail = 0.5 * 1.421413741 + t * tail
    tail = 0.5 * -0.284496736 + t * tail
    tail = 0.5 * 0.254829592 + t * tail
    tail = tail * t * density
    below = jnp.where(values >= 0, 1.0 - tail, tail)
    return values * below, below + values * (density * 0.3989422804014327)


def feed_kernel(steps, chunk, sub, has_partial, slot, *refs):
    names = iter(refs)
    take = lambda count: [next(names) for _ in range(count)]
    o_in, x_in, dy_in, gain_ref, wo_in, wu_in, wd_in = take(7)
    part_in = take(3) if has_partial else []
    if has_partial:
        take(1)
    out_to, dh_to, do_to, go_to, gd_ref, gu_ref = take(6)
    o_ref, x_ref, dy_ref, wo, wu, wd, out_s, dh_s, do_s, go_s = take(10)
    ig, fg, hg, b_s, h_s, c_s, cn_s, dyt_s, n_s, slope_s, t_s, sum_s, dc_s, st = take(14)
    parts, part_o = take(2) if has_partial else (None, None)
    load_sem, wu_sem, wd_sem, part_sem, save_sem = take(5)
    width = BLOCK
    step = pl.program_id(0)
    o_load = pltpu.make_async_copy(o_in, o_ref, load_sem.at[0])
    wo_load = pltpu.make_async_copy(wo_in, wo, load_sem.at[1])
    x_load = pltpu.make_async_copy(x_in.at[slot[0]], x_ref, load_sem.at[2])
    dy_load = pltpu.make_async_copy(dy_in.at[slot[0]], dy_ref, load_sem.at[3])

    def span(k):
        return pl.ds(pl.multiple_of(k * chunk, chunk), chunk)

    def wu_load(k):
        return pltpu.make_async_copy(wu_in.at[:, span(k)], wu.at[:, span(k)], wu_sem.at[k])

    def wd_load(k):
        return pltpu.make_async_copy(wd_in.at[span(k), :], wd.at[span(k), :], wd_sem.at[k])

    def part_load(which, k):
        return pltpu.make_async_copy(
            part_in[which].at[span(k), :], parts.at[k], part_sem.at[which, k]
        )

    def save(k):
        source, target = [(out_s, out_to.at[slot[0]]), (dh_s, dh_to), (do_s, do_to), (go_s, go_to)][k]
        return pltpu.make_async_copy(source, target, save_sem.at[k])

    @pl.when(step == 0)
    def _():
        for load in (o_load, wo_load, x_load):
            load.start()
        ig[...] = jnp.broadcast_to(gain_ref[:, D : 2 * D], (128, D)).T
        fg[...] = jnp.broadcast_to(gain_ref[:, 2 * D : 3 * D], (128, D)).T
        hg[...] = jnp.broadcast_to(gain_ref[:, 3 * D :], (128, FF)).T
        o_load.wait()
        o = o_ref[...].astype(F32)
        average, inverse = column_stats(o)
        b = ((o - average) * inverse * widened(ig[...], width)).astype(BF16)
        b_s[...] = b
        st[0:1] = average
        st[1:2] = inverse
        wo_load.wait()
        x_load.wait()
        wu_load(0).start()
        dy_load.start()
        h = x_ref[...].T.astype(F32) + left_t(wo[...], b)
        h_s[...] = h
        average, inverse = column_stats(h)
        st[2:3] = average
        st[3:4] = inverse
        c = ((h - average) * inverse * widened(fg[...], width)).astype(BF16)
        c_s[...] = c
        cn_s[...] = c.T
        dy_load.wait()
        dyt_s[...] = dy_ref[...].T
        for k in range(1, steps):
            wu_load(k).start()
        for k in range(steps):
            wd_load(k).start()
        if has_partial:
            for k in range(steps):
                part_load(0, k).start()
            pltpu.make_async_copy(part_in[2], part_o, load_sem.at[4]).start()

    @pl.when(step < steps)
    def _():
        wu_load(step).wait()
        base = pl.multiple_of(step * chunk, chunk)
        for k in range(chunk // sub):
            u = left_t(wu[:, pl.ds(base + k * sub, sub)], c_s[...])
            z, slope = gelu_both(u)
            n_s[pl.ds(base + k * sub, sub), :] = z
            slope_s[pl.ds(base + k * sub, sub), :] = slope.astype(BF16)

    @pl.when(step == steps - 1)
    def _():
        total = jnp.zeros((1, width), F32)
        for k in range(FF // sub):
            total = total + jnp.sum(n_s[k * sub : (k + 1) * sub, :], axis=0, keepdims=True)
        average = total * (1.0 / FF)
        total = jnp.zeros((1, width), F32)
        for k in range(FF // sub):
            centred = n_s[k * sub : (k + 1) * sub, :] - average
            total = total + jnp.sum(centred * centred, axis=0, keepdims=True)
        st[4:5] = average
        st[5:6] = lax.rsqrt(total * (1.0 / FF) + EPSILON)
        st[6:8] = jnp.zeros((2, width), F32)
        sum_s[...] = h_s[...]

    @pl.when((step >= steps) & (step < 2 * steps))
    def _():
        turn = step - steps
        wd_load(turn).wait()
        if has_partial:
            part_load(0, turn).wait()
        base = pl.multiple_of(turn * chunk, chunk)
        average = st[4:5]
        inverse = st[5:6]
        first = jnp.zeros((1, width), F32)
        second = jnp.zeros((1, width), F32)
        pieces = []
        for k in range(chunk // sub):
            rows = slice(k * sub, (k + 1) * sub)
            here = pl.ds(base + k * sub, sub)
            n = (n_s[here, :] - average) * inverse
            n_s[here, :] = n
            gain = widened(hg[here, :], width)
            e = (n * gain).astype(BF16)
            pieces.append(e)
            t = matmul(wd[here, :], dyt_s[...]) * gain
            t_s[here, :] = t
            first = first + jnp.sum(t, axis=0, keepdims=True)
            second = second + jnp.sum(t * n, axis=0, keepdims=True)
            grad = matmul(e, dy_ref[...])
            if has_partial:
                grad = grad + parts[turn, rows, :].astype(F32)
            gd_ref[rows, :] = grad.astype(BF16)
        sum_s[...] += left_t(wd[pl.ds(base, chunk), :], jnp.concatenate(pieces, axis=0))
        st[6:7] += first
        st[7:8] += second
        if has_partial:
            part_load(1, turn).start()

    @pl.when(step == 2 * steps - 1)
    def _():
        out_s[...] = sum_s[...].astype(BF16).T
        save(0).start()
        st[6:8] = st[6:8] * (1.0 / FF)
        dc_s[...] = jnp.zeros_like(dc_s)

    @pl.when(step >= 2 * steps)
    def _():
        turn = step - 2 * steps
        if has_partial:
            part_load(1, turn).wait()
        base = pl.multiple_of(turn * chunk, chunk)
        inverse = st[5:6]
        first = st[6:7]
        second = st[7:8]
        pieces = []
        for k in range(chunk // sub):
            rows = slice(k * sub, (k + 1) * sub)
            here = pl.ds(base + k * sub, sub)
            n = n_s[here, :]
            du = ((t_s[here, :] - first - n * second) * inverse * slope_s[here, :].astype(F32)).astype(BF16)
            pieces.append(du)
            grad = matmul(du, cn_s[...])
            if has_partial:
                grad = grad + parts[turn, rows, :].astype(F32)
            gu_ref[rows, :] = grad.astype(BF16)
        dc_s[...] += matmul(wu[:, pl.ds(base, chunk)], jnp.concatenate(pieces, axis=0))

    @pl.when(step == 3 * steps - 1)
    def _():
        n = (h_s[...] - st[2:3]) * st[3:4]
        t = dc_s[...] * widened(fg[...], width)
        first = jnp.sum(t, axis=0, keepdims=True) * (1.0 / D)
        second = jnp.sum(t * n, axis=0, keepdims=True) * (1.0 / D)
        dh = dyt_s[...].astype(F32) + (t - first - n * second) * st[3:4]
        dh_s[...] = dh
        save(1).start()
        dh_low = dh.astype(BF16)
        n = (o_ref[...].astype(F32) - st[0:1]) * st[1:2]
        t = matmul(wo[...], dh_low) * widened(ig[...], width)
        first = jnp.sum(t, axis=0, keepdims=True) * (1.0 / D)
        second = jnp.sum(t * n, axis=0, keepdims=True) * (1.0 / D)
        do_s[...] = ((t - first - n * second) * st[1:2]).astype(BF16)
        save(2).start()
        grad = matmul(b_s[...], dh_low.T)
        if has_partial:
            pltpu.make_async_copy(part_in[2], part_o, load_sem.at[4]).wait()
            grad = grad + part_o[...].astype(F32)
        go_s[...] = grad.astype(BF16)
        save(3).start()
        for k in range(4):
            save(k).wait()


def feed_both(slot, o_t, tokens, cotangent, gains, weights, partial=None, output=None, chunk=1536, sub=256):
    width = BLOCK
    steps = FF // chunk
    has_partial = partial is not None
    anywhere = pl.BlockSpec(memory_space=pl.ANY)
    second = lambda i, slot: (jnp.clip(i - steps, 0, steps - 1), 0)
    third = lambda i, slot: (jnp.clip(i - 2 * steps, 0, steps - 1), 0)
    dma = pltpu.SemaphoreType.DMA
    scratch = [
        pltpu.VMEM((D, width), o_t.dtype),
        pltpu.VMEM((width, D), BF16),
        pltpu.VMEM((width, D), BF16),
        pltpu.VMEM((D, D), BF16),
        pltpu.VMEM((D, FF), BF16),
        pltpu.VMEM((FF, D), BF16),
        pltpu.VMEM((width, D), BF16),
        pltpu.VMEM((D, width), F32),
        pltpu.VMEM((D, width), BF16),
        pltpu.VMEM((D, D), BF16),
        pltpu.VMEM((D, 128), F32),
        pltpu.VMEM((D, 128), F32),
        pltpu.VMEM((FF, 128), F32),
        pltpu.VMEM((D, width), BF16),
        pltpu.VMEM((D, width), F32),
        pltpu.VMEM((D, width), BF16),
        pltpu.VMEM((width, D), BF16),
        pltpu.VMEM((D, width), BF16),
        pltpu.VMEM((FF, width), F32),
        pltpu.VMEM((FF, width), BF16),
        pltpu.VMEM((FF, width), F32),
        pltpu.VMEM((D, width), F32),
        pltpu.VMEM((D, width), F32),
        pltpu.VMEM((8, width), F32),
    ]
    args = [o_t, tokens, cotangent, gains, *weights]
    if has_partial:
        args += [*partial, output]
        scratch += [pltpu.VMEM((steps, chunk, D), BF16), pltpu.VMEM((D, D), BF16)]
    scratch += [dma((5,)), dma((steps,)), dma((steps,)), dma((2, steps)), dma((4,))]
    return pl.pallas_call(
        functools.partial(feed_kernel, steps, chunk, sub, has_partial),
        grid_spec=pltpu.PrefetchScalarGridSpec(
            num_scalar_prefetch=1,
            grid=(3 * steps,),
            in_specs=[anywhere] * 3
            + [pl.BlockSpec(gains.shape, lambda i, slot: (0, 0), pipeline_mode=pl.Buffered(1))]
            + [anywhere] * (len(args) - 4),
            out_specs=[anywhere] * 4
            + [pl.BlockSpec((chunk, D), second), pl.BlockSpec((chunk, D), third)],
            scratch_shapes=scratch,
        ),
        input_output_aliases={len(args): 0} if has_partial else {},
        out_shape=[
            jax.ShapeDtypeStruct((2, width, D), BF16),
            jax.ShapeDtypeStruct((D, width), F32),
            jax.ShapeDtypeStruct((D, width), BF16),
            jax.ShapeDtypeStruct((D, D), BF16),
            jax.ShapeDtypeStruct((FF, D), BF16),
            jax.ShapeDtypeStruct((FF, D), BF16),
        ],
        compiler_params=pltpu.CompilerParams(vmem_limit_bytes=62 * 2**20),
        cost_estimate=pl.CostEstimate(
            flops=6 * width * D * (D + 2 * FF), bytes_accessed=50 * 2**20, transcendentals=width * FF
        ),
    )(slot, *args)


def long_kernel(*refs):
    own_x, left, right, left_two, right_two, across, w_ref, gain_ref = refs[:8]
    qkv_ref, o_ref, lse_ref, do_ref, a_ref, x_ref, dh_ref = refs[8:15]
    a_out, qkv_out, o_out, lse_out, mine_out, gq_out, dx_out = refs[15:22]
    a_all, qkv, o_own, lse_own, o_low, w, qp, op, lp, dop, ap, xp, dhp, dp, gq, dx = refs[22:38]
    x_all, w_near, w_own, load_sem, save_sem, swap_send, swap_recv = refs[38:]
    gain_row = gain_ref[:, 0:D]
    r = lax.axis_index("rows")
    s = lax.axis_index("seq")
    shifted = [(r, (s + shift) % SEQ) for shift in range(SEQ)]
    barrier = pltpu.get_barrier_semaphore()
    for device in shifted[1:]:
        pl.semaphore_signal(barrier, inc=1, device_id=device, device_id_type=MESH)
    pl.semaphore_wait(barrier, SEQ - 1)
    sources = [qkv_ref, o_ref, lse_ref, do_ref, a_ref, x_ref, dh_ref, w_ref]
    targets = [qp, op, lp, dop, ap, xp, dhp, w]
    loads = [
        pltpu.make_async_copy(source, target, load_sem.at[k])
        for k, (source, target) in enumerate(zip(sources, targets))
    ]
    nears = [
        pltpu.make_async_copy(
            w_ref.at[:, pl.ds(pl.multiple_of(part * D + (3 * s // 2) * 128, 128), 256)],
            w_near.at[part],
            load_sem.at[8 + part],
        )
        for part in range(3)
    ]
    x_from = [
        [own_x, right, right_two, across],
        [left, own_x, right, right_two],
        [left_two, left, own_x, right],
        [across, left_two, left, own_x],
    ]

    def x_load(k, j):
        return pltpu.make_async_copy(x_from[k][j], x_all.at[j], load_sem.at[11 + j])

    for k in range(SEQ):

        @pl.when(s == k)
        def _():
            for j in range(SEQ):
                x_load(k, j).start()

    for load in nears + loads:
        load.start()
    saves = [
        pltpu.make_async_copy(source, target, save_sem.at[k])
        for k, (source, target) in enumerate(
            [(a_all, a_out), (qkv, qkv_out), (o_own, o_out), (lse_own, lse_out)]
            + [(gq, gq_out), (dx, dx_out)]
        )
    ]

    def o_copy(h, shift):
        part = o_low.at[(s + shift) % SEQ, pl.ds(h * HEAD_DIM, HEAD_DIM), :]
        place = pl.ds(pl.multiple_of(s * (HEADS_OWN * HEAD_DIM) + h * HEAD_DIM, 16), HEAD_DIM)
        target = mine_out.at[place, :]
        if shift == 0:
            return pltpu.make_async_copy(part, target, save_sem.at[6 + h])
        return pltpu.make_async_remote_copy(
            src_ref=part,
            dst_ref=target,
            send_sem=swap_send.at[h, shift],
            recv_sem=swap_recv.at[h, shift],
            device_id=shifted[shift],
            device_id_type=MESH,
        )

    for part in range(3):
        nears[part].wait()

        @pl.when(s % 2 == 0)
        def _():
            w_own[part] = w_near[part, :, 0:192]

        @pl.when(s % 2 == 1)
        def _():
            w_own[part] = w_near[part, :, 64:256]

    for j in range(SEQ):
        start = j * BLOCK
        x_load(0, j).wait()
        a = norm_in(x_all[j].astype(F32), gain_row)
        a_all[start : start + BLOCK, :] = a
        a_t = a.T
        for part in range(3):
            qkv[part, :, start : start + BLOCK] = left_t(w_own[part], a_t).astype(BF16)
    saves[0].start()
    saves[1].start()
    for h in range(HEADS_OWN):
        rows = slice(h * HEAD_DIM, (h + 1) * HEAD_DIM)

        def write(query_block, here, o, lse):
            o_own[rows, here] = o
            lse_own[h, 0:1, here] = lse
            o_low[query_block, rows, :] = o.astype(BF16)

        attend_head(lambda part, columns: qkv[part, rows, columns], write, SEQ)
        for shift in range(SEQ):
            o_copy(h, shift).start()
    saves[2].start()
    saves[3].start()
    for load in loads:
        load.wait()

    def back_head(h):
        rows = pl.ds(pl.multiple_of(h * HEAD_DIM, HEAD_DIM), HEAD_DIM)
        queries_t = (qp[0, rows, :].astype(F32) * 0.125).astype(BF16)
        keys_t = qp[1, rows, :]
        do_t = dop[rows, :]
        lse = lp[pl.ds(pl.multiple_of(h * 8, 8), 8), :][0:1]
        delta = jnp.sum(do_t.astype(F32) * op[rows, :], axis=0, keepdims=True)
        keys = keys_t.T
        values = qp[2, rows, :].T
        queries = queries_t.T
        do_rows = do_t.T
        probs = jnp.exp(matmul(keys[:SPLIT], queries_t) - lse)
        probs = jnp.where(causal_mask(0, SPLIT, BLOCK), probs, 0.0)
        dprobs = matmul(values[:SPLIT], do_t)
        dlogits = (probs * (dprobs - delta)).astype(BF16)
        late = slice(SPLIT, BLOCK)
        corner = jnp.exp(matmul(keys[SPLIT:], queries_t[:, late]) - lse[:, late])
        corner = jnp.where(causal_mask(0, SPLIT, SPLIT), corner, 0.0)
        dcorner = matmul(values[SPLIT:], do_t[:, late])
        dcorner = (corner * (dcorner - delta[:, late])).astype(BF16)
        dq = matmul(keys_t[:, :SPLIT], dlogits)
        dq_late = dq[:, late] + matmul(keys_t[:, late], dcorner)
        dp[0, rows, :SPLIT] = (dq[:, :SPLIT] * 0.125).astype(BF16)
        dp[0, rows, late] = (dq_late * 0.125).astype(BF16)
        dp[1, rows, :SPLIT] = matmul(dlogits, queries).T.astype(BF16)
        dp[1, rows, late] = matmul(dcorner, queries[late]).T.astype(BF16)
        dp[2, rows, :SPLIT] = matmul(probs.astype(BF16), do_rows).T.astype(BF16)
        dp[2, rows, late] = matmul(corner.astype(BF16), do_rows[late]).T.astype(BF16)

    def back(turn, carry):
        for sub in range(TOGETHER):
            back_head(turn * TOGETHER + sub)
        return carry

    lax.fori_loop(0, HEADS // TOGETHER, back, 0)
    for part in range(3):
        gq[part * D : (part + 1) * D, :] = matmul(dp[part], ap[...]).astype(BF16)
    saves[4].start()
    dx[...] = first_norm_back(xp[...], dhp[...], w, dp, gain_row)
    saves[5].start()
    for save in saves:
        save.wait()
    for h in range(HEADS_OWN):
        for shift in range(SEQ):
            o_copy(h, shift).wait()


def first_norm_back(x, dh_t, w, dqkv, gain):
    x_t = x.T.astype(F32)
    average, inverse = column_stats(x_t)
    n = (x_t - average) * inverse
    t = matmul(w[:, 0:D], dqkv[0])
    for part in range(1, 3):
        t = t + matmul(w[:, part * D : (part + 1) * D], dqkv[part])
    t = t * widened(jnp.broadcast_to(gain, (128, D)).T, BLOCK)
    first = jnp.sum(t, axis=0, keepdims=True) * (1.0 / D)
    second = jnp.sum(t * n, axis=0, keepdims=True) * (1.0 / D)
    return (dh_t + (t - first - n * second) * inverse).astype(BF16).T


def long_forward(x_blocks, weight, gains, pack, collective_id):
    own_rows = HEADS_OWN * HEAD_DIM
    length = SEQ * BLOCK
    dma = pltpu.SemaphoreType.DMA
    anywhere = pl.BlockSpec(memory_space=pl.ANY)
    resident = pl.BlockSpec(memory_space=pltpu.VMEM)
    return pl.pallas_call(
        long_kernel,
        in_specs=[anywhere] * 7 + [resident] + [anywhere] * 7,
        out_specs=[anywhere] * 7,
        out_shape=[
            jax.ShapeDtypeStruct((length, D), BF16),
            jax.ShapeDtypeStruct((3, own_rows, length), BF16),
            jax.ShapeDtypeStruct((own_rows, length), F32),
            jax.ShapeDtypeStruct((HEADS_OWN, 8, length), F32),
            jax.ShapeDtypeStruct((D, BLOCK), BF16),
            jax.ShapeDtypeStruct((3 * D, D), BF16),
            jax.ShapeDtypeStruct((BLOCK, D), BF16),
        ],
        scratch_shapes=[
            pltpu.VMEM((length, D), BF16),
            pltpu.VMEM((3, own_rows, length), BF16),
            pltpu.VMEM((own_rows, length), F32),
            pltpu.VMEM((HEADS_OWN, 8, length), F32),
            pltpu.VMEM((SEQ, own_rows, BLOCK), BF16),
            pltpu.VMEM((D, 3 * D), BF16),
            pltpu.VMEM((3, D, BLOCK), BF16),
            pltpu.VMEM((D, BLOCK), F32),
            pltpu.VMEM((HEADS * 8, BLOCK), F32),
            pltpu.VMEM((D, BLOCK), BF16),
            pltpu.VMEM((BLOCK, D), BF16),
            pltpu.VMEM((BLOCK, D), BF16),
            pltpu.VMEM((D, BLOCK), F32),
            pltpu.VMEM((3, D, BLOCK), BF16),
            pltpu.VMEM((3 * D, D), BF16),
            pltpu.VMEM((BLOCK, D), BF16),
            pltpu.VMEM((SEQ, BLOCK, D), BF16),
            pltpu.VMEM((3, D, 256), BF16),
            pltpu.VMEM((3, D, own_rows), BF16),
            dma((11 + SEQ,)),
            dma((6 + HEADS_OWN,)),
            dma((HEADS_OWN, SEQ)),
            dma((HEADS_OWN, SEQ)),
        ],
        compiler_params=pltpu.CompilerParams(
            collective_id=collective_id, has_side_effects=True, vmem_limit_bytes=VMEM_LIMIT
        ),
        cost_estimate=pl.CostEstimate(
            flops=20 * 10**9, bytes_accessed=40 * 2**20, transcendentals=10**7
        ),
    )(*x_blocks, weight, gains, *pack)


PIECE = 768
HALF = PIECE // 2
COLS = D // 2
FEED_PIECES = (2 * FF + D) // PIECE
QKV_PIECES = 3 * D // PIECE
PIECES = FEED_PIECES + QKV_PIECES
ATTEND_TICK = 2
QKV_TICK = 5
BACK_TICK = 3
BACKS = 1
DX_TICK = 13


def sum_kernel(*refs):
    gd, gu, go, gq, do_ref, qkv_ref, o_ref, lse_ref, a_ref, gain_ref = refs[:10]
    x_ref, dh_ref, wd_ref, wu_ref, wo_ref, wq_ref, total_ref, dx_ref, sums_ref = refs[10:19]
    own, r0, r1, r2, r3, r4, fin, qkv, o_own, lse_own, a_all, gq_own, do_own, d_own = refs[19:33]
    dk_acc, dv_acc, back_ref, x_own, dh_own, wq, dx, grads, factors, sums = refs[33:43]
    own_sem, send_sem, recv_sem, fin_sem, in_sem, swap_send, swap_recv, gain_sem = refs[43:]
    r = lax.axis_index("rows")
    s = lax.axis_index("seq")
    core, xb, yb = r % 2, (r // 2) % 2, r // 4
    inside = (s == 1) | (s == 2)
    outside = (s == 0) | (s == 3)
    to_core = (r + 1 - 2 * core, s)
    to_x = (r + 2 - 4 * xb, s)
    to_y = (r + 4 - 8 * yb, s)
    to_pair = (r, s + 1 - 2 * (s % 2))
    to_middle = (r, 3 - s)
    shifted = [(r, (s + shift) % SEQ) for shift in range(SEQ)]
    barrier = pltpu.get_barrier_semaphore()
    for device in (to_core, to_x, to_y, *shifted[1:]):
        pl.semaphore_signal(barrier, inc=1, device_id=device, device_id_type=MESH)
    pl.semaphore_wait(barrier, 6)
    bits = [(xb, yb), (yb, xb)]
    partners = [(to_x, to_y), (to_y, to_x)]

    def rows_at(start, count):
        return pl.ds(pl.multiple_of(start, 16), count)

    def remote(source, target, send, recv, device):
        return pltpu.make_async_remote_copy(
            src_ref=source,
            dst_ref=target,
            send_sem=send,
            recv_sem=recv,
            device_id=device,
            device_id_type=MESH,
        )

    def numbered(source, target, kind, p, device):
        return remote(source, target, send_sem.at[kind, p], recv_sem.at[kind, p], device)

    def columns(o):
        return slice(o * COLS, (o + 1) * COLS)

    def base(o):
        return bits[o][0] * 192 + bits[o][1] * 96

    def core_copy(ref, q, p):
        part = ref.at[rows_at(q * PIECE + (1 - core) * HALF, HALF), :]
        return numbered(part, r0.at[p], 0, p, to_core)

    def own_copy(ref, q, p):
        part = ref.at[rows_at(q * PIECE + core * HALF, HALF), :]
        return pltpu.make_async_copy(part, own.at[p], own_sem.at[p])

    def first_copy(p, o):
        part = own.at[p, rows_at((1 - bits[o][0]) * 192, 192), columns(o)]
        return numbered(part, r1.at[p, o], 1 + o, p, partners[o][0])

    def second_copy(p, o):
        part = own.at[p, rows_at(bits[o][0] * 192 + (1 - bits[o][1]) * 96, 96), columns(o)]
        return numbered(part, r2.at[p, o], 3 + o, p, partners[o][1])

    def pair_copy(p, o):
        part = own.at[p, rows_at(base(o), 96), columns(o)]
        return numbered(part, r3.at[p, o], 5 + o, p, to_pair)

    def middle_copy(p, o):
        part = own.at[p, rows_at(base(o), 96), columns(o)]
        return numbered(part, r4.at[p, o], 7 + o, p, to_middle)

    def region(p, start, count, o):
        return total_ref.at[rows_at(p * PIECE + core * HALF + start, count), columns(o)]

    def fin_copy(p, o):
        return pltpu.make_async_copy(fin.at[p, o], region(p, base(o), 96, o), fin_sem.at[o, p])

    def pair_back(p, o):
        return numbered(fin.at[p, o], region(p, base(o), 96, o), 9 + o, p, to_pair)

    def second_back(p, o):
        part = region(p, base(o), 96, o)
        return numbered(part, part, 11 + o, p, partners[o][1])

    def first_back(p, o):
        part = region(p, bits[o][0] * 192, 192, o)
        return numbered(part, part, 13 + o, p, partners[o][0])

    def core_back(p):
        part = total_ref.at[rows_at(p * PIECE + core * HALF, HALF), :]
        return numbered(part, part, 15, p, to_core)

    def do_copy(shift):
        part = do_ref.at[(s + shift) % SEQ]
        if shift == 0:
            return pltpu.make_async_copy(part, do_own.at[s], in_sem.at[5])
        return remote(
            part, do_own.at[s], swap_send.at[0, shift], swap_recv.at[0, shift], shifted[shift]
        )

    def back_copy(h, shift):
        part = d_own.at[(s + shift) % SEQ, :, rows_at(h * HEAD_DIM, HEAD_DIM), :]
        target = back_ref.at[
            :, rows_at(s * (HEADS_OWN * HEAD_DIM) + h * HEAD_DIM, HEAD_DIM), :
        ]
        if shift == 0:
            return pltpu.make_async_copy(part, target, in_sem.at[6 + h])
        return remote(
            part, target, swap_send.at[1 + h, shift], swap_recv.at[1 + h, shift], shifted[shift]
        )

    loads = [
        pltpu.make_async_copy(qkv_ref, qkv, in_sem.at[0]),
        pltpu.make_async_copy(o_ref, o_own, in_sem.at[1]),
        pltpu.make_async_copy(lse_ref, lse_own, in_sem.at[2]),
        pltpu.make_async_copy(a_ref, a_all, in_sem.at[3]),
        pltpu.make_async_copy(gq, gq_own, in_sem.at[4]),
    ]
    late = [
        pltpu.make_async_copy(x_ref, x_own, in_sem.at[6 + HEADS_OWN]),
        pltpu.make_async_copy(dh_ref, dh_own, in_sem.at[7 + HEADS_OWN]),
        pltpu.make_async_copy(wq_ref, wq, in_sem.at[8 + HEADS_OWN]),
    ]
    dx_save = pltpu.make_async_copy(dx, dx_ref, in_sem.at[9 + HEADS_OWN])
    sums_save = pltpu.make_async_copy(sums, sums_ref, in_sem.at[10 + HEADS_OWN])
    for shift in range(1, SEQ):
        do_copy(shift).start()
    offset = 0
    for ref in (gd, gu, go):

        def begin(q, carry, ref=ref, offset=offset):
            core_copy(ref, q, q + offset).start()
            own_copy(ref, q, q + offset).start()
            return carry

        lax.fori_loop(0, ref.shape[0] // PIECE, begin, 0)
        offset += ref.shape[0] // PIECE
    do_copy(0).start()
    for load in loads:
        load.start()

    def added(index, other):
        own[index] = (own[index].astype(F32) + other.astype(F32)).astype(BF16)

    def after_core(p):
        own_copy(gd, 0, p).wait()
        core_copy(gd, 0, p).wait()
        own[p] = (own[p].astype(F32) + r0[p].astype(F32)).astype(BF16)
        for o in range(2):
            first_copy(p, o).start()

    def after_first(p):
        for o in range(2):
            first_copy(p, o).wait()
            added((p, rows_at(bits[o][0] * 192, 192), columns(o)), r1[p, o])
            second_copy(p, o).start()

    def after_second(p):
        for o in range(2):
            second_copy(p, o).wait()
            added((p, rows_at(base(o), 96), columns(o)), r2[p, o])

            @pl.when(outside)
            def _():
                pair_copy(p, o).start()

    def after_pair(p):
        for o in range(2):

            @pl.when(outside)
            def _():
                pair_copy(p, o).wait_send()

            @pl.when(inside)
            def _():
                pair_copy(p, o).wait_recv()
                added((p, rows_at(base(o), 96), columns(o)), r3[p, o])
                middle_copy(p, o).start()

    def after_middle(p):
        for o in range(2):

            @pl.when(inside)
            def _():
                middle_copy(p, o).wait()
                mine = own[p, rows_at(base(o), 96), columns(o)].astype(F32)
                fin[p, o] = (mine + r4[p, o].astype(F32)).astype(BF16)
                pair_back(p, o).start()
                fin_copy(p, o).start()

    def after_pair_back(p):
        for o in range(2):

            @pl.when(inside)
            def _():
                fin_copy(p, o).wait()
                pair_back(p, o).wait_send()

            @pl.when(outside)
            def _():
                pair_back(p, o).wait_recv()

            second_back(p, o).start()

    def after_second_back(p):
        for o in range(2):
            second_back(p, o).wait()
            first_back(p, o).start()

    def after_first_back(p):
        for o in range(2):
            first_back(p, o).wait()
        core_back(p).start()

    def after_core_back(p):
        core_back(p).wait()

    stages = [
        after_core,
        after_first,
        after_second,
        after_pair,
        after_middle,
        after_pair_back,
        after_second_back,
        after_first_back,
    ]

    def square(ref, p):
        return ref.at[rows_at(p * PIECE, PIECE), :]

    def grad_load(p):
        return pltpu.make_async_copy(square(total_ref, p), grads.at[p % 2], gain_sem.at[0, p % 2])

    def factor_load(ref, p):
        return pltpu.make_async_copy(ref, factors.at[p % 2], gain_sem.at[1, p % 2])

    def fetch(p):
        grad_load(p).start()

        @pl.when(p < 4)
        def _():
            factor_load(square(wd_ref, p), p).start()

        @pl.when((p >= 4) & (p < 8))
        def _():
            columns = pl.ds(pl.multiple_of((p - 4) * PIECE, PIECE), PIECE)
            factor_load(wu_ref.at[:, columns], p).start()

        @pl.when(p == 8)
        def _():
            factor_load(wo_ref, p).start()

    def row_sums(values):
        folded = values[:, 0:128]
        for k in range(1, D // 128):
            folded = folded + values[:, k * 128 : (k + 1) * 128]
        return jnp.sum(folded.T, axis=0, keepdims=True)

    def weigh(p):
        grad_load(p).wait()
        factor_load(wo_ref, p).wait()
        grad = grads[p % 2].astype(F32)

        @pl.when(p < 4)
        def _():
            place = pl.ds(pl.multiple_of(p * PIECE, PIECE), PIECE)
            sums[0:1, place] = row_sums(grad * factors[p % 2].astype(F32))

        @pl.when((p >= 4) & (p < 8))
        def _():
            term = jnp.sum(grad * factors[p % 2].T.astype(F32), axis=0, keepdims=True)
            sums[1:2, 0:D] = jnp.where(p == 4, 0.0, sums[1:2, 0:D]) + term

        @pl.when(p == 8)
        def _():
            sums[2:3, 0:D] = row_sums(grad * factors[p % 2].astype(F32))

    def head_rows(h):
        return rows_at(h * HEAD_DIM, HEAD_DIM)

    def attend(h, query_block):
        rows = head_rows(h)
        here = slice(query_block * BLOCK, (query_block + 1) * BLOCK)
        queries_t = (qkv[0, rows, here].astype(F32) * 0.125).astype(BF16)
        queries = queries_t.T
        do_t = do_own[query_block, rows, :]
        do_rows = do_t.T
        lse = lse_own[h, 0:1, here]
        delta = jnp.sum(do_t.astype(F32) * o_own[rows, here], axis=0, keepdims=True)
        dq = jnp.zeros((HEAD_DIM, BLOCK), F32)
        for key_block in range(query_block):
            there = slice(key_block * BLOCK, (key_block + 1) * BLOCK)
            keys_t = qkv[1, rows, there]
            probs = jnp.exp(matmul(keys_t.T, queries_t) - lse)
            dprobs = matmul(qkv[2, rows, there].T, do_t)
            dlogits = (probs * (dprobs - delta)).astype(BF16)
            dq = dq + matmul(keys_t, dlogits)
            dv_acc[there, :] += matmul(probs.astype(BF16), do_rows)
            dk_acc[there, :] += matmul(dlogits, queries)
        early = slice(query_block * BLOCK, query_block * BLOCK + SPLIT)
        late = slice(query_block * BLOCK + SPLIT, (query_block + 1) * BLOCK)
        keys_t = qkv[1, rows, here]
        keys = keys_t.T
        values = qkv[2, rows, here].T
        probs = jnp.exp(matmul(keys[:SPLIT], queries_t) - lse)
        probs = jnp.where(causal_mask(0, SPLIT, BLOCK), probs, 0.0)
        dlogits = (probs * (matmul(values[:SPLIT], do_t) - delta)).astype(BF16)
        corner = jnp.exp(matmul(keys[SPLIT:], queries_t[:, SPLIT:]) - lse[:, SPLIT:])
        corner = jnp.where(causal_mask(0, SPLIT, SPLIT), corner, 0.0)
        dcorner = matmul(values[SPLIT:], do_t[:, SPLIT:]) - delta[:, SPLIT:]
        dcorner = (corner * dcorner).astype(BF16)
        dq = dq + matmul(keys_t[:, :SPLIT], dlogits)
        dq_late = dq[:, SPLIT:] + matmul(keys_t[:, SPLIT:], dcorner)
        dq = jnp.concatenate([dq[:, :SPLIT], dq_late], axis=1)
        dv_acc[early, :] += matmul(probs.astype(BF16), do_rows)
        dk_acc[early, :] += matmul(dlogits, queries)
        dv_acc[late, :] += matmul(corner.astype(BF16), do_rows[SPLIT:])
        dk_acc[late, :] += matmul(dcorner, queries[SPLIT:])
        d_own[query_block, 0, rows, :] = (dq * 0.125).astype(BF16)

    def finish_head(h):
        rows = head_rows(h)
        total = jnp.zeros((3 * HEAD_DIM, D), F32)
        for block in range(SEQ):
            here = slice(block * BLOCK, (block + 1) * BLOCK)
            d_own[block, 1, rows, :] = dk_acc[here, :].T.astype(BF16)
            d_own[block, 2, rows, :] = dv_acc[here, :].T.astype(BF16)
            joined = d_own[block, :, rows, :].reshape(3 * HEAD_DIM, BLOCK)
            total = total + matmul(joined, a_all[here, :])
        for part in range(3):
            place = rows_at(part * D + s * (HEADS_OWN * HEAD_DIM) + h * HEAD_DIM, HEAD_DIM)
            term = total[part * HEAD_DIM : (part + 1) * HEAD_DIM, :]
            gq_own[place, :] = (gq_own[place, :].astype(F32) + term).astype(BF16)
        back_copy(h, 0).start()

    def tick(t, carry):
        for lag, stage in enumerate(stages):
            for sub in range(2):
                p = 2 * (t - lag) + sub

                @pl.when((p >= 0) & (p < FEED_PIECES))
                def _():
                    stage(p)

                q = 2 * (t - lag - QKV_TICK) + sub

                @pl.when((q >= 0) & (q < QKV_PIECES))
                def _():
                    stage(FEED_PIECES + q)

        @pl.when(t == ATTEND_TICK)
        def _():
            for load in loads:
                load.wait()
            for load in late:
                load.start()
            for shift in range(SEQ):
                do_copy(shift).wait()

        h = t - ATTEND_TICK

        @pl.when((h >= 0) & (h < HEADS_OWN))
        def _():
            dk_acc[...] = jnp.zeros_like(dk_acc)
            dv_acc[...] = jnp.zeros_like(dv_acc)
            for query_block in range(SEQ):
                attend(h, query_block)
            finish_head(h)

        @pl.when(h == HEADS_OWN - 1)
        def _():
            for q in range(QKV_PIECES):
                core_copy(gq_own, q, FEED_PIECES + q).start()
                own_copy(gq_own, q, FEED_PIECES + q).start()

        for unit in range(3 * HEADS_OWN):

            @pl.when(t == BACK_TICK + unit // BACKS)
            def _():
                back_copy(unit // 3, unit % 3 + 1).start()

        for sub in range(2):
            p = 2 * (t - len(stages) - 1) + sub

            @pl.when((p >= 0) & (p < FEED_PIECES))
            def _():
                weigh(p)

        for sub in range(2):
            p = 2 * (t - len(stages)) + sub

            @pl.when((p >= 0) & (p < FEED_PIECES))
            def _():
                after_core_back(p)
                fetch(p)

            q = p - 2 * QKV_TICK

            @pl.when((q >= 0) & (q < QKV_PIECES))
            def _():
                after_core_back(FEED_PIECES + q)

        @pl.when(t == DX_TICK)
        def _():
            for load in late:
                load.wait()
            for h in range(HEADS_OWN):
                for shift in range(SEQ):
                    back_copy(h, shift).wait()
            dx[...] = first_norm_back(x_own[...], dh_own[...], wq, back_ref, gain_ref[:, 0:D])
            dx_save.start()

        return carry

    last = QKV_TICK + (QKV_PIECES - 1) // 2 + len(stages) + 1
    lax.fori_loop(0, last, tick, 0)
    sums_save.start()
    dx_save.wait()
    sums_save.wait()


def summed_everywhere(*args, collective_id):
    n = PIECES
    length = SEQ * BLOCK
    own_rows = HEADS_OWN * HEAD_DIM
    dma = pltpu.SemaphoreType.DMA
    anywhere = pl.BlockSpec(memory_space=pl.ANY)
    return pl.pallas_call(
        sum_kernel,
        out_shape=[
            jax.ShapeDtypeStruct((n * PIECE, D), BF16),
            jax.ShapeDtypeStruct((BLOCK, D), BF16),
            jax.ShapeDtypeStruct((8, FF), F32),
        ],
        in_specs=[anywhere] * 9 + [pl.BlockSpec(memory_space=pltpu.VMEM)] + [anywhere] * 6,
        out_specs=[anywhere] * 3,
        scratch_shapes=[
            pltpu.VMEM((n, HALF, D), BF16),
            pltpu.VMEM((n, HALF, D), BF16),
            pltpu.VMEM((n, 2, 192, COLS), BF16),
            pltpu.VMEM((n, 2, 96, COLS), BF16),
            pltpu.VMEM((n, 2, 96, COLS), BF16),
            pltpu.VMEM((n, 2, 96, COLS), BF16),
            pltpu.VMEM((n, 2, 96, COLS), BF16),
            pltpu.VMEM((3, own_rows, length), BF16),
            pltpu.VMEM((own_rows, length), F32),
            pltpu.VMEM((HEADS_OWN, 8, length), F32),
            pltpu.VMEM((length, D), BF16),
            pltpu.VMEM((3 * D, D), BF16),
            pltpu.VMEM((SEQ, own_rows, BLOCK), BF16),
            pltpu.VMEM((SEQ, 3, own_rows, BLOCK), BF16),
            pltpu.VMEM((length, HEAD_DIM), F32),
            pltpu.VMEM((length, HEAD_DIM), F32),
            pltpu.VMEM((3, D, BLOCK), BF16),
            pltpu.VMEM((BLOCK, D), BF16),
            pltpu.VMEM((D, BLOCK), F32),
            pltpu.VMEM((D, 3 * D), BF16),
            pltpu.VMEM((BLOCK, D), BF16),
            pltpu.VMEM((2, PIECE, D), BF16),
            pltpu.VMEM((2, PIECE, D), BF16),
            pltpu.VMEM((8, FF), F32),
            dma((n,)),
            dma((16, n)),
            dma((16, n)),
            dma((2, n)),
            dma((11 + HEADS_OWN,)),
            dma((1 + HEADS_OWN, SEQ)),
            dma((1 + HEADS_OWN, SEQ)),
            dma((2, 2)),
        ],
        compiler_params=pltpu.CompilerParams(
            collective_id=collective_id, has_side_effects=True, vmem_limit_bytes=60 * 2**20
        ),
        cost_estimate=pl.CostEstimate(flops=0, bytes_accessed=n * PIECE * D * 64, transcendentals=0),
    )(*args)


def sent(value, *pairs):
    return lax.ppermute(value, "seq", pairs)


def finish_kernel(slots, total, wq, gain_ref, sums, dx_long, dx_pack, *refs):
    gd, gu, go, gq, si, sf, sh, sa, grad_out, acc, dx, load_sem, copy_sem = refs
    step = pl.program_id(0)
    loads = [
        pltpu.make_async_copy(source, dx.at[k], load_sem.at[k])
        for k, source in enumerate((dx_long, dx_pack))
    ]
    copies = [
        pltpu.make_async_copy(dx.at[k], grad_out.at[slots[k]], copy_sem.at[k]) for k in range(2)
    ]

    @pl.when(step == 0)
    def _():
        for load in loads:
            load.start()
        si[...] = (sums[2:3, 0:D] / gain_ref[:, D : 2 * D])[0]
        sf[...] = (sums[1:2, 0:D] / gain_ref[:, 2 * D : 3 * D])[0]
        sh[...] = (sums[0:1, :] / gain_ref[:, 3 * D :])[0]

    @pl.when(step == 2)
    def _():
        for load, copy in zip(loads, copies):
            load.wait()
            copy.start()

    @pl.when(step < 4)
    def _():
        gd[...] = total[...].astype(F32)

    @pl.when((step >= 4) & (step < 8))
    def _():
        gu[...] = total[...].T.astype(F32)

    @pl.when(step == 8)
    def _():
        go[...] = total[...].astype(F32)

    @pl.when(step >= 9)
    def _():
        grad = total[...].T.astype(F32)
        gq[...] = grad
        product = grad * wq[...].astype(F32)
        folded = product[:, 0:128]
        for k in range(1, D // 128):
            folded = folded + product[:, k * 128 : (k + 1) * 128]
        acc[...] = folded + jnp.where(step == 9, 0.0, acc[...])

    @pl.when(step == 11)
    def _():
        sa[...] = (jnp.sum(acc[...].T, axis=0, keepdims=True) / gain_ref[:, 0:D])[0]
        for copy in copies:
            copy.wait()


def finished(slots, total, weight, gains, sums, dx_long, dx_pack):
    square = lambda index: pl.BlockSpec((D, D), index)
    at_down = lambda i, slots: (jnp.clip(i, 0, 3), 0)
    at_up = lambda i, slots: (0, jnp.clip(i - 4, 0, 3))
    at_qkv = lambda i, slots: (0, jnp.clip(i - 9, 0, 2))
    still = lambda i, slots: (0, 0)
    once = lambda *shape: pl.BlockSpec(shape, still, pipeline_mode=pl.Buffered(1))
    row = lambda size: pl.BlockSpec((size,), lambda i, slots: (0,))
    anywhere = pl.BlockSpec(memory_space=pl.ANY)
    shapes = [(FF, D), (D, FF), (D, D), (D, 3 * D), (D,), (D,), (FF,), (D,)]
    dma = pltpu.SemaphoreType.DMA
    return pl.pallas_call(
        finish_kernel,
        grid_spec=pltpu.PrefetchScalarGridSpec(
            num_scalar_prefetch=1,
            grid=(PIECES,),
            in_specs=[square(lambda i, slots: (i, 0)), square(at_qkv)]
            + [once(1, 3 * D + FF), once(8, FF)]
            + [anywhere] * 2,
            out_specs=[square(at_down), square(at_up), square(still), square(at_qkv)]
            + [row(D), row(D), row(FF), row(D)]
            + [anywhere],
            scratch_shapes=[
                pltpu.VMEM((D, 128), F32),
                pltpu.VMEM((2, BLOCK, D), BF16),
                dma((2,)),
                dma((2,)),
            ],
        ),
        out_shape=[jax.ShapeDtypeStruct(shape, F32) for shape in shapes]
        + [jax.ShapeDtypeStruct((2, BLOCK, D), BF16)],
        compiler_params=pltpu.CompilerParams(vmem_limit_bytes=VMEM_LIMIT),
        cost_estimate=pl.CostEstimate(
            flops=2 * 10**7, bytes_accessed=46 * 2**20, transcendentals=0
        ),
    )(slots, total, weight, gains, sums, dx_long, dx_pack)


def split_layer(
    tokens,
    segment_ids,
    cotangent,
    query_key_value,
    out_weight,
    up_weight,
    down_weight,
    attend_gain,
    inner_gain,
    feed_gain,
    hidden_gain,
):
    long_first = segment_ids[0, -1] == 0
    x_long = jnp.where(long_first, tokens[0], tokens[1])
    left = sent(x_long, (0, 1), (1, 2), (2, 3))
    right = sent(x_long, (1, 0), (2, 1), (3, 2))
    long_slot = jnp.where(long_first, 0, 1).astype(jnp.int32)
    slots = jnp.stack([long_slot, 1 - long_slot])
    gains = jnp.concatenate([attend_gain, inner_gain, feed_gain, hidden_gain])[None]
    weights = (out_weight, up_weight, down_weight)
    a_pack, qkv_pack, o_pack, lse_pack, x_pack = pack_forward(
        slots[1:], tokens, query_key_value, gains
    )
    o_pack, left, right = lax.optimization_barrier((o_pack, left, right))
    left_two = sent(left, (1, 2), (2, 3))
    right_two = sent(right, (1, 0), (2, 1))
    across = sent(jnp.where(lax.axis_index("seq") == 1, left, right), (1, 3), (2, 0))
    output, dh_pack, do_pack, go_pack, gd_pack, gu_pack = feed_both(
        slots[1:], o_pack, tokens, cotangent, gains, weights
    )
    *x_far, do_pack = lax.optimization_barrier((left_two, right_two, across, do_pack))
    a_all, qkv_long, o_long, lse_long, o_mine, gq_pack, dx_pack = long_forward(
        (x_long, left, right, *x_far),
        query_key_value,
        gains,
        (qkv_pack, o_pack, lse_pack, do_pack, a_pack, x_pack, dh_pack),
        1,
    )
    output, dh_long, do_long, go, gd, gu = feed_both(
        slots[:1],
        o_mine,
        tokens,
        cotangent,
        gains,
        weights,
        (gd_pack, gu_pack, go_pack),
        output,
    )
    total, dx_long, sums = summed_everywhere(
        gd,
        gu,
        go,
        gq_pack,
        do_long.reshape(SEQ, HEADS_OWN * HEAD_DIM, BLOCK),
        qkv_long,
        o_long,
        lse_long,
        a_all,
        gains,
        x_long,
        dh_long,
        down_weight,
        up_weight,
        out_weight,
        query_key_value,
        collective_id=0,
    )
    down_grad, up_grad, out_grad, qkv_grad, *sums, tokens_grad = finished(
        slots, total, query_key_value, gains, sums, dx_long, dx_pack
    )
    inner_total, feed_total, hidden_total, attend_total = sums
    return (
        output,
        tokens_grad,
        qkv_grad,
        out_grad,
        up_grad,
        down_grad,
        attend_total,
        inner_total,
        feed_total,
        hidden_total,
    )


def per_device(tokens, *others):
    split = lax.axis_size("seq") == SEQ and lax.axis_size("rows") == 8
    if split and tokens.shape == (2, BLOCK, D):
        return split_layer(tokens, *others)
    return ring_layer(tokens, *others)


def solution(mesh):
    return jax.shard_map(
        per_device,
        mesh=mesh,
        in_specs=(
            P("rows", "seq", None),
            P("rows", None),
            P("rows", "seq", None),
            P(),
            P(),
            P(),
            P(),
            P(),
            P(),
            P(),
            P(),
        ),
        out_specs=(
            P("rows", "seq", None),
            P("rows", "seq", None),
            P(),
            P(),
            P(),
            P(),
            P(),
            P(),
            P(),
            P(),
        ),
        check_vma=False,
    )
```
